32 devices in a mesh: shard: 8 (over z, x), ctx: 2 (over y), tensor: 2 (over core).
Axes of the slice: x: 2, y: 2, z: 4, core: 2. Of those that a mesh axis runs over, the one named last changes fastest.
Arguments:
- clip_input: bfloat16 [8, 8, 392, 512], P('shard', 'ctx', None, 'tensor'), may hold values from -6 to 6
- cotangent: bfloat16 [8, 8, 392, 512], P('shard', 'ctx', None, 'tensor'), may hold values from -6 to 6
- gain_one: float32 [512], P('tensor'), may hold values from 0.1 to 1.9
- shift_one: float32 [512], P('tensor'), may hold values from -3 to 3
- w_qkv: bfloat16 [3, 512, 512], P(None, 'shard', 'tensor'), may hold values from -0.25 to 0.25
- b_qv: float32 [2, 512], P(None, 'tensor'), may hold values from -3 to 3
- w_proj: bfloat16 [512, 512], P('tensor', 'shard'), may hold values from -1.5 to 1.5
- b_proj: float32 [512], P('tensor'), may hold values from -3 to 3
- bias_table: float32 [16, 2535], P('tensor'), may hold values from -3 to 3
- gain_two: float32 [512], P('tensor'), may hold values from 0.1 to 1.9
- shift_two: float32 [512], P('tensor'), may hold values from -3 to 3
- w_fc1: bfloat16 [512, 2048], P('shard', 'tensor'), may hold values from -0.25 to 0.25
- b_fc1: float32 [2048], P('tensor'), may hold values from -3 to 3
- w_fc2: bfloat16 [2048, 512], P('tensor', 'shard'), may hold values from -0.125 to 0.125
- b_fc2: float32 [512], P('tensor'), may hold values from -3 to 3
- rel_index: int32 [392, 392], replicated, may hold values from 0 to 2534
- regions: int32 [8, 392], P('ctx'), may hold values from 0 to 3
Outputs:
- block_out: float32 [8, 8, 392, 512], P('shard', 'ctx', None, 'tensor')
- grad_input: float32 [8, 8, 392, 512], P('shard', 'ctx', None, 'tensor')
- grad_gain_one: float32 [512], P('tensor')
- grad_shift_one: float32 [512], P('tensor')
- grad_w_qkv: float32 [3, 512, 512], P(None, 'shard', 'tensor')
- grad_b_qv: float32 [2, 512], P(None, 'tensor')
- grad_w_proj: float32 [512, 512], P('tensor', 'shard')
- grad_b_proj: float32 [512], P('tensor')
- grad_table: float32 [16, 2535], P('tensor')
- grad_gain_two: float32 [512], P('tensor')
- grad_shift_two: float32 [512], P('tensor')
- grad_w_fc1: float32 [512, 2048], P('shard', 'tensor')
- grad_b_fc1: float32 [2048], P('tensor')
- grad_w_fc2: float32 [2048, 512], P('tensor', 'shard')
- grad_b_fc2: float32 [512], P('tensor')
The draws below stay inside these ranges and needn't reach their ends.
Inputs may be any that keep to these rules, and one draw needn't show every extreme that they name: `rel_index`: a table entry for every pair of a window's tokens.
All inputs are finite; a program needn't handle non-finite values.
Results may differ from the reference program's by a relative error of at most 0.015.
Values may be sent and summed in bfloat16 or wider, within the bound.
No kernel may reach another device: no remote copies, remote signals or barrier semaphores. Data moves between devices by JAX's collectives and lax.ppermute only.
A program may use at most 192 MiB of HBM per device.

```python
import jax
import jax.numpy as jnp
from jax import lax

D = 512
HEADS = 16
HD = 32
FF = 2048
WT = 8
WH = 7
WW = 7
WTOK = 392
WINDOWS = 8
TABLE = 2535
CLIPS = 8


def set_ends(entries, stream_key, smallest, top_value):
    place = [jax.random.randint(jax.random.fold_in(stream_key, axis), (), 0, length) for axis, length in enumerate(entries.shape)]
    main_axis = entries.shape.index(max(entries.shape))
    neighbour = place[:main_axis] + [(place[main_axis] + 1) % entries.shape[main_axis]] + place[main_axis + 1:]
    return entries.at[tuple(place)].set(smallest).at[tuple(neighbour)].set(top_value)


def spiked(array, rng, source, target, blocks, factor):
    def block_of(dim):
        return (jnp.arange(array.shape[dim]) // (array.shape[dim] // blocks)).reshape((-1,) + (1,) * (array.ndim - 1 - dim))

    one_side = jax.random.permutation(rng, blocks)[block_of(target)]
    other_side = (block_of(target) + blocks // 2) % blocks
    return jnp.where((block_of(source) == one_side) | (block_of(source) == other_side), factor * array, array)


def steps_of(rng, dims, cuts, smallest, largest):
    def one(axis_at, parts):
        steps = jax.random.uniform(jax.random.fold_in(jax.random.fold_in(rng, 6), axis_at), (parts,), jnp.float32, smallest / len(cuts), largest / len(cuts))
        return jnp.repeat(jnp.exp(steps), dims[axis_at] // parts).reshape((-1,) + (1,) * (len(dims) - axis_at - 1))

    factor_of = one(*cuts[0])
    for cut in cuts[1:]:
        factor_of = factor_of * one(*cut)
    return factor_of


def scatter_about(own_key, shape, scale, reach, cuts=(), held_as=jnp.bfloat16):
    values = jax.random.normal(own_key, shape, jnp.float32) * scale
    if len(cuts) > 0:
        values = steps_of(own_key, shape, cuts, -0.22, 0.18) * values
    return jnp.clip(values, min=-reach, max=reach).astype(held_as)


def gaussian_with(own_key, extent, scale, most, cuts, heavy, held_as=jnp.bfloat16):
    values = scale * jax.random.normal(own_key, extent, jnp.float32)
    if cuts:
        values = values * steps_of(own_key, extent, cuts, -0.22, 0.18)
    return jnp.clip(spiked(values, jax.random.fold_in(own_key, 3), *heavy), -most, most).astype(held_as)


def setup_inputs(seed: int = 0) -> dict:
    streams_of = jax.random.split(jax.random.key(seed), 18)
    clip_input = gaussian_with(streams_of[0], (CLIPS, WINDOWS, WTOK, D), 1.0, 6.0, ((0, 8), (1, 2), (3, 2)), (0, 3, 8, 2.0))
    cotangent = gaussian_with(streams_of[1], (CLIPS, WINDOWS, WTOK, D), 1.0, 6.0, ((0, 8), (1, 2), (3, 2)), (0, 3, 8, 2.0))
    gain_one = jnp.clip(1.0 + 0.18 * jax.random.normal(streams_of[2], (D,), jnp.float32), 0.1, 1.9)
    shift_one = scatter_about(streams_of[3], (D,), 0.5, 3.0, ((0, 2),), jnp.float32)
    w_qkv = scatter_about(streams_of[4], (3, D, D), D ** -0.5, 0.25, ((1, 8), (2, 2)))
    b_qv = scatter_about(streams_of[5], (2, D), 0.5, 3.0, ((1, 2),), jnp.float32)
    w_proj = scatter_about(streams_of[6], (D, D), (D // 32) ** -0.5, 1.5, ((0, 2), (1, 8)))
    b_proj = scatter_about(streams_of[7], (D,), 0.5, 3.0, ((0, 2),), jnp.float32)
    bias_table = scatter_about(streams_of[8], (HEADS, TABLE), 0.5, 3.0, ((0, 2),), jnp.float32)
    gain_two = jnp.clip(1.0 + 0.18 * jax.random.normal(streams_of[9], (D,), jnp.float32), 0.1, 1.9)
    shift_two = scatter_about(streams_of[10], (D,), 0.5, 3.0, ((0, 2),), jnp.float32)
    w_fc1 = scatter_about(streams_of[11], (D, FF), D ** -0.5, 0.25, ((0, 8), (1, 2)))
    b_fc1 = scatter_about(streams_of[12], (FF,), 0.5, 3.0, ((0, 2),), jnp.float32)
    w_fc2 = scatter_about(streams_of[13], (FF, D), FF ** -0.5, 0.125, ((0, 2), (1, 8)))
    b_fc2 = scatter_about(streams_of[14], (D,), 0.5, 3.0, ((0, 2),), jnp.float32)
    rel_index = set_ends(jax.random.randint(streams_of[15], (WTOK, WTOK), 0, TABLE), jax.random.fold_in(streams_of[15], 1), 0, TABLE - 1).astype(jnp.int32)
    regions = set_ends(jax.random.randint(streams_of[16], (WINDOWS, WTOK), 0, 4), jax.random.fold_in(streams_of[16], 1), 0, 3).astype(jnp.int32)
    return {"clip_input": clip_input, "cotangent": cotangent, "gain_one": gain_one, "shift_one": shift_one, "w_qkv": w_qkv, "b_qv": b_qv, "w_proj": w_proj, "b_proj": b_proj, "bias_table": bias_table, "gain_two": gain_two, "shift_two": shift_two, "w_fc1": w_fc1, "b_fc1": b_fc1, "w_fc2": w_fc2, "b_fc2": b_fc2, "rel_index": rel_index, "regions": regions}


HIGHEST = lax.Precision.HIGHEST
EPSILON = 1e-05

@jax.custom_vjp
def low(v):
    return lax.optimization_barrier(v.astype(jnp.bfloat16)).astype(jnp.float32)

@jax.custom_vjp
def low_back(v):
    return v

def low_keep(v):
    return (low(v), None)

def low_pass(kept, grad):
    return (grad,)

def back_keep(v):
    return (v, None)

def back_low(kept, grad):
    return (low(grad),)
low.defvjp(low_keep, low_pass)
low_back.defvjp(back_keep, back_low)

def exact_gelu(values):
    return jax.nn.gelu(values, approximate=False)

def to_grid(windows):
    feature_count = windows.shape[-1]
    grid_cells = windows.reshape(2, 2, 2, WT, WH, WW, feature_count).transpose(0, 3, 1, 4, 2, 5, 6)
    return grid_cells.reshape(2 * WT, 2 * WH, 2 * WW, feature_count)

def to_windows(grid_cells):
    feature_count = grid_cells.shape[-1]
    grid_tiles = grid_cells.reshape(2, WT, 2, WH, 2, WW, feature_count).transpose(0, 2, 4, 1, 3, 5, 6)
    return grid_tiles.reshape(WINDOWS, WTOK, feature_count)

def cyclic(windows, direction):
    offsets = (direction * (WT // 2), direction * (WH // 2), direction * (WW // 2))
    return to_windows(jnp.roll(to_grid(windows), offsets, axis=(0, 1, 2)))

def layer_norm(values, norm_gain, norm_shift):
    center = lax.optimization_barrier(jnp.mean(values, -1, keepdims=True))
    spread = lax.optimization_barrier(jnp.mean(values * values, -1, keepdims=True)) - center * center
    return (values - center) * lax.rsqrt(spread + EPSILON) * norm_gain + norm_shift

def clip_forward(weights, clip_rows, rel_index, regions):
    gain_one, shift_one, w_qkv, b_qv, w_proj, b_proj, bias_table, gain_two, shift_two, w_fc1, b_fc1, w_fc2, b_fc2 = weights
    first_norm = low(layer_norm(clip_rows, gain_one, shift_one))
    moved_rows = low_back(cyclic(first_norm, -1))
    projected = jnp.einsum('wtd,cde->cwte', moved_rows, w_qkv, precision=HIGHEST)
    queries = low_back(low(projected[0] + b_qv[0])).reshape(WINDOWS, WTOK, HEADS, HD)
    key_rows = low_back(low(projected[1])).reshape(WINDOWS, WTOK, HEADS, HD)
    values = low_back(low(projected[2] + b_qv[1])).reshape(WINDOWS, WTOK, HEADS, HD)
    bias_full = bias_table[:, rel_index]
    mask_add = jnp.where(regions[:, :, None] == regions[:, None, :], 0.0, -100.0)
    scores = jnp.einsum('wqhd,wkhd->whqk', queries, key_rows, precision=HIGHEST) * HD ** (-0.5)
    scores = low_back(scores + bias_full[None] + mask_add[:, None])
    soft_probs = low(jax.nn.softmax(scores, axis=-1))
    attended = low(jnp.einsum('whqk,wkhd->wqhd', soft_probs, values, precision=HIGHEST)).reshape(WINDOWS, WTOK, D)
    restored = low_back(cyclic(attended, 1)).reshape(-1, D)
    branch = low_back(jnp.dot(restored, w_proj, precision=HIGHEST) + b_proj)
    middle = clip_rows.reshape(-1, D) + branch
    second_norm = low(layer_norm(middle, gain_two, shift_two))
    hidden = low_back(jnp.dot(second_norm, w_fc1, precision=HIGHEST) + b_fc1)
    active = low(exact_gelu(hidden))
    result = middle + low_back(jnp.dot(active, w_fc2, precision=HIGHEST) + b_fc2)
    return result.reshape(WINDOWS, WTOK, D)

def reference(clip_input, cotangent, gain_one, shift_one, w_qkv, b_qv, w_proj, b_proj, bias_table, gain_two, shift_two, w_fc1, b_fc1, w_fc2, b_fc2, rel_index, regions):
    weights = tuple((argument.astype(jnp.float32) for argument in (gain_one, shift_one, w_qkv, b_qv, w_proj, b_proj, bias_table, gain_two, shift_two, w_fc1, b_fc1, w_fc2, b_fc2)))

    def forward(params, clip_rows):
        return clip_forward(params, clip_rows, rel_index, regions)

    def per_clip(totals, paired):
        clip_rows, upstream = paired
        result, pullback = jax.vjp(forward, weights, clip_rows)
        grad_weights, grad_clip = pullback(upstream)
        return (jax.tree.map(jnp.add, totals, grad_weights), (result, grad_clip))
    zeros = jax.tree.map(jnp.zeros_like, weights)
    totals, (block_out, grad_input) = lax.scan(per_clip, zeros, (clip_input.astype(jnp.float32), cotangent.astype(jnp.float32)))
    return (block_out, grad_input, totals[0], totals[1], totals[2], totals[3], totals[4], totals[5], totals[6], totals[7], totals[8], totals[9], totals[10], totals[11], totals[12])
```

```python
import functools

import jax
import jax.numpy as jnp
import numpy as np
from jax import lax
from jax.experimental import pallas as pl
from jax.experimental.pallas import tpu as pltpu
from jax.sharding import PartitionSpec as P

BF = jnp.bfloat16
F32 = jnp.float32
HD = 32
WT, WH, WW = 8, 7, 7
WTOK = WT * WH * WW
TOKS = 400
HALF_ROWS = 208
TABLE = 2535
COARSE = 10
FINE = 256
ROWS = 16
GROUP = 4
EPSILON = 1e-05
LOG2E = 1.4426950408889634
VMEM_LIMIT = 56 * 1024 * 1024


def dot(a, b, ca, cb):
    return lax.dot_general(a, b, (((ca,), (cb,)), ((), ())), preferred_element_type=F32)


def one_hot(fine_row, width):
    rows = lax.broadcasted_iota(jnp.int32, (FINE, width), 0)
    return jnp.where(rows == fine_row, 1.0, 0.0).astype(BF)


def lane_tiles(width):
    return [(t, t * 128, min(128, width - t * 128)) for t in range(-(-width // 128))]


def put_rows(scratch, start, rows):
    for t, begin, size in lane_tiles(rows.shape[1]):
        scratch[t, start : start + rows.shape[0], :size] = rows[:, begin : begin + size]


def strided_rows(scratch, start, count, step, width):
    parts = [scratch[t, pl.ds(start, count, stride=step), :][:, :size] for t, _, size in lane_tiles(width)]
    return jnp.concatenate(parts, 1)


def lookup_kernel(heads, coarse, idx_ref, table_ref, out_ref, scratch):
    width = idx_ref.shape[1]
    for r in range(ROWS):
        idx = idx_ref[r : r + 1, :]
        hot = one_hot(jnp.bitwise_and(idx, FINE - 1), width)
        level = lax.shift_right_logical(idx, 8)
        picked = dot(table_ref[...], hot, 1, 0)
        acc = jnp.zeros((heads, width), F32)
        for c in range(coarse):
            acc = acc + jnp.where(level == c, picked[c * heads : (c + 1) * heads], 0.0)
        put_rows(scratch, r * heads, acc)
    for h in range(heads):
        out_ref[h] = strided_rows(scratch, h, ROWS, heads, width).astype(BF)


def lookup(idx, table, heads):
    rows, width = idx.shape
    coarse = table.shape[0] // heads
    return pl.pallas_call(
        functools.partial(lookup_kernel, heads, coarse),
        grid=(rows // ROWS,),
        in_specs=[
            pl.BlockSpec((ROWS, width), lambda i: (i, 0)),
            pl.BlockSpec(table.shape, lambda i: (0, 0)),
        ],
        out_specs=pl.BlockSpec((heads, ROWS, width), lambda i: (0, i, 0)),
        out_shape=jax.ShapeDtypeStruct((heads, rows, width), BF),
        scratch_shapes=[pltpu.VMEM((-(-width // 128), ROWS * heads, 128), F32)],
        compiler_params=pltpu.CompilerParams(vmem_limit_bytes=VMEM_LIMIT),
        cost_estimate=pl.CostEstimate(flops=2 * rows * width * FINE * table.shape[0], bytes_accessed=rows * width * heads * 2, transcendentals=0),
        name="table_lookup",
    )(idx, table)


def fold_kernel(heads, coarse, core_ref, idx_ref, own_ref, got_ref, out_ref, scratch):
    width = idx_ref.shape[1]
    step = pl.program_id(0)

    @pl.when(step == 0)
    def _():
        out_ref[...] = jnp.zeros_like(out_ref)

    @pl.when(jnp.logical_or(step > 0, core_ref[0] == 0))
    def _():
        for h in range(heads):
            put_rows(scratch, h * ROWS, own_ref[h].astype(F32) + got_ref[h].astype(F32))
        total = jnp.zeros(out_ref.shape, F32)
        for r in range(ROWS):
            idx = idx_ref[r : r + 1, :]
            hot = one_hot(jnp.bitwise_and(idx, FINE - 1), width)
            level = lax.shift_right_logical(idx, 8)
            grads = strided_rows(scratch, r, heads, ROWS, width)
            parts = [jnp.where(level == c, grads, 0.0) for c in range(coarse)]
            total = total + dot(jnp.concatenate(parts, 0).astype(BF), hot, 1, 1)
        out_ref[...] += total


def fold(core, idx, pair, got, heads, coarse):
    rows, width = idx.shape
    shift = (pair.shape[1] - rows) // ROWS
    return pl.pallas_call(
        functools.partial(fold_kernel, heads, coarse),
        grid_spec=pltpu.PrefetchScalarGridSpec(
            num_scalar_prefetch=1,
            grid=(rows // ROWS,),
            in_specs=[
                pl.BlockSpec((ROWS, width), lambda i, core: (i, 0)),
                pl.BlockSpec((heads, ROWS, width), lambda i, core: (0, core[0] * shift + i, 0)),
                pl.BlockSpec((heads, ROWS, width), lambda i, core: (0, i, 0)),
            ],
            out_specs=pl.BlockSpec((coarse * heads, FINE), lambda i, core: (0, 0)),
            scratch_shapes=[pltpu.VMEM((-(-width // 128), ROWS * heads, 128), F32)],
        ),
        out_shape=jax.ShapeDtypeStruct((coarse * heads, FINE), F32),
        compiler_params=pltpu.CompilerParams(vmem_limit_bytes=VMEM_LIMIT),
        cost_estimate=pl.CostEstimate(flops=2 * rows * width * FINE * coarse * heads, bytes_accessed=rows * width * heads * 4, transcendentals=0),
        name="table_fold",
    )(core, idx, pair, got)


def pick_bias(first, own_ref, got_ref, j, half):
    low = lax.select_n(first, got_ref[j], own_ref[j])
    skip = 2 * half - 400
    high = lax.select_n(first, own_ref[j, skip:, :], got_ref[j, skip:, :])
    return jnp.concatenate([low, high], 0).astype(F32)


def attend_kernel(group, hd, core_ref, q_ref, k_ref, v_ref, rq_ref, rk_ref, own_ref, got_ref, att_ref, exact_ref, lse_ref):
    first = core_ref[0] == 0
    ones = jnp.ones((16, q_ref.shape[2]), BF)
    for j in range(group):
        part = pl.ds(j * hd, hd)
        qa = jnp.concatenate([q_ref[0, part, :], rq_ref[0]], 0)
        ka = jnp.concatenate([k_ref[0, part, :], rk_ref[0]], 0)
        va = jnp.concatenate([v_ref[0, part, :], ones], 0)
        scores = dot(ka, qa, 0, 0) + pick_bias(first, own_ref, got_ref, j, own_ref.shape[1])
        peak = jnp.max(scores, 0, keepdims=True)
        weights = jnp.exp2(scores - peak).astype(BF)
        mixed = dot(va, weights, 1, 0)
        total = mixed[hd : hd + 1]
        out = mixed[:hd] / total
        att_ref[0, part, :] = out.astype(BF)
        exact_ref[0, part, :] = out
        lse_ref[0, 0, j : j + 1, :] = peak + jnp.log2(total)


def attend(core, q, k, v, rq, rk, own, got, hd, group):
    wins, feats, toks = q.shape
    heads = feats // hd
    half = own.shape[1]
    feat_spec = pl.BlockSpec((1, group * hd, toks), lambda h, w, core: (w, h, 0))
    reg_spec = pl.BlockSpec((1, 16, toks), lambda h, w, core: (w, 0, 0))
    bias_spec = pl.BlockSpec((group, half, toks), lambda h, w, core: (h, 0, 0))
    return pl.pallas_call(
        functools.partial(attend_kernel, group, hd),
        grid_spec=pltpu.PrefetchScalarGridSpec(
            num_scalar_prefetch=1,
            grid=(heads // group, wins),
            in_specs=[feat_spec, feat_spec, feat_spec, reg_spec, reg_spec, bias_spec, bias_spec],
            out_specs=[feat_spec, feat_spec, pl.BlockSpec((1, 1, group, toks), lambda h, w, core: (w, h, 0, 0))],
        ),
        out_shape=[
            jax.ShapeDtypeStruct(q.shape, BF),
            jax.ShapeDtypeStruct(q.shape, F32),
            jax.ShapeDtypeStruct((wins, heads // group, group, toks), F32),
        ],
        compiler_params=pltpu.CompilerParams(vmem_limit_bytes=VMEM_LIMIT),
        cost_estimate=pl.CostEstimate(flops=4 * wins * feats * toks * toks, bytes_accessed=wins * feats * toks * 12, transcendentals=wins * heads * toks * toks),
        name="attend",
    )(core, q, k, v, rq, rk, own, got)


def split3(row):
    hi = row.astype(BF)
    rest = row - hi.astype(F32)
    mid = rest.astype(BF)
    return hi.astype(F32), mid.astype(F32), rest - mid.astype(F32)


def rows16(parts, width):
    rows = lax.broadcasted_iota(jnp.int32, (16, width), 0)
    out = jnp.zeros((16, width), F32)
    for i, part in enumerate(parts):
        out = jnp.where(rows == i, part, out)
    return out.astype(BF)


def attend_back_kernel(group, hd, scale, core_ref, q_ref, k_ref, v_ref, rq_ref, rk_ref, own_ref, got_ref, exact_ref, lse_ref, g_ref, dq_ref, dk_ref, dv_ref, pair_ref, sums):
    first = core_ref[0] == 0
    toks = q_ref.shape[2]
    win = pl.program_id(1)
    minus = rows16([-1.0, -1.0, -1.0], toks)
    for j in range(group):
        part = pl.ds(j * hd, hd)
        q = q_ref[0, part, :]
        k = k_ref[0, part, :]
        g = g_ref[0, part, :]
        qa = jnp.concatenate([q, rq_ref[0], rows16(split3(lse_ref[0, 0, j : j + 1, :]), toks)], 0)
        ka = jnp.concatenate([k, rk_ref[0], minus], 0)
        va = jnp.concatenate([v_ref[0, part, :], minus], 0)
        along = jnp.sum(g.astype(F32) * exact_ref[0, part, :], 0, keepdims=True)
        ga = jnp.concatenate([g, rows16(split3(along), toks)], 0)
        probs = jnp.exp2(dot(ka, qa, 0, 0) + pick_bias(first, own_ref, got_ref, j, own_ref.shape[1]))
        grads = (probs * dot(va, ga, 0, 0)).astype(BF)
        low = probs.astype(BF)
        dv_ref[0, part, :] = dot(g, low, 1, 1).astype(BF)
        dk_ref[0, part, :] = (dot(q, grads, 1, 1) * (1.0 / LOG2E)).astype(BF)
        dq_ref[0, part, :] = (dot(k, grads, 1, 0) * scale).astype(BF)
        wide = grads.astype(F32)

        @pl.when(win == 0)
        def _():
            sums[j] = wide

        @pl.when(win > 0)
        def _():
            sums[j] = sums[j] + wide

        @pl.when(win == pl.num_programs(1) - 1)
        def _():
            pair_ref[j] = sums[j].astype(BF)


def attend_back(core, q, k, v, rq, rk, own, got, exact, lse, g, hd, group, scale):
    wins, feats, toks = q.shape
    heads = feats // hd
    half = own.shape[1]
    feat_spec = pl.BlockSpec((1, group * hd, toks), lambda h, w, core: (w, h, 0))
    reg_spec = pl.BlockSpec((1, 16, toks), lambda h, w, core: (w, 0, 0))
    bias_spec = pl.BlockSpec((group, half, toks), lambda h, w, core: (h, 0, 0))
    return pl.pallas_call(
        functools.partial(attend_back_kernel, group, hd, scale),
        grid_spec=pltpu.PrefetchScalarGridSpec(
            num_scalar_prefetch=1,
            grid=(heads // group, wins),
            in_specs=[feat_spec, feat_spec, feat_spec, reg_spec, reg_spec, bias_spec, bias_spec, feat_spec, pl.BlockSpec((1, 1, group, toks), lambda h, w, core: (w, h, 0, 0)), feat_spec],
            out_specs=[feat_spec, feat_spec, feat_spec, pl.BlockSpec((group, toks, toks), lambda h, w, core: (h, 0, 0))],
            scratch_shapes=[pltpu.VMEM((group, toks, toks), F32)],
        ),
        out_shape=[jax.ShapeDtypeStruct(q.shape, BF)] * 3 + [jax.ShapeDtypeStruct((heads, toks, toks), BF)],
        compiler_params=pltpu.CompilerParams(vmem_limit_bytes=VMEM_LIMIT),
        cost_estimate=pl.CostEstimate(flops=10 * wins * feats * toks * toks, bytes_accessed=wins * feats * toks * 16, transcendentals=wins * heads * toks * toks),
        name="attend_back",
    )(core, q, k, v, rq, rk, own, got, exact, lse, g)


def cost(flops, moved, trans=0):
    return pl.CostEstimate(flops=int(flops), bytes_accessed=int(moved), transcendentals=int(trans))


def params():
    return pltpu.CompilerParams(vmem_limit_bytes=VMEM_LIMIT)


def whole_spec(array):
    rank = len(array.shape)
    return pl.BlockSpec(array.shape, lambda w: (0,) * rank)


def window_spec(array):
    rank = len(array.shape)
    return pl.BlockSpec((1,) + array.shape[1:], lambda w: (w,) + (0,) * (rank - 1))


def normed(values):
    width = values.shape[1]
    center = jnp.sum(values, 1, keepdims=True) / width
    spread = jnp.sum(values * values, 1, keepdims=True) / width - center * center
    inv = lax.rsqrt(spread + EPSILON)
    return (values - center) * inv, inv


def norm_back(upstream, xhat, inv, gain):
    width = xhat.shape[1]
    scaled = upstream * gain
    total = jnp.sum(scaled, 1, keepdims=True) / width
    along = jnp.sum(scaled * xhat, 1, keepdims=True) / width
    return inv * (scaled - total - xhat * along)


def front_kernel(scale, x_ref, gain_ref, shift_ref, w_ref, b_ref, q_ref, k_ref, v_ref):
    xhat, _ = normed(x_ref[0].astype(F32))
    first = (xhat * gain_ref[...] + shift_ref[...]).astype(BF)
    for t in range(2):
        cols = w_ref.shape[2] // 3
        rows = pl.ds(t * cols, cols)
        made = dot(first, w_ref[t], 1, 0)
        q = (made[:, :cols] + b_ref[0:1, t * cols : (t + 1) * cols]) * scale
        v = made[:, 2 * cols :] + b_ref[1:2, t * cols : (t + 1) * cols]
        q_ref[0, rows, :] = q.T.astype(BF)
        k_ref[0, rows, :] = made[:, cols : 2 * cols].T.astype(BF)
        v_ref[0, rows, :] = v.T.astype(BF)


def front(x, gain, shift, w, b, scale):
    wins, toks, width = x.shape
    feats = 2 * (w.shape[2] // 3)
    out = jax.ShapeDtypeStruct((wins, feats, toks), BF)
    return pl.pallas_call(
        functools.partial(front_kernel, scale),
        grid=(wins,),
        in_specs=[window_spec(x), whole_spec(gain), whole_spec(shift), whole_spec(w), whole_spec(b)],
        out_specs=[window_spec(out)] * 3,
        out_shape=[out] * 3,
        compiler_params=params(),
        cost_estimate=cost(6 * wins * toks * width * feats, 4 * wins * toks * width * 2 + w.size * 2),
        name="front",
    )(x, gain, shift, w, b)


def middle_kernel(x_ref, att_ref, proj_ref, bp_ref, gain_ref, shift_ref, fc1_ref, b1_ref, fc2_ref, b2_ref, out_ref, mid_ref, second_ref, act_ref, slope_ref):
    cols = proj_ref.shape[2]
    branch = sum(dot(att_ref[0, pl.ds(t * cols, cols), :], proj_ref[t], 0, 1) for t in range(2))
    middle = x_ref[0].astype(F32) + (branch + bp_ref[...])
    mid_ref[0] = middle
    xhat, _ = normed(middle)
    second = (xhat * gain_ref[...] + shift_ref[...]).astype(BF)
    second_ref[0] = second
    wide = fc1_ref.shape[2]
    step = wide // 2
    total = jnp.zeros(middle.shape, F32)
    for t in range(2):
        for s in range(0, wide, step):
            at = t * wide + s
            hidden = dot(second, fc1_ref[t, :, s : s + step], 1, 0) + b1_ref[:, at : at + step]
            phi = 0.5 + 0.5 * lax.erf(hidden * (0.5**0.5))
            active = (hidden * phi).astype(BF)
            bell = jnp.exp2(hidden * hidden * (-0.5 * LOG2E)) * (1.0 / (2.0 * np.pi) ** 0.5)
            act_ref[0, :, at : at + step] = active
            slope_ref[0, :, at : at + step] = (phi + hidden * bell).astype(BF)
            total = total + dot(active, fc2_ref[t, :, s : s + step], 1, 1)
    out_ref[0] = middle + (total + b2_ref[...])


def middle_forward(x, att, proj, bp, gain, shift, fc1, b1, fc2, b2):
    wins, toks, width = x.shape
    hidden = 2 * fc1.shape[2]
    wide = jax.ShapeDtypeStruct((wins, toks, hidden), BF)
    plain = jax.ShapeDtypeStruct(x.shape, F32)
    outs = [plain, plain, jax.ShapeDtypeStruct(x.shape, BF), wide, wide]
    fixed = (proj, bp, gain, shift, fc1, b1, fc2, b2)
    return pl.pallas_call(
        middle_kernel,
        grid=(wins,),
        in_specs=[window_spec(x), window_spec(att)] + [whole_spec(a) for a in fixed],
        out_specs=[window_spec(o) for o in outs],
        out_shape=outs,
        compiler_params=params(),
        cost_estimate=cost(2 * wins * toks * width * (width + 2 * hidden), wins * toks * (width * 14 + hidden * 4) + fc1.size * 4),
        name="middle_forward",
    )(x, att, *fixed)


def store_halves(ref, scratch):
    cols = ref.shape[2]
    for t in range(2):
        ref[t] = scratch[:, t * cols : (t + 1) * cols].astype(BF)


def middle_back_kernel(cot_ref, mid_ref, second_ref, act_ref, slope_ref, att_ref, gain_ref, fc1_ref, fc2_ref, proj_ref, gm_ref, gr_ref, d2_ref, d1_ref, dp_ref, small_ref, b1_ref, acc2, acc1, accp):
    win = pl.program_id(0)

    @pl.when(win == 0)
    def _():
        acc2[...] = jnp.zeros_like(acc2)
        acc1[...] = jnp.zeros_like(acc1)
        accp[...] = jnp.zeros_like(accp)
        small_ref[...] = jnp.zeros_like(small_ref)
        b1_ref[...] = jnp.zeros_like(b1_ref)

    cot = cot_ref[0]
    second = second_ref[0]
    wide = fc1_ref.shape[2]
    step = wide // 2
    grad_second = jnp.zeros(cot.shape, F32)
    for t in range(2):
        for s in range(0, wide, step):
            at = t * wide + s
            span = slice(at, at + step)
            acc2[:, span] += dot(cot, act_ref[0, :, span], 0, 0)
            grad = dot(cot, fc2_ref[t, :, s : s + step], 1, 0) * slope_ref[0, :, span].astype(F32)
            grad = grad.astype(BF)
            b1_ref[:, span] += jnp.sum(grad.astype(F32), 0, keepdims=True)
            acc1[:, span] += dot(second, grad, 0, 0)
            grad_second = grad_second + dot(grad, fc1_ref[t, :, s : s + step], 1, 1)
    upstream = cot.astype(F32)
    xhat, inv = normed(mid_ref[0])
    grad_mid = upstream + norm_back(grad_second, xhat, inv, gain_ref[...])
    gm_ref[0] = grad_mid
    branch = grad_mid.astype(BF)
    cols = proj_ref.shape[2]
    for t in range(2):
        gr_ref[0, pl.ds(t * cols, cols), :] = dot(proj_ref[t], branch, 0, 1).astype(BF)
    accp[...] += dot(branch, att_ref[0], 0, 1)
    small_ref[0:1, :] += jnp.sum(upstream, 0, keepdims=True)
    small_ref[1:2, :] += jnp.sum(grad_second * xhat, 0, keepdims=True)
    small_ref[2:3, :] += jnp.sum(grad_second, 0, keepdims=True)
    small_ref[3:4, :] += jnp.sum(branch.astype(F32), 0, keepdims=True)

    @pl.when(win == pl.num_programs(0) - 1)
    def _():
        store_halves(d2_ref, acc2)
        store_halves(d1_ref, acc1)
        store_halves(dp_ref, accp)


def middle_back(cot, mid, second, act, slope, att, gain, fc1, fc2, proj):
    wins, toks, width = cot.shape
    hidden = act.shape[2]
    windows = (cot, mid, second, act, slope, att)
    fixed = (gain, fc1, fc2, proj)
    outs = [jax.ShapeDtypeStruct(mid.shape, F32), jax.ShapeDtypeStruct(att.shape, BF)]
    sums = [jax.ShapeDtypeStruct(fc2.shape, BF), jax.ShapeDtypeStruct(fc1.shape, BF), jax.ShapeDtypeStruct(proj.shape, BF), jax.ShapeDtypeStruct((4, width), F32), jax.ShapeDtypeStruct((1, hidden), F32)]
    return pl.pallas_call(
        middle_back_kernel,
        grid=(wins,),
        in_specs=[window_spec(a) for a in windows] + [whole_spec(a) for a in fixed],
        out_specs=[window_spec(o) for o in outs] + [whole_spec(o) for o in sums],
        out_shape=outs + sums,
        scratch_shapes=[pltpu.VMEM((width, hidden), F32), pltpu.VMEM((width, hidden), F32), pltpu.VMEM((width, att.shape[1]), F32)],
        compiler_params=params(),
        cost_estimate=cost(4 * wins * toks * width * (width + 2 * hidden), wins * toks * (width * 16 + hidden * 4) + fc1.size * 8),
        name="middle_back",
    )(*windows, *fixed)


def back_kernel(x_ref, dq_ref, dk_ref, dv_ref, gm_ref, gain_ref, shift_ref, w_ref, gx_ref, dw_ref, small_ref, acc):
    win = pl.program_id(0)

    @pl.when(win == 0)
    def _():
        acc[...] = jnp.zeros_like(acc)
        small_ref[...] = jnp.zeros_like(small_ref)

    xhat, inv = normed(x_ref[0].astype(F32))
    first = (xhat * gain_ref[...] + shift_ref[...]).astype(BF)
    cols = w_ref.shape[2] // 3
    moved = jnp.zeros(xhat.shape, F32)
    for t in range(2):
        rows = pl.ds(t * cols, cols)
        grads = jnp.concatenate([dq_ref[0, rows, :], dk_ref[0, rows, :], dv_ref[0, rows, :]], 0)
        moved = moved + dot(grads, w_ref[t], 0, 1)
        acc[t] += dot(first, grads, 0, 1)
    grad_first = moved.astype(BF).astype(F32)
    gx_ref[0] = (gm_ref[0] + norm_back(grad_first, xhat, inv, gain_ref[...])).astype(gx_ref.dtype)
    ones = jnp.ones((8, dq_ref.shape[2]), BF)
    small_ref[0:1, :] += dot(ones, dq_ref[0], 1, 1)[0:1]
    small_ref[1:2, :] += dot(ones, dv_ref[0], 1, 1)[0:1]
    small_ref[2:3, :] += jnp.sum(grad_first * xhat, 0, keepdims=True)
    small_ref[3:4, :] += jnp.sum(grad_first, 0, keepdims=True)

    @pl.when(win == pl.num_programs(0) - 1)
    def _():
        dw_ref[...] = acc[...].astype(BF)


def back(x, dq, dk, dv, gm, gain, shift, w):
    wins, toks, width = x.shape
    windows = (x, dq, dk, dv, gm)
    fixed = (gain, shift, w)
    outs = [jax.ShapeDtypeStruct(x.shape, F32), jax.ShapeDtypeStruct(w.shape, BF), jax.ShapeDtypeStruct((4, width), F32)]
    return pl.pallas_call(
        back_kernel,
        grid=(wins,),
        in_specs=[window_spec(a) for a in windows] + [whole_spec(a) for a in fixed],
        out_specs=[window_spec(outs[0]), whole_spec(outs[1]), whole_spec(outs[2])],
        out_shape=outs,
        scratch_shapes=[pltpu.VMEM(w.shape, F32)],
        compiler_params=params(),
        cost_estimate=cost(12 * wins * toks * width * width, wins * toks * width * 16 + w.size * 4),
        name="back",
    )(*windows, *fixed)


def bits_of(axis):
    return lax.axis_size(axis).bit_length() - 1


def bit_on(axis, bit):
    return lax.shift_right_logical(lax.axis_index(axis), bit) % 2 == 1


def swap(value, axis, bit=0):
    pairs = [(source, source ^ (1 << bit)) for source in range(lax.axis_size(axis))]
    return lax.ppermute(value, axis, pairs)


def ordered(on, mine, other, axis):
    return jnp.concatenate((jnp.where(on, other, mine), jnp.where(on, mine, other)), axis)


def bit_order(axis):
    count = bits_of(axis)
    return [b for b in range(1, count)] + ([0] if count else [])


def gather_rows(part):
    count = bits_of("shard")
    rows, cols = part.shape
    held = part.reshape((1,) * count + (rows, cols))
    for bit in bit_order("shard"):
        held = ordered(bit_on("shard", bit), held, swap(held, "shard", bit), count - 1 - bit)
    return held.reshape(-1, cols)


def both_halves(mine):
    on = lax.axis_index("tensor") == 1
    return ordered(on, mine[None], swap(mine, "tensor")[None], 0)


def add_rounded(a, b):
    return (a.astype(F32) + b.astype(F32)).astype(BF)


def choose(array, index, axis):
    return lax.dynamic_slice_in_dim(array, index, 1, axis)


def scatter_halves(halves):
    core = lax.axis_index("tensor")
    got = swap(choose(halves, 1 - core, 0), "tensor")
    return add_rounded(choose(halves, core, 0), got)[0]


def scatter_rows(part):
    count = bits_of("shard")
    rows, cols = part.shape
    held = part.reshape((2,) * count + (rows >> count, cols))
    for bit in reversed(bit_order("shard")):
        axis = count - 1 - bit
        own = bit_on("shard", bit).astype(jnp.int32)
        got = swap(choose(held, 1 - own, axis), "shard", bit)
        held = add_rounded(choose(held, own, axis), got)
    held = held.reshape(rows >> count, cols)
    for bit in range(bits_of("ctx")):
        held = held.astype(F32) + swap(held.astype(BF), "ctx", bit).astype(F32)
        if bit + 1 < bits_of("ctx"):
            held = held.astype(BF)
    return held.astype(F32)


def sum_all(value):
    for axis in ("shard", "ctx"):
        for bit in range(bits_of(axis)):
            value = value + swap(value, axis, bit)
    return value


def roll_axis(shaped, axis_pos, levels, backward):
    token_axis = 4 + axis_pos
    length = shaped.shape[token_axis]
    border = length - length // 2 if backward else length // 2
    before = lax.slice_in_dim(shaped, 0, border, axis=token_axis)
    after = lax.slice_in_dim(shaped, border, length, axis=token_axis)
    moving = after if backward else before
    if axis_pos < levels:
        moving = swap(moving, "ctx", levels - 1 - axis_pos)
    else:
        moving = jnp.roll(moving, 1 if backward else -1, axis=1 + axis_pos)
    return jnp.concatenate((moving, before) if backward else (after, moving), axis=token_axis)


def window_roll(windows, clips, counts, backward):
    shaped = windows.reshape((clips,) + counts + (WT, WH, WW, windows.shape[-1]))
    for axis_pos in range(3):
        shaped = roll_axis(shaped, axis_pos, bits_of("ctx"), backward)
    return shaped.reshape(windows.shape)


HELD = WTOK // 2
SENT_IN = 200
SENT_OUT = 208


def frame_sources():
    source = np.zeros((4, HELD), np.int64)
    for h in range(2 * WH):
        for w in range(2 * WW):
            here = (h // WH) * 2 + w // WW
            there_h, there_w = (h + WH // 2) % (2 * WH), (w + WW // 2) % (2 * WW)
            there = (there_h // WH) * 2 + there_w // WW
            for a in range(WT // 2):
                row = (a * WH + h % WH) * WW + w % WW
                source[here, row] = there * HELD + (a * WH + there_h % WH) * WW + there_w % WW
    return source


def selector(picks, width):
    cells = lax.broadcasted_iota(jnp.int32, (picks.size, width), 1)
    return (jnp.asarray(picks.reshape(-1, 1), jnp.int32) == cells).astype(BF)


def shift_in(windows):
    source = frame_sources()
    there, row = source // HELD, source % HELD
    near = np.full((4, TOKS), -1)
    near[:, :HELD] = there * WTOK + HELD + row
    far = np.full((4, TOKS), -1)
    far[:, HELD:WTOK] = there * SENT_IN + row
    width = windows.shape[-1]
    got = swap(windows[:, :SENT_IN].reshape(-1, width), "ctx")
    kept = dot(selector(near, 4 * WTOK), windows.reshape(-1, width), 1, 0)
    return (kept + dot(selector(far, 4 * SENT_IN), got, 1, 0)).astype(BF).reshape(4, TOKS, width)


def shift_out(windows):
    source = frame_sources().reshape(-1)
    place = np.argsort(source).reshape(4, HELD)
    there, row = place // HELD, place % HELD
    near = np.full((4, WTOK), -1)
    near[:, HELD:] = there * TOKS + row
    far = np.full((4, WTOK), -1)
    far[:, :HELD] = there * SENT_OUT + row + HELD - (TOKS - SENT_OUT)
    width = windows.shape[-1]
    got = swap(windows[:, TOKS - SENT_OUT :].reshape(-1, width), "ctx")
    kept = dot(selector(near, 4 * TOKS), windows.reshape(-1, width), 1, 0)
    return (kept + dot(selector(far, 4 * SENT_OUT), got, 1, 0)).reshape(4, WTOK, width)


def to_shifted(windows, clips, counts):
    if bits_of("ctx") == 1 and clips == 1:
        moved = shift_in(windows)
    else:
        moved = jnp.pad(window_roll(windows, clips, counts, False), ((0, 0), (0, TOKS - WTOK), (0, 0)))
    half = moved.shape[0] // 2
    core = lax.axis_index("tensor")
    mine = lax.dynamic_slice_in_dim(moved, core * half, half, 0)
    other = swap(lax.dynamic_slice_in_dim(moved, (1 - core) * half, half, 0), "tensor")
    return ordered(core == 1, mine, other, 2)


def from_shifted(values, clips, counts):
    values = values.astype(BF)
    width = values.shape[2] // 2
    core = lax.axis_index("tensor")
    mine = lax.dynamic_slice_in_dim(values, core * width, width, 2)
    other = swap(lax.dynamic_slice_in_dim(values, (1 - core) * width, width, 2), "tensor")
    windows = ordered(core == 1, mine, other, 0)
    if bits_of("ctx") == 1 and clips == 1:
        return shift_out(windows)
    return window_roll(windows[:, :WTOK], clips, counts, True).astype(F32)


def region_rows(regions):
    padded = jnp.pad(regions, ((0, 0), (0, TOKS - WTOK)))
    query_rows, key_rows = [], []
    pieces = []
    rest = np.float32(-100.0 * LOG2E)
    for _ in range(3):
        piece = np.float32(rest.astype(jnp.bfloat16))
        pieces.append(float(piece))
        rest = np.float32(rest - piece)
    for region in range(4):
        same = padded == region
        for piece in pieces:
            query_rows.append(same.astype(F32))
            key_rows.append(jnp.where(same, 0.0, piece))
    blank = jnp.zeros(padded.shape, F32)
    past = jnp.broadcast_to(jnp.arange(TOKS) >= WTOK, padded.shape)
    query_rows += [blank] * 3 + [blank + 1.0]
    key_rows += [blank] * 3 + [jnp.where(past, -1e30, 0.0)]
    return jnp.stack(query_rows, 1).astype(BF), jnp.stack(key_rows, 1).astype(BF)


def on_device(
    clip_input,
    cotangent,
    gain_one,
    shift_one,
    w_qkv,
    b_qv,
    w_proj,
    b_proj,
    bias_table,
    gain_two,
    shift_two,
    w_fc1,
    b_fc1,
    w_fc2,
    b_fc2,
    rel_index,
    regions,
):
    clips, window_count, tokens, half_width = clip_input.shape
    width = 2 * half_width
    heads = 2 * bias_table.shape[0]
    levels = bits_of("ctx")
    counts = tuple(1 if axis_pos < levels else 2 for axis_pos in range(3))
    core = lax.axis_index("tensor")
    core_row = core.astype(jnp.int32).reshape(1)
    total_windows = clips * window_count
    held_windows = total_windows // 2
    scale = HD ** (-0.5)

    vectors = jnp.concatenate((gain_one, shift_one, b_qv.reshape(-1), b_proj, gain_two, shift_two, b_fc2, b_fc1, bias_table.reshape(-1)))
    pairs = both_halves(vectors)
    names = pairs[:, : 8 * half_width].reshape(2, 8, half_width).transpose(1, 0, 2).reshape(8, 1, width)
    gain1, shift1, bq, bv, bp, gain2, shift2, b2 = [names[i] for i in range(8)]
    start = 8 * half_width
    b1 = pairs[:, start : start + b_fc1.shape[0]].reshape(1, -1)
    table = pairs[:, start + b_fc1.shape[0] :].reshape(heads, TABLE)

    x = to_shifted(clip_input.reshape(total_windows, tokens, half_width), clips, counts)
    qkv_part = w_qkv.transpose(1, 0, 2).reshape(w_qkv.shape[1], -1)
    rest_part = jnp.concatenate((w_proj.T, w_fc1, w_fc2.T), 1)
    qkv_mine = gather_rows(qkv_part)
    rest_mine = gather_rows(rest_part)
    cot = to_shifted(cotangent.reshape(total_windows, tokens, half_width), clips, counts)

    table = jnp.pad(table * LOG2E, ((0, 0), (0, COARSE * FINE - TABLE)))
    table = table.reshape(heads, COARSE, FINE).transpose(1, 0, 2).reshape(COARSE * heads, FINE).astype(BF)
    index = jnp.pad(rel_index.T, ((0, TOKS - tokens), (0, TOKS - tokens)))
    index = lax.dynamic_slice_in_dim(index, core * (TOKS - HALF_ROWS), HALF_ROWS, 0)
    bias_own = lookup(index, table, heads)
    bias_got = swap(bias_own, "tensor")
    labels = jnp.tile(regions, (clips, 1))
    labels = lax.dynamic_slice_in_dim(labels, core * held_windows, held_windows, 0)
    query_rows, key_rows = region_rows(labels)

    qkv = both_halves(qkv_mine)
    queries, keys, values = front(x, gain1, shift1, qkv, jnp.concatenate((bq, bv), 0), scale * LOG2E)
    att, exact, lse = attend(core_row, queries, keys, values, query_rows, key_rows, bias_own, bias_got, HD, GROUP)
    edge = half_width
    proj = both_halves(rest_mine[:, :edge])
    fc1 = both_halves(rest_mine[:, edge : edge + w_fc1.shape[1]])
    fc2 = both_halves(rest_mine[:, edge + w_fc1.shape[1] :])
    out, mid, second, act, slope = middle_forward(x, att, proj, bp, gain2, shift2, fc1, b1, fc2, b2)
    block_out = from_shifted(out, clips, counts)
    grad_mid, grad_att, d_fc2, d_fc1, d_proj, small_mid, d_b1 = middle_back(cot, mid, second, act, slope, att, gain2, fc1, fc2, proj)
    dq, dk, dv, pair = attend_back(core_row, queries, keys, values, query_rows, key_rows, bias_own, bias_got, exact, lse, grad_att, HD, GROUP, scale)
    sent = lax.dynamic_slice_in_dim(pair, (1 - core) * (TOKS - HALF_ROWS), HALF_ROWS, 1)
    pair_got = swap(sent, "tensor")
    grad_x, d_qkv, small_end = back(x, dq, dk, dv, grad_mid, gain1, shift1, qkv)
    folded = fold(core_row, index, pair, pair_got, heads, COARSE)
    grad_input = from_shifted(grad_x, clips, counts)

    rest_grads = jnp.concatenate((scatter_halves(d_proj), scatter_halves(d_fc1), scatter_halves(d_fc2)), 1)
    rest_grads = scatter_rows(rest_grads)
    qkv_grads = scatter_rows(scatter_halves(d_qkv))

    small = jnp.concatenate((small_mid, small_end), 0).reshape(8, 2, half_width).transpose(1, 0, 2).reshape(2, -1)
    folded = folded.reshape(COARSE, heads, FINE).transpose(1, 0, 2).reshape(2, -1)
    small = jnp.concatenate((small, d_b1.reshape(2, -1), folded), 1).reshape(2, -1, 256)
    small = choose(small, core, 0) + swap(choose(small, 1 - core, 0), "tensor")
    small = sum_all(small[0]).reshape(-1)
    names = small[: 8 * half_width].reshape(8, half_width)
    d_b1 = small[start : start + b_fc1.shape[0]]
    grad_table = small[start + b_fc1.shape[0] :].reshape(heads // 2, COARSE * FINE)[:, :TABLE]

    rows = w_fc1.shape[0]
    return (
        block_out.reshape(clip_input.shape),
        grad_input.reshape(clip_input.shape),
        names[6],
        names[7],
        qkv_grads.reshape(rows, 3, half_width).transpose(1, 0, 2),
        jnp.stack((names[4], names[5])),
        rest_grads[:, :edge].T,
        names[3],
        grad_table,
        names[1],
        names[2],
        rest_grads[:, edge : edge + w_fc1.shape[1]],
        d_b1,
        rest_grads[:, edge + w_fc1.shape[1] :].T,
        names[0],
    )


def solution(mesh):
    in_specs = (
        P("shard", "ctx", None, "tensor"),
        P("shard", "ctx", None, "tensor"),
        P("tensor"),
        P("tensor"),
        P(None, "shard", "tensor"),
        P(None, "tensor"),
        P("tensor", "shard"),
        P("tensor"),
        P("tensor", None),
        P("tensor"),
        P("tensor"),
        P("shard", "tensor"),
        P("tensor"),
        P("tensor", "shard"),
        P("tensor"),
        P(),
        P("ctx", None),
    )
    out_specs = (
        P("shard", "ctx", None, "tensor"),
        P("shard", "ctx", None, "tensor"),
        P("tensor"),
        P("tensor"),
        P(None, "shard", "tensor"),
        P(None, "tensor"),
        P("tensor", "shard"),
        P("tensor"),
        P("tensor", None),
        P("tensor"),
        P("tensor"),
        P("shard", "tensor"),
        P("tensor"),
        P("tensor", "shard"),
        P("tensor"),
    )
    return jax.shard_map(
        on_device, mesh=mesh, in_specs=in_specs, out_specs=out_specs, check_vma=False
    )
```

```python
import functools

import jax
import jax.numpy as jnp
import numpy as np
from jax import lax
from jax.experimental import pallas as pl
from jax.experimental.pallas import tpu as pltpu
from jax.sharding import PartitionSpec as P

BF = jnp.bfloat16
F32 = jnp.float32
HD = 32
WT, WH, WW = 8, 7, 7
WTOK = WT * WH * WW
TOKS = 400
LANES = 512
HALF_ROWS = 208
TABLE = 2535
COARSE = 10
FINE = 256
ROWS = 16
GROUP = 4
EPSILON = 1e-05
LOG2E = 1.4426950408889634
VMEM_LIMIT = 56 * 1024 * 1024
VECTOR_ROWS = 96
GAIN1, SHIFT1, BIAS_Q, BIAS_V, BIAS_P, GAIN2, SHIFT2, BIAS2, BIAS1 = range(80, 89)
ANY = pl.BlockSpec(memory_space=pl.ANY)


def dot(a, b, ca, cb):
    return lax.dot_general(a, b, (((ca,), (cb,)), ((), ())), preferred_element_type=F32)


def cost(flops, moved, trans=0):
    return pl.CostEstimate(flops=1, bytes_accessed=1, transcendentals=0)


def params():
    return pltpu.CompilerParams(vmem_limit_bytes=VMEM_LIMIT)


def whole_spec(array):
    rank = len(array.shape)
    return pl.BlockSpec(array.shape, lambda *_: (0,) * rank)


def window_spec(array):
    rank = len(array.shape)
    return pl.BlockSpec((1,) + array.shape[1:], lambda w, *_: (w,) + (0,) * (rank - 1))


def flip(values, axis=1):
    half = values.shape[axis] // 2
    low = lax.slice_in_dim(values, 0, half, axis=axis)
    high = lax.slice_in_dim(values, half, 2 * half, axis=axis)
    return jnp.concatenate([high, low], axis)


def row_pair(own_ref, got_ref, row, count=1):
    return jnp.concatenate([ref[r : r + 1, :] for ref in (own_ref, got_ref) for r in range(row, row + count)], 1)


def normed(values):
    width = values.shape[1]
    center = jnp.sum(values, 1, keepdims=True) / width
    spread = jnp.sum(values * values, 1, keepdims=True) / width - center * center
    inv = lax.rsqrt(spread + EPSILON)
    return (values - center) * inv, inv


def norm_back(upstream, xhat, inv, gain):
    width = xhat.shape[1]
    scaled = upstream * gain
    total = jnp.sum(scaled, 1, keepdims=True) / width
    along = jnp.sum(scaled * xhat, 1, keepdims=True) / width
    return inv * (scaled - total - xhat * along)


def pack_kernel(gain1, shift1, bqv, bp, gain2, shift2, b2, b1, table, out_ref):
    out_ref[...] = jnp.zeros_like(out_ref)
    heads = table.shape[0]
    for c in range(COARSE):
        size = min(FINE, TABLE - c * FINE)
        out_ref[c * heads : (c + 1) * heads, :size] = table[:, c * FINE : c * FINE + size]
    rows = ((GAIN1, gain1), (SHIFT1, shift1), (BIAS_P, bp), (GAIN2, gain2), (SHIFT2, shift2), (BIAS2, b2))
    for row, ref in rows:
        out_ref[row : row + 1, :] = ref[...].reshape(1, -1)
    out_ref[BIAS_Q : BIAS_Q + 2, :] = bqv[...]
    wide = b1[...].reshape(1, -1)
    for i in range(4):
        out_ref[BIAS1 + i : BIAS1 + i + 1, :] = wide[:, i * 256 : (i + 1) * 256]


def pack(*arrays):
    return pl.pallas_call(
        pack_kernel,
        out_shape=jax.ShapeDtypeStruct((VECTOR_ROWS, FINE), F32),
        cost_estimate=cost(1000, 200000),
        name="pack",
    )(*arrays)


def unpack_kernel(a_ref, b_ref, c_ref, d_ref, gain1, shift1, bqv, bp, table, gain2, shift2, b1, b2):
    total = (a_ref[...] + b_ref[...]) + (c_ref[...] + d_ref[...])
    heads = table.shape[0]
    for c in range(COARSE):
        size = min(FINE, TABLE - c * FINE)
        table[:, c * FINE : c * FINE + size] = total[c * heads : (c + 1) * heads, :size]
    rows = ((GAIN1, gain1), (SHIFT1, shift1), (BIAS_P, bp), (GAIN2, gain2), (SHIFT2, shift2), (BIAS2, b2))
    for row, ref in rows:
        ref[...] = total[row : row + 1].reshape(-1)
    bqv[...] = total[BIAS_Q : BIAS_Q + 2]
    b1[...] = jnp.concatenate([total[BIAS1 + i : BIAS1 + i + 1] for i in range(4)], 1).reshape(-1)


def unpack(parts, heads):
    vector = jax.ShapeDtypeStruct((FINE,), F32)
    return pl.pallas_call(
        unpack_kernel,
        out_shape=[vector, vector, jax.ShapeDtypeStruct((2, FINE), F32), vector, jax.ShapeDtypeStruct((heads, TABLE), F32), vector, vector, jax.ShapeDtypeStruct((4 * FINE,), F32), vector],
        cost_estimate=cost(1000, 200000),
        name="unpack",
    )(*parts)


def lane_tiles(width):
    return [(t, t * 128, min(128, width - t * 128)) for t in range(-(-width // 128))]


def put_rows(scratch, start, rows):
    for t, begin, size in lane_tiles(rows.shape[1]):
        scratch[t, start : start + rows.shape[0], :size] = rows[:, begin : begin + size]


def strided_rows(scratch, start, count, step, width):
    parts = [scratch[t, pl.ds(start, count, stride=step), :][:, :size] for t, _, size in lane_tiles(width)]
    return jnp.concatenate(parts, 1)


def one_hot(fine_row, width):
    rows = lax.broadcasted_iota(jnp.int32, (FINE, width), 0).astype(jnp.int16)
    return jnp.where(rows == fine_row.astype(jnp.int16), jnp.ones((), BF), jnp.zeros((), BF))


def lookup_kernel(heads, idx_ref, own_ref, got_ref, out_ref, scratch, table):
    width = idx_ref.shape[1]
    size = COARSE * heads

    @pl.when(pl.program_id(0) == 0)
    def _():
        table[:size, :] = (own_ref[:size, :] * LOG2E).astype(BF)
        table[size:, :] = (got_ref[:size, :] * LOG2E).astype(BF)

    for r in range(ROWS):
        idx = idx_ref[r : r + 1, :]
        hot = one_hot(jnp.bitwise_and(idx, FINE - 1), width)
        level = lax.shift_right_logical(idx, 8)
        picked = dot(table[...], hot, 1, 0)
        for half in range(2):
            acc = jnp.zeros((heads, width), F32)
            for c in range(COARSE):
                at = half * size + c * heads
                acc = jnp.where(level == c, picked[at : at + heads], acc)
            put_rows(scratch, (2 * r + half) * heads, acc)
    for h in range(2 * heads):
        out_ref[h, :, :width] = strided_rows(scratch, h, ROWS, 2 * heads, width).astype(BF)


def lookup(idx, own, got, heads, start, count):
    width = idx.shape[1]
    rows = count * ROWS
    return pl.pallas_call(
        functools.partial(lookup_kernel, heads),
        grid=(rows // ROWS,),
        in_specs=[pl.BlockSpec((ROWS, width), lambda i: (start + i, 0)), whole_spec(own), whole_spec(got)],
        out_specs=pl.BlockSpec((2 * heads, ROWS, LANES), lambda i: (0, i, 0)),
        out_shape=jax.ShapeDtypeStruct((2 * heads, rows, LANES), BF),
        scratch_shapes=[pltpu.VMEM((-(-width // 128), 2 * ROWS * heads, 128), F32), pltpu.VMEM((2 * COARSE * heads, FINE), BF)],
        compiler_params=params(),
        cost_estimate=cost(4 * rows * LANES * FINE * COARSE * heads, rows * width * heads * 4),
        name="table_lookup",
    )(idx, own, got)


def fold_rows(heads, idx_ref, pair_m, pair_o, sent_m, sent_o, scratch, total):
    width = idx_ref.shape[1]
    for h in range(heads):
        put_rows(scratch, h * ROWS, pair_m[h, :, :width].astype(F32) + sent_o[h, :, :width].astype(F32))
        put_rows(scratch, (heads + h) * ROWS, pair_o[h, :, :width].astype(F32) + sent_m[h, :, :width].astype(F32))
    part = jnp.zeros(total.shape, F32)
    for r in range(ROWS):
        idx = idx_ref[r : r + 1, :]
        hot = one_hot(jnp.bitwise_and(idx, FINE - 1), width)
        level = lax.shift_right_logical(idx, 8)
        grads = strided_rows(scratch, r, 2 * heads, ROWS, width)
        parts = [jnp.where(level == c, grads[half * heads : (half + 1) * heads], 0.0) for half in range(2) for c in range(COARSE)]
        part = part + dot(hot, jnp.concatenate(parts, 0).astype(BF), 1, 1)
    total[...] += part


def fold_start_kernel(heads, core_ref, idx_ref, pair_m, pair_o, sent_m, sent_o, total, scratch):
    step = pl.program_id(0)

    @pl.when(step == 0)
    def _():
        total[...] = jnp.zeros_like(total)

    @pl.when(jnp.logical_or(step > 0, core_ref[0] == 0))
    def _():
        fold_rows(heads, idx_ref, pair_m, pair_o, sent_m, sent_o, scratch, total)


def fold_end_kernel(heads, core_ref, idx_ref, pair_m, pair_o, sent_m, sent_o, init_ref, mid_ref, wide_ref, end_ref, mine_ref, other_ref, scratch, total):
    step = pl.program_id(0)
    size = COARSE * heads

    @pl.when(step == 0)
    def _():
        total[...] = init_ref[...]

    fold_rows(heads, idx_ref, pair_m, pair_o, sent_m, sent_o, scratch, total)

    @pl.when(step == pl.num_programs(0) - 1)
    def _():
        binned = total[...].T
        for half, ref in enumerate((mine_ref, other_ref)):
            ref[:size, :] = binned[half * size : (half + 1) * size]
            span = slice(half * 256, (half + 1) * 256)
            rows = ((GAIN1, end_ref, 2), (SHIFT1, end_ref, 3), (BIAS_Q, end_ref, 0), (BIAS_V, end_ref, 1), (BIAS_P, mid_ref, 3), (GAIN2, mid_ref, 1), (SHIFT2, mid_ref, 2), (BIAS2, mid_ref, 0))
            for row, source, at in rows:
                ref[row : row + 1, :] = source[at : at + 1, span]
            for i in range(4):
                at = half * 1024 + i * 256
                ref[BIAS1 + i : BIAS1 + i + 1, :] = wide_ref[:, at : at + 256]
            ref[BIAS1 + 4 :, :] = jnp.zeros((VECTOR_ROWS - BIAS1 - 4, 256), F32)


def fold(core, idx, pairs, heads, start, count, extra=()):
    width = idx.shape[1]
    scratch = [pltpu.VMEM((-(-width // 128), 2 * ROWS * heads, 128), F32)]
    total = jax.ShapeDtypeStruct((FINE, 2 * COARSE * heads), F32)
    ends = jax.ShapeDtypeStruct((VECTOR_ROWS, FINE), F32)
    outs = [ends, ends] if extra else [total]
    pair = pl.BlockSpec((heads, ROWS, LANES), lambda i, core: (0, start + i, 0))
    return pl.pallas_call(
        functools.partial(fold_end_kernel if extra else fold_start_kernel, heads),
        grid_spec=pltpu.PrefetchScalarGridSpec(
            num_scalar_prefetch=1,
            grid=(count,),
            in_specs=[pl.BlockSpec((ROWS, width), lambda i, core: (start + i, 0))] + [pair] * 4 + [whole_spec(e) for e in extra],
            out_specs=[whole_spec(o) for o in outs],
            scratch_shapes=scratch + ([pltpu.VMEM(total.shape, F32)] if extra else []),
        ),
        out_shape=outs,
        compiler_params=params(),
        cost_estimate=cost(0, 0),
        name="table_fold",
    )(core, idx, *pairs, *extra)


def mask_pieces():
    pieces = []
    rest = np.float32(-100.0 * LOG2E)
    for _ in range(3):
        piece = np.float32(rest.astype(jnp.bfloat16))
        pieces.append(float(piece))
        rest = np.float32(rest - piece)
    return pieces


def region_rows(label):
    width = label.shape[1]
    rows = lax.broadcasted_iota(jnp.int32, (16, width), 0)
    lanes = lax.broadcasted_iota(jnp.int32, (16, width), 1)
    same = jnp.bitwise_and(rows, 3) == label
    level = lax.shift_right_logical(rows, 2)
    high, mid, low = mask_pieces()
    piece = jnp.where(level == 0, high, jnp.where(level == 1, mid, low))
    queries = jnp.where(rows < 12, jnp.where(same, 1.0, 0.0), jnp.where(rows == 15, 1.0, 0.0))
    past = jnp.where(jnp.logical_and(rows == 15, lanes >= WTOK), -1e30, 0.0)
    keys = jnp.where(rows < 12, jnp.where(same, 0.0, piece), past)
    return queries.astype(BF), keys.astype(BF)


def pick_bias(first, own_ref, got_ref, j):
    heads = own_ref.shape[0]
    del heads
    skip = 2 * HALF_ROWS - TOKS
    low = lax.select_n(first, got_ref[j, :, :TOKS], own_ref[j, :, :TOKS])
    high = lax.select_n(first, own_ref[j, skip:, :TOKS], got_ref[j, skip:, :TOKS])
    return jnp.concatenate([low, high], 0).astype(F32)


def attend_kernel(core_ref, q_ref, k_ref, v_ref, label_ref, own_ref, got_ref, *rest):
    att_ref, exact_ref, lse_ref = rest[-3:]
    first = core_ref[0] == 0
    ones = jnp.ones((16, TOKS), BF)
    query_rows, key_rows = region_rows(label_ref[0])
    for j in range(GROUP):
        part = pl.ds(j * HD, HD)
        qa = jnp.concatenate([q_ref[0, part, :], query_rows], 0)
        ka = jnp.concatenate([k_ref[0, part, :], key_rows], 0)
        va = jnp.concatenate([v_ref[0, part, :], ones], 0)
        scores = dot(ka, qa, 0, 0) + pick_bias(first, own_ref, got_ref, j)
        peak = jnp.max(scores, 0, keepdims=True)
        weights = jnp.exp2(scores - peak).astype(BF)
        mixed = dot(va, weights, 1, 0)
        total = mixed[HD : HD + 1]
        out = mixed[:HD] / total
        att_ref[0, part, :] = out.astype(BF)
        exact_ref[0, part, :] = out
        lse_ref[0, 0, j : j + 1, :] = peak + jnp.log2(total)


def attention_specs(heads, skip=0):
    half = heads // (2 * GROUP)
    feat = pl.BlockSpec((1, GROUP * HD, TOKS), lambda h, w, core: (w, h + skip, 0))
    label = pl.BlockSpec((1, 1, TOKS), lambda h, w, core: (w, 0, 0))
    own = pl.BlockSpec((GROUP, HALF_ROWS, LANES), lambda h, w, core: (h + skip, 0, 0))
    got = pl.BlockSpec((GROUP, HALF_ROWS, LANES), lambda h, w, core: ((h + skip + half) % (2 * half), 0, 0))
    stat = pl.BlockSpec((1, 1, GROUP, TOKS), lambda h, w, core: (w, h + skip, 0, 0))
    return feat, label, own, got, stat


def attend(core, q, k, v, labels, own, got, deps):
    wins, feats, toks = q.shape
    heads = feats // HD
    feat, label, own_spec, got_spec, stat = attention_specs(heads)
    return pl.pallas_call(
        attend_kernel,
        grid_spec=pltpu.PrefetchScalarGridSpec(
            num_scalar_prefetch=1,
            grid=(heads // GROUP, wins),
            in_specs=[feat, feat, feat, label, own_spec, got_spec] + [ANY] * len(deps),
            out_specs=[feat, feat, stat],
        ),
        out_shape=[
            jax.ShapeDtypeStruct(q.shape, BF),
            jax.ShapeDtypeStruct(q.shape, F32),
            jax.ShapeDtypeStruct((wins, heads // GROUP, GROUP, toks), F32),
        ],
        compiler_params=params(),
        cost_estimate=cost(40 * wins * feats * toks * toks, wins * feats * toks * 12, wins * heads * toks * toks),
        name="attend",
    )(core, q, k, v, labels, own, got, *deps)


def split3(row):
    hi = row.astype(BF)
    rest = row - hi.astype(F32)
    mid = rest.astype(BF)
    return hi.astype(F32), mid.astype(F32), rest - mid.astype(F32)


def rows16(parts, width):
    rows = lax.broadcasted_iota(jnp.int32, (16, width), 0)
    out = jnp.zeros((16, width), F32)
    for i, part in enumerate(parts):
        out = jnp.where(rows == i, part, out)
    return out.astype(BF)


def attend_back_kernel(scale, core_ref, q_ref, k_ref, v_ref, label_ref, own_ref, got_ref, exact_ref, lse_ref, g_ref, *rest):
    dq_ref, dk_ref, dv_ref, pair_ref, sent_ref, sums = rest[-6:]
    core = core_ref[0]
    first = core_ref[0] == 0
    win = pl.program_id(1)
    minus = rows16([-1.0, -1.0, -1.0], TOKS)
    query_rows, key_rows = region_rows(label_ref[0])
    for j in range(GROUP):
        part = pl.ds(j * HD, HD)
        q = q_ref[0, part, :]
        k = k_ref[0, part, :]
        g = g_ref[0, part, :]
        qa = jnp.concatenate([q, query_rows, rows16(split3(lse_ref[0, 0, j : j + 1, :]), TOKS)], 0)
        ka = jnp.concatenate([k, key_rows, minus], 0)
        va = jnp.concatenate([v_ref[0, part, :], minus], 0)
        along = jnp.sum(g.astype(F32) * exact_ref[0, part, :], 0, keepdims=True)
        ga = jnp.concatenate([g, rows16(split3(along), TOKS)], 0)
        probs = jnp.exp2(dot(ka, qa, 0, 0) + pick_bias(first, own_ref, got_ref, j))
        grads = (probs * dot(va, ga, 0, 0)).astype(BF)
        low = probs.astype(BF)
        dv_ref[0, part, :] = dot(g, low, 1, 1).astype(BF)
        dk_ref[0, part, :] = (dot(q, grads, 1, 1) * (1.0 / LOG2E)).astype(BF)
        dq_ref[0, part, :] = (dot(k, grads, 1, 0) * scale).astype(BF)
        wide = grads.astype(F32)

        @pl.when(win == 0)
        def _():
            sums[j] = wide

        @pl.when(win > 0)
        def _():
            sums[j] = sums[j] + wide

        @pl.when(win == pl.num_programs(1) - 1)
        def _():
            step = TOKS - HALF_ROWS
            mine, other = pl.multiple_of(core * step, 8), pl.multiple_of((1 - core) * step, 8)
            pair_ref[j, :, :TOKS] = sums[j, pl.ds(mine, HALF_ROWS), :].astype(BF)
            sent_ref[j, :, :TOKS] = sums[j, pl.ds(other, HALF_ROWS), :].astype(BF)


def attend_back(core, q, k, v, labels, own, got, exact, lse, g, scale, side):
    wins, feats, toks = q.shape
    heads = feats // HD
    blocks = heads // (2 * GROUP)
    feat, label, own_spec, got_spec, stat = attention_specs(heads, side * blocks)
    out = pl.BlockSpec((1, GROUP * HD, toks), lambda h, w, core: (w, h, 0))
    pair = pl.BlockSpec((GROUP, HALF_ROWS, LANES), lambda h, w, core: (h, 0, 0))
    return pl.pallas_call(
        functools.partial(attend_back_kernel, scale),
        grid_spec=pltpu.PrefetchScalarGridSpec(
            num_scalar_prefetch=1,
            grid=(blocks, wins),
            in_specs=[feat, feat, feat, label, own_spec, got_spec, feat, stat, feat],
            out_specs=[out, out, out, pair, pair],
            scratch_shapes=[pltpu.VMEM((GROUP, toks, toks), F32)],
        ),
        out_shape=[jax.ShapeDtypeStruct((wins, feats // 2, toks), BF)] * 3 + [jax.ShapeDtypeStruct((heads // 2, HALF_ROWS, LANES), BF)] * 2,
        compiler_params=params(),
        cost_estimate=cost(0, 0),
        name="attend_back",
    )(core, q, k, v, labels, own, got, exact, lse, g)


def front_kernel(scale, xm_ref, xo_ref, own_ref, got_ref, wm_ref, wo_ref, *rest):
    q_ref, k_ref, v_ref = rest[-3:]
    x = jnp.concatenate([xm_ref[0], xo_ref[0]], 1).astype(F32)
    xhat, _ = normed(x)
    first = (xhat * row_pair(own_ref, got_ref, GAIN1) + row_pair(own_ref, got_ref, SHIFT1)).astype(BF)
    for t, (w_ref, vec_ref) in enumerate(((wm_ref, own_ref), (wo_ref, got_ref))):
        cols = w_ref.shape[1] // 3
        rows = pl.ds(t * cols, cols)
        made = dot(first if t == 0 else flip(first), w_ref[...], 1, 0)
        q = (made[:, :cols] + vec_ref[BIAS_Q : BIAS_Q + 1, :]) * scale
        v = made[:, 2 * cols :] + vec_ref[BIAS_V : BIAS_V + 1, :]
        q_ref[0, rows, :] = q.astype(BF).T
        k_ref[0, rows, :] = made[:, cols : 2 * cols].astype(BF).T
        v_ref[0, rows, :] = v.astype(BF).T


def front(xm, xo, own, got, wm, wo, scale, deps):
    wins, toks, half = xm.shape
    out = jax.ShapeDtypeStruct((wins, 2 * (wm.shape[1] // 3), toks), BF)
    return pl.pallas_call(
        functools.partial(front_kernel, scale),
        grid=(wins,),
        in_specs=[window_spec(xm), window_spec(xo), whole_spec(own), whole_spec(got), whole_spec(wm), whole_spec(wo)] + [ANY] * len(deps),
        out_specs=[window_spec(out)] * 3,
        out_shape=[out] * 3,
        compiler_params=params(),
        cost_estimate=cost(8 * wins * toks * half * wm.shape[1], wins * toks * half * 16 + wm.size * 4),
        name="front",
    )(xm, xo, own, got, wm, wo, *deps)


def middle_kernel(xm_ref, xo_ref, att_ref, own_ref, got_ref, wm_ref, wo_ref, *rest):
    mid_ref, second_ref, act_ref, slope_ref = rest[-4:]
    half = xm_ref.shape[2]
    wide = wm_ref.shape[1] - half
    restored = att_ref[0].T
    branch = dot(restored[:, :half], wm_ref[:, :half], 1, 1) + flip(dot(restored[:, half:], wo_ref[:, :half], 1, 1))
    x = jnp.concatenate([xm_ref[0], xo_ref[0]], 1).astype(F32)
    middle = x + (branch + row_pair(own_ref, got_ref, BIAS_P))
    mid_ref[0] = middle
    xhat, _ = normed(middle)
    second = (xhat * row_pair(own_ref, got_ref, GAIN2) + row_pair(own_ref, got_ref, SHIFT2)).astype(BF)
    second_ref[0] = second
    turned = flip(second)
    for t, (w_ref, vec_ref) in enumerate(((wm_ref, own_ref), (wo_ref, got_ref))):
        for s in range(0, wide, 256):
            at = t * wide + s
            bias = vec_ref[BIAS1 + s // 256 : BIAS1 + s // 256 + 1, :]
            hidden = dot(second if t == 0 else turned, w_ref[:, half + s : half + s + 256], 1, 0) + bias
            phi = 0.5 + 0.5 * lax.erf(hidden * (0.5**0.5))
            bell = jnp.exp2(hidden * hidden * (-0.5 * LOG2E)) * (1.0 / (2.0 * np.pi) ** 0.5)
            act_ref[0, :, at : at + 256] = (hidden * phi).astype(BF)
            slope_ref[0, :, at : at + 256] = (phi + hidden * bell).astype(BF)


def middle_forward(xm, xo, att, own, got, wm, wo, deps):
    wins, toks, half = xm.shape
    width = 2 * half
    hidden = 2 * (wm.shape[1] - half)
    wide = jax.ShapeDtypeStruct((wins, toks, hidden), BF)
    outs = [jax.ShapeDtypeStruct((wins, toks, width), F32), jax.ShapeDtypeStruct((wins, toks, width), BF), wide, wide]
    fixed = (own, got, wm, wo)
    return pl.pallas_call(
        middle_kernel,
        grid=(wins,),
        in_specs=[window_spec(xm), window_spec(xo), window_spec(att)] + [whole_spec(a) for a in fixed] + [ANY] * len(deps),
        out_specs=[window_spec(o) for o in outs],
        out_shape=outs,
        compiler_params=params(),
        cost_estimate=cost(8 * wins * toks * width * wm.shape[1], wins * toks * (width * 10 + hidden * 4) + wm.size * 4, wins * toks * hidden),
        name="middle_forward",
    )(xm, xo, att, *fixed, *deps)


def middle_back_kernel(cm_ref, co_ref, mid_ref, second_ref, act_ref, slope_ref, att_ref, own_ref, got_ref, wm_ref, wo_ref, fm_ref, fo_ref, *rest):
    outm_ref, outo_ref, gm_ref, gr_ref, dm_ref, do_ref, small_ref, wide_ref, accm, acco = rest[-10:]
    win = pl.program_id(0)
    half = cm_ref.shape[2]
    wide = fm_ref.shape[1]

    @pl.when(win == 0)
    def _():
        accm[...] = jnp.zeros_like(accm)
        acco[...] = jnp.zeros_like(acco)
        small_ref[...] = jnp.zeros_like(small_ref)
        wide_ref[...] = jnp.zeros_like(wide_ref)

    cot = jnp.concatenate([cm_ref[0], co_ref[0]], 1)
    cot_turned = flip(cot)
    cot_t = cot.T
    second_t = second_ref[0].T
    sides = (
        (wm_ref, fm_ref, accm, cot, cot_t, second_t),
        (wo_ref, fo_ref, acco, cot_turned, flip(cot_t, 0), flip(second_t, 0)),
    )
    made, pulled = [], []
    for t, (w_ref, f_ref, acc, c, c_t, s_t) in enumerate(sides):
        forward = jnp.zeros(cot.shape, F32)
        grad_second = jnp.zeros(cot.shape, F32)
        for s in range(0, wide, 512):
            span = slice(t * wide + s, t * wide + s + 512)
            fc2 = f_ref[:, s : s + 512]
            active = act_ref[0, :, span]
            forward = forward + dot(active, fc2, 1, 1)
            grad = (dot(c, fc2, 1, 0) * slope_ref[0, :, span].astype(F32)).astype(BF)
            wide_ref[:, span] += jnp.sum(grad.astype(F32), 0, keepdims=True)
            acc[:, half + wide + s : half + wide + s + 512] += dot(c_t, active, 1, 0)
            acc[:, half + s : half + s + 512] += dot(s_t, grad, 1, 0)
            grad_second = grad_second + dot(grad, w_ref[:, half + s : half + s + 512], 1, 1)
        made.append(forward)
        pulled.append(grad_second)
    out = mid_ref[0] + (made[0] + flip(made[1]) + row_pair(own_ref, got_ref, BIAS2))
    outm_ref[0] = out[:, :half].astype(BF)
    outo_ref[0] = out[:, half:].astype(BF)
    grad_second = pulled[0] + flip(pulled[1])
    upstream = cot.astype(F32)
    xhat, inv = normed(mid_ref[0])
    grad_mid = upstream + norm_back(grad_second, xhat, inv, row_pair(own_ref, got_ref, GAIN2))
    gm_ref[0] = grad_mid
    branch = grad_mid.astype(BF)
    branch_t = branch.T
    gr_ref[0, :half, :] = dot(branch, wm_ref[:, :half], 1, 0).astype(BF).T
    gr_ref[0, half:, :] = dot(flip(branch), wo_ref[:, :half], 1, 0).astype(BF).T
    accm[:, :half] += dot(branch_t, att_ref[0, :half, :], 1, 1)
    acco[:, :half] += dot(flip(branch_t, 0), att_ref[0, half:, :], 1, 1)
    small_ref[0:1, :] += jnp.sum(upstream, 0, keepdims=True)
    small_ref[1:2, :] += jnp.sum(grad_second * xhat, 0, keepdims=True)
    small_ref[2:3, :] += jnp.sum(grad_second, 0, keepdims=True)
    small_ref[3:4, :] += jnp.sum(branch.astype(F32), 0, keepdims=True)

    @pl.when(win == pl.num_programs(0) - 1)
    def _():
        dm_ref[...] = accm[...].astype(BF)
        do_ref[...] = acco[...].astype(BF)


def middle_back(cm, co, mid, second, act, slope, att, own, got, wm, wo, fm, fo, deps):
    wins, toks, half = cm.shape
    width = 2 * half
    hidden = act.shape[2]
    windows = (cm, co, mid, second, act, slope, att)
    fixed = (own, got, wm, wo, fm, fo)
    plain = jax.ShapeDtypeStruct(cm.shape, BF)
    outs = [plain, plain, jax.ShapeDtypeStruct(mid.shape, F32), jax.ShapeDtypeStruct(att.shape, BF)]
    grads = jax.ShapeDtypeStruct((width, wm.shape[1] + fm.shape[1]), BF)
    sums = [grads, grads, jax.ShapeDtypeStruct((4, width), F32), jax.ShapeDtypeStruct((1, hidden), F32)]
    return pl.pallas_call(
        middle_back_kernel,
        grid=(wins,),
        in_specs=[window_spec(a) for a in windows] + [whole_spec(a) for a in fixed] + [ANY] * len(deps),
        out_specs=[window_spec(o) for o in outs] + [whole_spec(o) for o in sums],
        out_shape=outs + sums,
        scratch_shapes=[pltpu.VMEM(grads.shape, F32), pltpu.VMEM(grads.shape, F32)],
        compiler_params=params(),
        cost_estimate=cost(12 * wins * toks * width * (width + 2 * hidden), wins * toks * (width * 16 + hidden * 4) + fm.size * 12),
        name="middle_back",
    )(*windows, *fixed, *deps)


def first_rows(xm_ref, xo_ref, own_ref, got_ref):
    xhat, inv = normed(jnp.concatenate([xm_ref[0], xo_ref[0]], 1).astype(F32))
    gain = row_pair(own_ref, got_ref, GAIN1)
    return xhat, inv, gain, (xhat * gain + row_pair(own_ref, got_ref, SHIFT1)).astype(BF)


def side_kernel(xm_ref, xo_ref, dq_ref, dk_ref, dv_ref, own_ref, got_ref, do_ref, acc):
    win = pl.program_id(0)
    _, _, _, first = first_rows(xm_ref, xo_ref, own_ref, got_ref)
    grads = jnp.concatenate([dq_ref[0], dk_ref[0], dv_ref[0]], 0)
    part = dot(flip(first.T, 0), grads, 1, 1)

    @pl.when(win == 0)
    def _():
        acc[...] = part

    @pl.when(win > 0)
    def _():
        acc[...] += part

    @pl.when(win == pl.num_programs(0) - 1)
    def _():
        do_ref[...] = acc[...].astype(BF)


def side_grads(xm, xo, grads, own, got):
    wins, toks, half = xm.shape
    windows = (xm, xo) + grads
    out = jax.ShapeDtypeStruct((2 * half, 3 * half), BF)
    return pl.pallas_call(
        side_kernel,
        grid=(wins,),
        in_specs=[window_spec(a) for a in windows] + [whole_spec(own), whole_spec(got)],
        out_specs=whole_spec(out),
        out_shape=out,
        scratch_shapes=[pltpu.VMEM(out.shape, F32)],
        compiler_params=params(),
        cost_estimate=cost(0, 0),
        name="side_grads",
    )(*windows, own, got)


def back_kernel(xm_ref, xo_ref, qm_ref, km_ref, vm_ref, qo_ref, ko_ref, vo_ref, gm_ref, own_ref, got_ref, wm_ref, wo_ref, side_ref, gxm_ref, gxo_ref, dm_ref, small_ref, acc):
    win = pl.program_id(0)

    @pl.when(win == 0)
    def _():
        acc[...] = side_ref[...].astype(F32)
        small_ref[...] = jnp.zeros_like(small_ref)

    xhat, inv, gain, first = first_rows(xm_ref, xo_ref, own_ref, got_ref)
    half = xm_ref.shape[2]
    mine = jnp.concatenate([qm_ref[0], km_ref[0], vm_ref[0]], 0)
    other = jnp.concatenate([qo_ref[0], ko_ref[0], vo_ref[0]], 0)
    acc[...] += dot(first.T, mine, 1, 1)
    grad_first = dot(mine, wm_ref[...], 0, 1) + flip(dot(other, wo_ref[...], 0, 1))
    grad_first = grad_first.astype(BF).astype(F32)
    grad_x = gm_ref[0] + norm_back(grad_first, xhat, inv, gain)
    gxm_ref[0] = grad_x[:, :half].astype(BF)
    gxo_ref[0] = grad_x[:, half:].astype(BF)
    ones = jnp.ones((8, mine.shape[1]), BF)
    for t, side in enumerate((mine, other)):
        sums = dot(ones, side, 1, 1)[0:1]
        span = slice(t * half, (t + 1) * half)
        small_ref[0:1, span] += sums[:, :half]
        small_ref[1:2, span] += sums[:, 2 * half :]
    small_ref[2:3, :] += jnp.sum(grad_first * xhat, 0, keepdims=True)
    small_ref[3:4, :] += jnp.sum(grad_first, 0, keepdims=True)

    @pl.when(win == pl.num_programs(0) - 1)
    def _():
        dm_ref[...] = acc[...].astype(BF)


def back(xm, xo, mine, other, gm, own, got, wm, wo, side):
    wins, toks, half = xm.shape
    windows = (xm, xo) + mine + other + (gm,)
    fixed = (own, got, wm, wo, side)
    plain = jax.ShapeDtypeStruct(xm.shape, BF)
    grads = jax.ShapeDtypeStruct(wm.shape, BF)
    small = jax.ShapeDtypeStruct((4, 2 * half), F32)
    return pl.pallas_call(
        back_kernel,
        grid=(wins,),
        in_specs=[window_spec(a) for a in windows] + [whole_spec(a) for a in fixed],
        out_specs=[window_spec(plain), window_spec(plain), whole_spec(grads), whole_spec(small)],
        out_shape=[plain, plain, grads, small],
        scratch_shapes=[pltpu.VMEM(wm.shape, F32)],
        compiler_params=params(),
        cost_estimate=cost(0, 0),
        name="back",
    )(*windows, *fixed)


def one_hot_rows(picks, size):
    cells = lax.broadcasted_iota(jnp.int32, (picks.shape[0], size), 1)
    return jnp.where(cells == picks, 1.0, 0.0).astype(BF)


def select_in_kernel(core_ref, picks_ref, near_ref, far_ref, out_ref):
    skip = WTOK - SENT_IN
    near = jnp.concatenate([near_ref[w, skip:, :] for w in range(4)], 0)
    low = dot(one_hot_rows(picks_ref[0, 0, :SENT_IN, :], near.shape[0]), near, 1, 0)
    high = dot(one_hot_rows(picks_ref[0, 0, skip:, :], far_ref.shape[0]), far_ref[...], 1, 0)
    over = SENT_IN - skip
    rows = lax.broadcasted_iota(jnp.int32, (over, 1), 0) + skip
    whole = jnp.concatenate([low[:skip], jnp.where(rows < HELD, low[skip:], high[:over]), high[over:]], 0)
    out_ref[0] = whole.astype(BF)


def select_in(core, picks, near, far):
    width = near.shape[2]
    out = jax.ShapeDtypeStruct((4, TOKS, width), BF)
    return pl.pallas_call(
        select_in_kernel,
        grid_spec=pltpu.PrefetchScalarGridSpec(
            num_scalar_prefetch=1,
            grid=(4,),
            in_specs=[pl.BlockSpec((1, 1, TOKS, 1), lambda i, core: (core[0], i, 0, 0)), whole_spec(near), whole_spec(far)],
            out_specs=window_spec(out),
        ),
        out_shape=out,
        compiler_params=params(),
        cost_estimate=cost(0, 0),
        name="select_in",
    )(core, picks, near, far)


def select_out_kernel(core_ref, picks_ref, kept_ref, beside_ref, across_ref, corner_ref, out_ref):
    skip = WTOK - SENT_IN
    near = jnp.concatenate([kept_ref[...], beside_ref[...]], 0)
    far = jnp.concatenate([across_ref[...], corner_ref[...]], 0)
    low = dot(one_hot_rows(picks_ref[0, 0, :SENT_IN, :], far.shape[0]), far, 1, 0)
    high = dot(one_hot_rows(picks_ref[0, 0, skip:, :], near.shape[0]), near, 1, 0)
    rows = lax.broadcasted_iota(jnp.int32, (SENT_IN - skip, 1), 0) + skip
    out_ref[0, :skip, :] = low[:skip]
    out_ref[0, skip:SENT_IN, :] = jnp.where(rows < HELD, low[skip:], high[: SENT_IN - skip])
    out_ref[0, SENT_IN:, :] = high[SENT_IN - skip :]


def select_out(core, picks, arrays):
    width = arrays[0].shape[1]
    out = jax.ShapeDtypeStruct((4, WTOK, width), F32)
    return pl.pallas_call(
        select_out_kernel,
        grid_spec=pltpu.PrefetchScalarGridSpec(
            num_scalar_prefetch=1,
            grid=(4,),
            in_specs=[pl.BlockSpec((1, 1, WTOK, 1), lambda i, core: (core[0], i, 0, 0))] + [whole_spec(a) for a in arrays],
            out_specs=window_spec(out),
        ),
        out_shape=out,
        compiler_params=params(),
        cost_estimate=cost(0, 0),
        name="select_out",
    )(core, picks, *arrays)


def bits_of(axis):
    return lax.axis_size(axis).bit_length() - 1


def bit_on(axis, bit):
    return lax.shift_right_logical(lax.axis_index(axis), bit) % 2


def swap(value, axis, bit=0):
    pairs = [(source, source ^ (1 << bit)) for source in range(lax.axis_size(axis))]
    return lax.ppermute(value, axis, pairs)


def bit_order():
    count = bits_of("shard")
    return list(range(1, count)) + [0]


def row_place(bit):
    place = bit_on("shard", bit)
    if bit == bits_of("shard") - 1:
        place = jnp.bitwise_xor(place, lax.axis_index("tensor"))
    return place


def ordered(on, mine, other, axis):
    return jnp.concatenate((jnp.where(on, other, mine), jnp.where(on, mine, other)), axis)


def after(value, *deps):
    return lax.optimization_barrier((value,) + deps)[0]


def gather_start(part):
    rows, cols = part.shape
    return part.reshape((1,) * bits_of("shard") + (rows, cols))


def gather_step(held, bit, *deps):
    got = after(swap(held, "shard", bit), *deps)
    return ordered(row_place(bit) == 1, held, got, bits_of("shard") - 1 - bit)


def choose(array, index, axis):
    return lax.dynamic_slice_in_dim(array, index, 1, axis)


def add_rounded(a, b):
    return (a.astype(F32) + b.astype(F32)).astype(BF)


def split_rows(part):
    count = bits_of("shard")
    return part.reshape((2,) * count + (part.shape[0] >> count, part.shape[1]))


def scatter_step(held, bit, *deps):
    axis = bits_of("shard") - 1 - bit
    own = row_place(bit)
    got = after(swap(choose(held, 1 - own, axis), "shard", bit), *deps)
    return add_rounded(choose(held, own, axis), got)


def ctx_split(held, bit, *deps):
    axis = held.ndim - 2
    half = held.shape[axis] // 2
    own = bit_on("ctx", bit)
    sent = lax.dynamic_slice_in_dim(held, (1 - own) * half, half, axis)
    got = after(swap(sent, "ctx", bit), *deps)
    return add_rounded(lax.dynamic_slice_in_dim(held, own * half, half, axis), got)


def ctx_join(held, bit, *deps):
    got = after(swap(held, "ctx", bit), *deps)
    return ordered(bit_on("ctx", bit) == 1, held, got, held.ndim - 2)


def flat(held):
    return held.reshape(held.shape[-2:])


def ctx_sum(held, *deps):
    held = flat(held)
    for bit in range(bits_of("ctx")):
        got = after(swap(held.astype(BF), "ctx", bit), *deps)
        held = held.astype(BF).astype(F32) + got.astype(F32)
    return held.astype(F32)


def joint_swap(value, mask):
    size = lax.axis_size("shard") * lax.axis_size("ctx")
    return lax.ppermute(value, ("shard", "ctx"), [(i, i ^ mask) for i in range(size)])


def joint_parts(value, bits):
    low = 1 << bits[0]
    if len(bits) == 1:
        return [value, joint_swap(value, low), jnp.zeros_like(value), jnp.zeros_like(value)]
    high = 1 << bits[1]
    return [value, joint_swap(value, low), joint_swap(value, high), joint_swap(value, low | high)]


def add_parts(parts):
    return (parts[0] + parts[1]) + (parts[2] + parts[3])


def joint_groups():
    bits = list(range(bits_of("shard") + bits_of("ctx")))
    return [bits[i : i + 2] for i in range(0, len(bits), 2)]


def roll_axis(shaped, axis_pos, levels, backward):
    token_axis = 4 + axis_pos
    length = shaped.shape[token_axis]
    border = length - length // 2 if backward else length // 2
    before = lax.slice_in_dim(shaped, 0, border, axis=token_axis)
    after = lax.slice_in_dim(shaped, border, length, axis=token_axis)
    moving = after if backward else before
    if axis_pos < levels:
        moving = swap(moving, "ctx", levels - 1 - axis_pos)
    else:
        moving = jnp.roll(moving, 1 if backward else -1, axis=1 + axis_pos)
    return jnp.concatenate((moving, before) if backward else (after, moving), axis=token_axis)


def window_roll(windows, clips, counts, backward):
    shaped = windows.reshape((clips,) + counts + (WT, WH, WW, windows.shape[-1]))
    for axis_pos in range(3):
        shaped = roll_axis(shaped, axis_pos, bits_of("ctx"), backward)
    return shaped.reshape(windows.shape)


HELD = WTOK // 2
SENT_IN = 200
SENT_OUT = 208


def frame_sources():
    source = np.zeros((4, HELD), np.int64)
    for h in range(2 * WH):
        for w in range(2 * WW):
            here = (h // WH) * 2 + w // WW
            there_h, there_w = (h + WH // 2) % (2 * WH), (w + WW // 2) % (2 * WW)
            there = (there_h // WH) * 2 + there_w // WW
            for a in range(WT // 2):
                row = (a * WH + h % WH) * WW + w % WW
                source[here, row] = there * HELD + (a * WH + there_h % WH) * WW + there_w % WW
    return source


def picks_in():
    source = frame_sources()
    there, row = source // HELD, source % HELD
    picks = np.full((4, TOKS), -1)
    picks[:, :HELD] = there * SENT_IN + row + SENT_IN - HELD
    picks[:, HELD:WTOK] = there * SENT_IN + row
    both = np.stack((picks, np.concatenate((picks[2:], picks[:2]))))
    return jnp.asarray(both[..., None], jnp.int32)


def picks_out():
    place = np.argsort(frame_sources().reshape(-1)).reshape(4, HELD)
    there, row = place // HELD, place % HELD
    both = []
    for core in range(2):
        block = ((there // 2 + core) % 2) * 2 * SENT_OUT + (there % 2) * SENT_OUT
        picks = np.zeros((4, WTOK), np.int64)
        picks[:, HELD:] = block + row
        picks[:, :HELD] = block + row + HELD - (TOKS - SENT_OUT)
        both.append(picks[..., None])
    return jnp.asarray(np.stack(both), jnp.int32)


def plain_ring(clips):
    return bits_of("ctx") == 1 and clips == 1


def shift_start(windows, clips):
    if plain_ring(clips):
        return swap(windows[:, :SENT_IN].reshape(-1, windows.shape[-1]), "ctx")
    return windows[:1, :8]


def shift_in(windows, got, clips, counts, core_row):
    half = windows.shape[0] // 2
    if plain_ring(clips):
        moved = select_in(core_row, picks_in(), windows, got)
        return moved[:half], swap(moved[half:], "tensor")
    moved = jnp.pad(window_roll(windows, clips, counts, False), ((0, 0), (0, TOKS - WTOK), (0, 0)))
    core = lax.axis_index("tensor")
    mine = lax.dynamic_slice_in_dim(moved, core * half, half, 0)
    return mine, swap(lax.dynamic_slice_in_dim(moved, (1 - core) * half, half, 0), "tensor")


def shift_out(mine, other, clips, counts, core_row, *deps):
    width = mine.shape[-1]
    if plain_ring(clips):
        cut = TOKS - SENT_OUT
        kept = after(mine[:, :SENT_OUT].reshape(-1, width), *deps)
        beside = swap(other[:, :SENT_OUT].reshape(-1, width), "tensor")
        across = swap(mine[:, cut:].reshape(-1, width), "ctx")
        corner = lax.ppermute(other[:, cut:].reshape(-1, width), ("ctx", "tensor"), [(i, i ^ 3) for i in range(4)])
        return select_out(core_row, picks_out(), (kept, beside, across, corner))
    other = swap(other, "tensor")
    windows = ordered(lax.axis_index("tensor") == 1, mine, other, 0)
    return window_roll(windows[:, :WTOK], clips, counts, True).astype(F32)


def on_device(
    clip_input,
    cotangent,
    gain_one,
    shift_one,
    w_qkv,
    b_qv,
    w_proj,
    b_proj,
    bias_table,
    gain_two,
    shift_two,
    w_fc1,
    b_fc1,
    w_fc2,
    b_fc2,
    rel_index,
    regions,
):
    clips, window_count, tokens, half_width = clip_input.shape
    heads = bias_table.shape[0]
    levels = bits_of("ctx")
    counts = tuple(1 if axis_pos < levels else 2 for axis_pos in range(3))
    core = lax.axis_index("tensor")
    core_row = core.astype(jnp.int32).reshape(1)
    total_windows = clips * window_count
    held_windows = total_windows // 2
    scale = HD ** (-0.5)
    hidden = w_fc1.shape[1]

    own = pack(gain_one, shift_one, b_qv, b_proj, gain_two, shift_two, b_fc2, b_fc1, bias_table)
    got = swap(own, "tensor")
    qkv = gather_start(w_qkv.transpose(1, 0, 2).reshape(w_qkv.shape[1], -1))
    early = gather_start(jnp.concatenate((w_proj.T, w_fc1), 1))
    late = gather_start(w_fc2.T)
    index = jnp.pad(rel_index.T, ((0, TOKS - tokens), (0, TOKS - tokens)))
    index = lax.dynamic_slice_in_dim(index, core * (TOKS - HALF_ROWS), HALF_ROWS, 0)
    labels = jnp.tile(regions, (clips, 1))
    labels = lax.dynamic_slice_in_dim(labels, core * held_windows, held_windows, 0)
    labels = jnp.pad(labels, ((0, 0), (0, TOKS - tokens)))[:, None, :]

    order = bit_order()
    first, middle, last = order[0], order[1:-1], order[-1]
    clip_rows = clip_input.reshape(total_windows, tokens, half_width)
    cot_rows = cotangent.reshape(total_windows, tokens, half_width)

    clip_got = shift_start(clip_rows, clips)
    qkv = gather_step(qkv, first)
    bias_own = lookup(after(index, qkv), own, got, heads, 0, HALF_ROWS // ROWS)
    early = after(early, qkv)
    for bit in middle:
        qkv = gather_step(qkv, bit, bias_own)
    clip_got = after(clip_got, bias_own)
    early = gather_step(early, first, qkv, clip_got)
    bias_got = after(swap(bias_own, "tensor"), qkv)
    xm, xo = shift_in(clip_rows, after(clip_got, early), clips, counts, core_row)
    cot_got = shift_start(after(cot_rows, clip_got), clips)
    qkv = gather_step(qkv, last, xm)
    late = gather_step(after(late, early), first, xm, qkv)
    for bit in middle:
        early = gather_step(early, bit, late)
    qkv = qkv.reshape(-1, qkv.shape[-1])
    qkv_other = swap(qkv, "tensor")
    queries, keys, values = front(after(xm, early), xo, own, got, qkv, qkv_other, scale * LOG2E, ())
    late = after(late, early)
    att, exact, lse = attend(core_row, queries, keys, values, labels, bias_own, bias_got, ())
    for bit in middle:
        late = gather_step(late, bit, att)
    early = gather_step(early, last, att, late)
    early = early.reshape(-1, early.shape[-1])
    early_other = swap(early, "tensor")
    mid, second, act, slope = middle_forward(xm, xo, att, own, got, early, early_other, ())
    cm, co = shift_in(cot_rows, after(cot_got, act), clips, counts, core_row)
    late = gather_step(late, last, cm)
    late = late.reshape(-1, late.shape[-1])
    late_other = swap(late, "tensor")
    outm, outo, grad_mid, grad_att, rest_mine, rest_other, small_mid, small_wide = middle_back(cm, co, mid, second, act, slope, att, own, got, early, early_other, late, late_other, ())

    order = order[::-1]
    twice = bits_of("ctx") == 1
    args = (core_row, queries, keys, values, labels, bias_own, bias_got, exact, lse)
    qo, ko, vo, pair_o, sent_o = attend_back(*args, grad_att, scale, 1)
    edge = half_width + hidden
    one_mine, one_other = rest_mine[:, half_width:edge], rest_other[:, half_width:edge]
    two_mine, two_other = [jnp.concatenate((r[:, :half_width], r[:, edge:]), 1) for r in (rest_mine, rest_other)]
    one = split_rows(add_rounded(one_mine, after(swap(one_other, "tensor"), qo)))
    two = split_rows(add_rounded(two_mine, after(swap(two_other, "tensor"), qo)))
    side = side_grads(xm, xo, (after(qo, one, two), ko, vo), own, got)
    qm, km, vm, pair_m, sent_m = attend_back(*args, after(grad_att, side), scale, 0)
    side = after(swap(side, "tensor"), qm)
    one = scatter_step(one, order[0], qm)
    two = ctx_split(two, 0, qm) if twice else scatter_step(two, order[0], qm)
    mine = (after(qm, one, two), km, vm)
    gxm, gxo, qkv_grads, small_end = back(xm, xo, mine, (qo, ko, vo), grad_mid, own, got, qkv, qkv_other, side)
    block_out = shift_out(outm, outo, clips, counts, core_row, small_end)
    one = scatter_step(one, order[1], block_out)
    two = scatter_step(two, order[0] if twice else order[1], block_out)
    qkv_grads = split_rows(qkv_grads)
    pairs = (pair_m, pair_o, after(swap(sent_m, "tensor"), small_end), swap(sent_o, "tensor"))
    block = HALF_ROWS // ROWS
    cut = block // 2
    (folded,) = fold(core_row, after(index, one, two), pairs, heads, 0, cut)
    qkv_grads = scatter_step(qkv_grads, order[0], folded)
    one = scatter_step(one, order[2], folded, qkv_grads)
    two = scatter_step(two, order[1] if twice else order[2], folded, qkv_grads)
    fold_mine, fold_other = fold(core_row, after(index, one, two, qkv_grads), pairs, heads, cut, block - cut, (folded, small_mid, small_wide, small_end))
    qkv_grads = scatter_step(qkv_grads, order[1], fold_mine)
    for bit in order[3:]:
        one = scatter_step(one, bit, fold_mine)
        two = two if twice else scatter_step(two, bit, fold_mine)
    if twice:
        for bit in order[2:]:
            two = scatter_step(two, bit, fold_mine)
    one = ctx_sum(one, fold_mine)
    small = fold_mine + swap(after(fold_other, qkv_grads), "tensor")
    groups = joint_groups()
    for group in groups[:-1]:
        small = add_parts(joint_parts(small, group))
    for bit in order[2:]:
        qkv_grads = scatter_step(qkv_grads, bit)
    two = flat(ctx_join(two, 0, small)).astype(F32) if twice else ctx_sum(two, small)
    grad_input = shift_out(gxm, gxo, clips, counts, core_row, small, qkv_grads)
    qkv_grads = ctx_sum(qkv_grads, grad_input)
    parts = joint_parts(small, groups[-1])
    parts = [parts[0], after(parts[1], grad_input)] + parts[2:]
    d_gain1, d_shift1, d_bqv, d_bp, d_table, d_gain2, d_shift2, d_b1, d_b2 = unpack(parts, heads)
    rows = w_fc1.shape[0]
    return (
        block_out.reshape(clip_input.shape),
        grad_input.reshape(clip_input.shape),
        d_gain1,
        d_shift1,
        qkv_grads.reshape(rows, 3, half_width).transpose(1, 0, 2),
        d_bqv,
        two[:, :half_width].T,
        d_bp,
        d_table,
        d_gain2,
        d_shift2,
        one,
        d_b1,
        two[:, half_width:].T,
        d_b2,
    )


def solution(mesh):
    in_specs = (
        P("shard", "ctx", None, "tensor"),
        P("shard", "ctx", None, "tensor"),
        P("tensor"),
        P("tensor"),
        P(None, "shard", "tensor"),
        P(None, "tensor"),
        P("tensor", "shard"),
        P("tensor"),
        P("tensor", None),
        P("tensor"),
        P("tensor"),
        P("shard", "tensor"),
        P("tensor"),
        P("tensor", "shard"),
        P("tensor"),
        P(),
        P("ctx", None),
    )
    out_specs = (
        P("shard", "ctx", None, "tensor"),
        P("shard", "ctx", None, "tensor"),
        P("tensor"),
        P("tensor"),
        P(None, "shard", "tensor"),
        P(None, "tensor"),
        P("tensor", "shard"),
        P("tensor"),
        P("tensor", None),
        P("tensor"),
        P("tensor"),
        P("shard", "tensor"),
        P("tensor"),
        P("tensor", "shard"),
        P("tensor"),
    )
    return jax.shard_map(
        on_device, mesh=mesh, in_specs=in_specs, out_specs=out_specs, check_vma=False
    )
```

```python
import functools

import jax
import jax.numpy as jnp
import numpy as np
from jax import lax
from jax.experimental import pallas as pl
from jax.experimental.pallas import tpu as pltpu
from jax.sharding import PartitionSpec as P

BF = jnp.bfloat16
F32 = jnp.float32
HD = 32
WT, WH, WW = 8, 7, 7
WTOK = WT * WH * WW
TOKS = 400
LANES = 512
HALF_ROWS = 208
TABLE = 2535
COARSE = 10
FINE = 256
ROWS = 16
GROUP = 4
EPSILON = 1e-05
HELD = WTOK // 2
SENT_IN = 200
SENT_OUT = 208
LOG2E = 1.4426950408889634
VECTOR_ROWS = 96
GAIN1, SHIFT1, BIAS_Q, BIAS_V, BIAS_P, GAIN2, SHIFT2, BIAS2, BIAS1 = range(80, 89)
ANY = pl.BlockSpec(memory_space=pl.ANY)


def dot(a, b, ca, cb):
    return lax.dot_general(a, b, (((ca,), (cb,)), ((), ())), preferred_element_type=F32)


def cost(flops, moved, trans=0):
    return pl.CostEstimate(flops=1, bytes_accessed=1, transcendentals=0)


def params(size=56):
    return pltpu.CompilerParams(vmem_limit_bytes=size * 1024 * 1024)


def whole_spec(array):
    rank = len(array.shape)
    return pl.BlockSpec(array.shape, lambda *_: (0,) * rank)


def window_spec(array):
    rank = len(array.shape)
    return pl.BlockSpec((1,) + array.shape[1:], lambda w, *_: (w,) + (0,) * (rank - 1))


def flip(values, axis=1):
    half = values.shape[axis] // 2
    low = lax.slice_in_dim(values, 0, half, axis=axis)
    high = lax.slice_in_dim(values, half, 2 * half, axis=axis)
    return jnp.concatenate([high, low], axis)


def row_pair(own_ref, got_ref, row, count=1):
    return jnp.concatenate([ref[r : r + 1, :] for ref in (own_ref, got_ref) for r in range(row, row + count)], 1)


def normed(values):
    width = values.shape[1]
    center = jnp.sum(values, 1, keepdims=True) / width
    spread = jnp.sum(values * values, 1, keepdims=True) / width - center * center
    inv = lax.rsqrt(spread + EPSILON)
    return (values - center) * inv, inv


def norm_back(upstream, xhat, inv, gain):
    width = xhat.shape[1]
    scaled = upstream * gain
    total = jnp.sum(scaled, 1, keepdims=True) / width
    along = jnp.sum(scaled * xhat, 1, keepdims=True) / width
    return inv * (scaled - total - xhat * along)


def pack_kernel(gain1, shift1, bqv, bp, gain2, shift2, b2, b1, table, out_ref):
    out_ref[...] = jnp.zeros_like(out_ref)
    heads = table.shape[0]
    for c in range(COARSE):
        size = min(FINE, TABLE - c * FINE)
        out_ref[c * heads : (c + 1) * heads, :size] = table[:, c * FINE : c * FINE + size]
    rows = ((GAIN1, gain1), (SHIFT1, shift1), (BIAS_P, bp), (GAIN2, gain2), (SHIFT2, shift2), (BIAS2, b2))
    for row, ref in rows:
        out_ref[row : row + 1, :] = ref[...].reshape(1, -1)
    out_ref[BIAS_Q : BIAS_Q + 2, :] = bqv[...]
    wide = b1[...].reshape(1, -1)
    for i in range(4):
        out_ref[BIAS1 + i : BIAS1 + i + 1, :] = wide[:, i * 256 : (i + 1) * 256]


def pack(*arrays):
    return pl.pallas_call(
        pack_kernel,
        out_shape=jax.ShapeDtypeStruct((VECTOR_ROWS, FINE), F32),
        cost_estimate=cost(1000, 200000),
        name="pack",
    )(*arrays)


def unpack_kernel(a_ref, b_ref, c_ref, d_ref, gain1, shift1, bqv, bp, table, gain2, shift2, b1, b2):
    a, b, c, d = [ref[...].astype(F32) for ref in (a_ref, b_ref, c_ref, d_ref)]
    total = (a + b) + (c + d)
    heads = table.shape[0]
    for c in range(COARSE):
        size = min(FINE, TABLE - c * FINE)
        table[:, c * FINE : c * FINE + size] = total[c * heads : (c + 1) * heads, :size]
    rows = ((GAIN1, gain1), (SHIFT1, shift1), (BIAS_P, bp), (GAIN2, gain2), (SHIFT2, shift2), (BIAS2, b2))
    for row, ref in rows:
        ref[...] = total[row : row + 1].reshape(-1)
    bqv[...] = total[BIAS_Q : BIAS_Q + 2]
    b1[...] = jnp.concatenate([total[BIAS1 + i : BIAS1 + i + 1] for i in range(4)], 1).reshape(-1)


def unpack(parts, heads):
    vector = jax.ShapeDtypeStruct((FINE,), F32)
    return pl.pallas_call(
        unpack_kernel,
        out_shape=[vector, vector, jax.ShapeDtypeStruct((2, FINE), F32), vector, jax.ShapeDtypeStruct((heads, TABLE), F32), vector, vector, jax.ShapeDtypeStruct((4 * FINE,), F32), vector],
        cost_estimate=cost(1000, 200000),
        name="unpack",
    )(*parts)


def lane_tiles(width):
    return [(t, t * 128, min(128, width - t * 128)) for t in range(-(-width // 128))]


def put_rows(scratch, start, rows):
    for t, begin, size in lane_tiles(rows.shape[1]):
        scratch[t, start : start + rows.shape[0], :size] = rows[:, begin : begin + size]


def strided_rows(scratch, start, count, step, width):
    parts = [scratch[t, pl.ds(start, count, stride=step), :][:, :size] for t, _, size in lane_tiles(width)]
    return jnp.concatenate(parts, 1)


def one_hot(fine_row, width):
    rows = lax.broadcasted_iota(jnp.int32, (FINE, width), 0).astype(jnp.int16)
    return jnp.where(rows == fine_row.astype(jnp.int16), jnp.ones((), BF), jnp.zeros((), BF))


def lookup_kernel(heads, idx_ref, own_ref, got_ref, *rest):
    out_ref, scratch, table = rest[-3:]
    width = idx_ref.shape[1]
    size = COARSE * heads

    @pl.when(pl.program_id(0) == 0)
    def _():
        table[:size, :] = (own_ref[:size, :] * LOG2E).astype(BF)
        table[size:, :] = (got_ref[:size, :] * LOG2E).astype(BF)

    for r in range(ROWS):
        idx = idx_ref[r : r + 1, :]
        hot = one_hot(jnp.bitwise_and(idx, FINE - 1), width)
        level = lax.shift_right_logical(idx, 8)
        picked = dot(table[...], hot, 1, 0)
        for half in range(2):
            acc = jnp.zeros((heads, width), F32)
            for c in range(COARSE):
                at = half * size + c * heads
                acc = jnp.where(level == c, picked[at : at + heads], acc)
            put_rows(scratch, (2 * r + half) * heads, acc)
    for h in range(2 * heads):
        out_ref[h, :, :width] = strided_rows(scratch, h, ROWS, 2 * heads, width).astype(BF)


def lookup(idx, own, got, heads, start, count, filled=()):
    width = idx.shape[1]
    return pl.pallas_call(
        functools.partial(lookup_kernel, heads),
        grid=(count,),
        in_specs=[pl.BlockSpec((ROWS, width), lambda i: (start + i, 0)), whole_spec(own), whole_spec(got)] + [ANY] * len(filled),
        out_specs=pl.BlockSpec((2 * heads, ROWS, LANES), lambda i: (0, start + i, 0)),
        out_shape=jax.ShapeDtypeStruct((2 * heads, HALF_ROWS, LANES), BF),
        input_output_aliases={3: 0} if filled else {},
        scratch_shapes=[pltpu.VMEM((-(-width // 128), 2 * ROWS * heads, 128), F32), pltpu.VMEM((2 * COARSE * heads, FINE), BF)],
        compiler_params=params(),
        cost_estimate=cost(0, 0),
        name="table_lookup",
    )(idx, own, got, *filled)


def fold_rows(heads, idx_ref, pair_m, pair_o, sent_m, sent_o, scratch, total):
    width = idx_ref.shape[1]
    for h in range(heads):
        put_rows(scratch, h * ROWS, pair_m[h, :, :width].astype(F32) + sent_o[h, :, :width].astype(F32))
        put_rows(scratch, (heads + h) * ROWS, pair_o[h, :, :width].astype(F32) + sent_m[h, :, :width].astype(F32))
    part = jnp.zeros(total.shape, F32)
    fine = jnp.bitwise_and(idx_ref[...], FINE - 1).T.astype(jnp.int16)
    cells = lax.broadcasted_iota(jnp.int32, (width, FINE), 1).astype(jnp.int16)
    for r in range(ROWS):
        hot = jnp.where(cells == fine[:, r : r + 1], jnp.ones((), BF), jnp.zeros((), BF))
        level = lax.shift_right_logical(idx_ref[r : r + 1, :], 8)
        grads = strided_rows(scratch, r, 2 * heads, ROWS, width)
        parts = [jnp.where(level == c, grads[half * heads : (half + 1) * heads], 0.0) for half in range(2) for c in range(COARSE)]
        part = part + dot(jnp.concatenate(parts, 0).astype(BF), hot, 1, 0)
    total[...] += part


def fold_start_kernel(heads, core_ref, idx_ref, pair_m, pair_o, sent_m, sent_o, total, scratch):
    step = pl.program_id(0)

    @pl.when(step == 0)
    def _():
        total[...] = jnp.zeros_like(total)

    @pl.when(jnp.logical_or(step > 0, core_ref[0] == 0))
    def _():
        fold_rows(heads, idx_ref, pair_m, pair_o, sent_m, sent_o, scratch, total)


def fold_end_kernel(heads, core_ref, idx_ref, pair_m, pair_o, sent_m, sent_o, init_ref, mid_ref, wide_ref, end_ref, mine_ref, other_ref, scratch, total):
    step = pl.program_id(0)
    size = COARSE * heads

    @pl.when(step == 0)
    def _():
        total[...] = init_ref[...]

    fold_rows(heads, idx_ref, pair_m, pair_o, sent_m, sent_o, scratch, total)

    @pl.when(step == pl.num_programs(0) - 1)
    def _():
        binned = total
        for half, ref in enumerate((mine_ref, other_ref)):
            ref[:size, :] = binned[half * size : (half + 1) * size]
            span = slice(half * 256, (half + 1) * 256)
            rows = ((GAIN1, end_ref, 2), (SHIFT1, end_ref, 3), (BIAS_Q, end_ref, 0), (BIAS_V, end_ref, 1), (BIAS_P, mid_ref, 3), (GAIN2, mid_ref, 1), (SHIFT2, mid_ref, 2), (BIAS2, mid_ref, 0))
            for row, source, at in rows:
                ref[row : row + 1, :] = source[at : at + 1, span]
            for i in range(4):
                at = half * 1024 + i * 256
                ref[BIAS1 + i : BIAS1 + i + 1, :] = wide_ref[:, at : at + 256]
            ref[BIAS1 + 4 :, :] = jnp.zeros((VECTOR_ROWS - BIAS1 - 4, 256), F32)


def fold(core, idx, pairs, heads, start, count, extra=()):
    width = idx.shape[1]
    scratch = [pltpu.VMEM((-(-width // 128), 2 * ROWS * heads, 128), F32)]
    total = jax.ShapeDtypeStruct((2 * COARSE * heads, FINE), F32)
    ends = jax.ShapeDtypeStruct((VECTOR_ROWS, FINE), F32)
    outs = [ends, ends] if extra else [total]
    pair = pl.BlockSpec((heads, ROWS, LANES), lambda i, core: (0, start + i, 0))
    return pl.pallas_call(
        functools.partial(fold_end_kernel if extra else fold_start_kernel, heads),
        grid_spec=pltpu.PrefetchScalarGridSpec(
            num_scalar_prefetch=1,
            grid=(count,),
            in_specs=[pl.BlockSpec((ROWS, width), lambda i, core: (start + i, 0))] + [pair] * 4 + [whole_spec(e) for e in extra],
            out_specs=[whole_spec(o) for o in outs],
            scratch_shapes=scratch + ([pltpu.VMEM(total.shape, F32)] if extra else []),
        ),
        out_shape=outs,
        compiler_params=params(),
        cost_estimate=cost(0, 0),
        name="table_fold",
    )(core, idx, *pairs, *extra)


def mask_pieces():
    pieces = []
    rest = np.float32(-100.0 * LOG2E)
    for _ in range(3):
        piece = np.float32(rest.astype(jnp.bfloat16))
        pieces.append(float(piece))
        rest = np.float32(rest - piece)
    return pieces


def region_rows(label):
    width = label.shape[1]
    rows = lax.broadcasted_iota(jnp.int32, (16, width), 0)
    lanes = lax.broadcasted_iota(jnp.int32, (16, width), 1)
    same = jnp.bitwise_and(rows, 3) == label
    level = lax.shift_right_logical(rows, 2)
    high, mid, low = mask_pieces()
    piece = jnp.where(level == 0, high, jnp.where(level == 1, mid, low))
    queries = jnp.where(rows < 12, jnp.where(same, 1.0, 0.0), jnp.where(rows == 15, 1.0, 0.0))
    past = jnp.where(jnp.logical_and(rows == 15, lanes >= WTOK), -1e30, 0.0)
    keys = jnp.where(rows < 12, jnp.where(same, 0.0, piece), past)
    return queries.astype(BF), keys.astype(BF)


def pick_bias(first, own_ref, got_ref, j):
    skip = 2 * HALF_ROWS - TOKS
    low = lax.select_n(first, got_ref[j, :, :TOKS], own_ref[j, :, :TOKS])
    high = lax.select_n(first, own_ref[j, skip:, :TOKS], got_ref[j, skip:, :TOKS])
    return jnp.concatenate([low, high], 0).astype(F32)


def attend_kernel(core_ref, q_ref, k_ref, v_ref, label_ref, own_ref, got_ref, att_ref, exact_ref, lse_ref):
    first = core_ref[0] == 0
    ones = jnp.ones((16, TOKS), BF)
    windows = range(q_ref.shape[0])
    regions = [region_rows(label_ref[w]) for w in windows]
    for j in range(GROUP):
        part = pl.ds(j * HD, HD)
        bias = pick_bias(first, own_ref, got_ref, j)
        for w in windows:
            query_rows, key_rows = regions[w]
            qa = jnp.concatenate([q_ref[w, part, :], query_rows], 0)
            ka = jnp.concatenate([k_ref[w, part, :], key_rows], 0)
            va = jnp.concatenate([v_ref[w, part, :], ones], 0)
            scores = dot(ka, qa, 0, 0) + bias
            peak = jnp.max(scores, 0, keepdims=True)
            weights = jnp.exp2(scores - peak).astype(BF)
            mixed = dot(va, weights, 1, 0)
            total = mixed[HD : HD + 1]
            out = mixed[:HD] / total
            att_ref[w, part, :] = out.astype(BF)
            exact_ref[w, part, :] = out
            lse_ref[w, 0, j : j + 1, :] = peak + jnp.log2(total)


def attention_specs(wins, heads, skip=0):
    half = heads // (2 * GROUP)
    feat = pl.BlockSpec((wins, GROUP * HD, TOKS), lambda h, core: (0, h + skip, 0))
    label = pl.BlockSpec((wins, 1, TOKS), lambda h, core: (0, 0, 0))
    own = pl.BlockSpec((GROUP, HALF_ROWS, LANES), lambda h, core: (h + skip, 0, 0))
    got = pl.BlockSpec((GROUP, HALF_ROWS, LANES), lambda h, core: ((h + skip + half) % (2 * half), 0, 0))
    stat = pl.BlockSpec((wins, 1, GROUP, TOKS), lambda h, core: (0, h + skip, 0, 0))
    return feat, label, own, got, stat


def attend(core, q, k, v, labels, own, got):
    wins, feats, toks = q.shape
    heads = feats // HD
    feat, label, own_spec, got_spec, stat = attention_specs(wins, heads)
    return pl.pallas_call(
        attend_kernel,
        grid_spec=pltpu.PrefetchScalarGridSpec(
            num_scalar_prefetch=1,
            grid=(heads // GROUP,),
            in_specs=[feat, feat, feat, label, own_spec, got_spec],
            out_specs=[feat, feat, stat],
        ),
        out_shape=[
            jax.ShapeDtypeStruct(q.shape, BF),
            jax.ShapeDtypeStruct(q.shape, F32),
            jax.ShapeDtypeStruct((wins, heads // GROUP, GROUP, toks), F32),
        ],
        compiler_params=params(),
        cost_estimate=cost(0, 0),
        name="attend",
    )(core, q, k, v, labels, own, got)


def split3(row):
    hi = row.astype(BF)
    rest = row - hi.astype(F32)
    mid = rest.astype(BF)
    return hi.astype(F32), mid.astype(F32), rest - mid.astype(F32)


def rows16(parts, width):
    rows = lax.broadcasted_iota(jnp.int32, (16, width), 0)
    out = jnp.zeros((16, width), F32)
    for i, part in enumerate(parts):
        out = jnp.where(rows == i, part, out)
    return out.astype(BF)


def attend_back_kernel(scale, core_ref, q_ref, k_ref, v_ref, label_ref, own_ref, got_ref, exact_ref, lse_ref, g_ref, dq_ref, dk_ref, dv_ref, pair_ref, sent_ref, sums):
    core = core_ref[0]
    first = core == 0
    step = TOKS - HALF_ROWS
    mine, other = pl.multiple_of(core * step, 8), pl.multiple_of((1 - core) * step, 8)
    minus = rows16([-1.0, -1.0, -1.0], TOKS)
    windows = range(q_ref.shape[0])
    regions = [region_rows(label_ref[w]) for w in windows]
    for j in range(GROUP):
        part = pl.ds(j * HD, HD)
        bias = pick_bias(first, own_ref, got_ref, j)
        total = None
        for w in windows:
            query_rows, key_rows = regions[w]
            q = q_ref[w, part, :]
            k = k_ref[w, part, :]
            g = g_ref[w, part, :]
            qa = jnp.concatenate([q, query_rows, rows16(split3(lse_ref[w, 0, j : j + 1, :]), TOKS)], 0)
            ka = jnp.concatenate([k, key_rows, minus], 0)
            va = jnp.concatenate([v_ref[w, part, :], minus], 0)
            along = jnp.sum(g.astype(F32) * exact_ref[w, part, :], 0, keepdims=True)
            ga = jnp.concatenate([g, rows16(split3(along), TOKS)], 0)
            probs = jnp.exp2(dot(ka, qa, 0, 0) + bias)
            wide = probs * dot(va, ga, 0, 0)
            grads = wide.astype(BF)
            low = probs.astype(BF)
            dv_ref[w, part, :] = dot(g, low, 1, 1).astype(BF)
            dk_ref[w, part, :] = (dot(q, grads, 1, 1) * (1.0 / LOG2E)).astype(BF)
            dq_ref[w, part, :] = (dot(k, grads, 1, 0) * scale).astype(BF)
            total = wide if total is None else total + wide
        sums[...] = total
        pair_ref[j, :, :TOKS] = sums[pl.ds(mine, HALF_ROWS), :].astype(BF)
        sent_ref[j, :, :TOKS] = sums[pl.ds(other, HALF_ROWS), :].astype(BF)


def attend_back(core, q, k, v, labels, own, got, exact, lse, g, scale, side):
    wins, feats, toks = q.shape
    heads = feats // HD
    blocks = heads // (2 * GROUP)
    feat, label, own_spec, got_spec, stat = attention_specs(wins, heads, side * blocks)
    out = pl.BlockSpec((wins, GROUP * HD, toks), lambda h, core: (0, h, 0))
    pair = pl.BlockSpec((GROUP, HALF_ROWS, LANES), lambda h, core: (h, 0, 0))
    return pl.pallas_call(
        functools.partial(attend_back_kernel, scale),
        grid_spec=pltpu.PrefetchScalarGridSpec(
            num_scalar_prefetch=1,
            grid=(blocks,),
            in_specs=[feat, feat, feat, label, own_spec, got_spec, feat, stat, feat],
            out_specs=[out, out, out, pair, pair],
            scratch_shapes=[pltpu.VMEM((toks, toks), F32)],
        ),
        out_shape=[jax.ShapeDtypeStruct((wins, feats // 2, toks), BF)] * 3 + [jax.ShapeDtypeStruct((heads // 2, HALF_ROWS, LANES), BF)] * 2,
        compiler_params=params(),
        cost_estimate=cost(0, 0),
        name="attend_back",
    )(core, q, k, v, labels, own, got, exact, lse, g)


def front_kernel(scale, xm_ref, xo_ref, own_ref, got_ref, wm_ref, wo_ref, *rest):
    q_ref, k_ref, v_ref, first_ref = rest[-4:]
    x = jnp.concatenate([xm_ref[0], xo_ref[0]], 1).astype(F32)
    xhat, _ = normed(x)
    first = (xhat * row_pair(own_ref, got_ref, GAIN1) + row_pair(own_ref, got_ref, SHIFT1)).astype(BF)
    first_ref[0] = first.T
    for t, (w_ref, vec_ref) in enumerate(((wm_ref, own_ref), (wo_ref, got_ref))):
        cols = w_ref.shape[1] // 3
        rows = pl.ds(t * cols, cols)
        made = dot(first if t == 0 else flip(first), w_ref[...], 1, 0)
        q = (made[:, :cols] + vec_ref[BIAS_Q : BIAS_Q + 1, :]) * scale
        v = made[:, 2 * cols :] + vec_ref[BIAS_V : BIAS_V + 1, :]
        q_ref[0, rows, :] = q.astype(BF).T
        k_ref[0, rows, :] = made[:, cols : 2 * cols].astype(BF).T
        v_ref[0, rows, :] = v.astype(BF).T


def front(xm, xo, own, got, wm, wo, scale, deps):
    wins, toks, half = xm.shape
    out = jax.ShapeDtypeStruct((wins, 2 * (wm.shape[1] // 3), toks), BF)
    return pl.pallas_call(
        functools.partial(front_kernel, scale),
        grid=(wins,),
        in_specs=[window_spec(xm), window_spec(xo), whole_spec(own), whole_spec(got), whole_spec(wm), whole_spec(wo)] + [ANY] * len(deps),
        out_specs=[window_spec(out)] * 4,
        out_shape=[out] * 4,
        compiler_params=params(),
        cost_estimate=cost(8 * wins * toks * half * wm.shape[1], wins * toks * half * 16 + wm.size * 4),
        name="front",
    )(xm, xo, own, got, wm, wo, *deps)


def middle_kernel(xm_ref, xo_ref, att_ref, own_ref, got_ref, wm_ref, wo_ref, *rest):
    mid_ref, second_ref, act_ref, slope_ref = rest[-4:]
    half = xm_ref.shape[2]
    wide = wm_ref.shape[1] - half
    restored = att_ref[0].T
    branch = dot(restored[:, :half], wm_ref[:, :half], 1, 1) + flip(dot(restored[:, half:], wo_ref[:, :half], 1, 1))
    x = jnp.concatenate([xm_ref[0], xo_ref[0]], 1).astype(F32)
    middle = x + (branch + row_pair(own_ref, got_ref, BIAS_P))
    mid_ref[0] = middle
    xhat, _ = normed(middle)
    second = (xhat * row_pair(own_ref, got_ref, GAIN2) + row_pair(own_ref, got_ref, SHIFT2)).astype(BF)
    second_ref[0] = second
    turned = flip(second)
    for t, (w_ref, vec_ref) in enumerate(((wm_ref, own_ref), (wo_ref, got_ref))):
        for s in range(0, wide, 256):
            at = t * wide + s
            bias = vec_ref[BIAS1 + s // 256 : BIAS1 + s // 256 + 1, :]
            hidden = dot(second if t == 0 else turned, w_ref[:, half + s : half + s + 256], 1, 0) + bias
            phi = 0.5 + 0.5 * lax.erf(hidden * (0.5**0.5))
            bell = jnp.exp2(hidden * hidden * (-0.5 * LOG2E)) * (1.0 / (2.0 * np.pi) ** 0.5)
            act_ref[0, :, at : at + 256] = (hidden * phi).astype(BF)
            slope_ref[0, :, at : at + 256] = (phi + hidden * bell).astype(BF)


def middle_forward(xm, xo, att, own, got, wm, wo, deps):
    wins, toks, half = xm.shape
    width = 2 * half
    hidden = 2 * (wm.shape[1] - half)
    wide = jax.ShapeDtypeStruct((wins, toks, hidden), BF)
    outs = [jax.ShapeDtypeStruct((wins, toks, width), F32), jax.ShapeDtypeStruct((wins, toks, width), BF), wide, wide]
    fixed = (own, got, wm, wo)
    return pl.pallas_call(
        middle_kernel,
        grid=(wins,),
        in_specs=[window_spec(xm), window_spec(xo), window_spec(att)] + [whole_spec(a) for a in fixed] + [ANY] * len(deps),
        out_specs=[window_spec(o) for o in outs],
        out_shape=outs,
        compiler_params=params(28),
        cost_estimate=cost(8 * wins * toks * width * wm.shape[1], wins * toks * (width * 10 + hidden * 4) + wm.size * 4, wins * toks * hidden),
        name="middle_forward",
    )(xm, xo, att, *fixed, *deps)


def put_pieces(out, nearm_ref, nearo_ref, farm_ref, faro_ref):
    half = out.shape[1] // 2
    for ref, rows, cols in ((nearm_ref, 0, 0), (nearo_ref, 0, half), (farm_ref, TOKS - SENT_OUT, 0), (faro_ref, TOKS - SENT_OUT, half)):
        ref[0] = out[rows : rows + SENT_OUT, cols : cols + half]


def middle_back_kernel(cm_ref, co_ref, mid_ref, second_ref, act_ref, slope_ref, att_ref, own_ref, got_ref, wm_ref, wo_ref, fm_ref, fo_ref, *rest):
    nearm_ref, nearo_ref, farm_ref, faro_ref, gm_ref, gr_ref, onem_ref, oneo_ref, twom_ref, twoo_ref, small_ref, wide_ref, accm, acco = rest[-14:]
    win = pl.program_id(0)
    half = cm_ref.shape[2]
    wide = fm_ref.shape[1]

    @pl.when(win == 0)
    def _():
        accm[...] = jnp.zeros_like(accm)
        acco[...] = jnp.zeros_like(acco)
        small_ref[...] = jnp.zeros_like(small_ref)
        wide_ref[...] = jnp.zeros_like(wide_ref)

    cot = jnp.concatenate([cm_ref[0], co_ref[0]], 1)
    cot_turned = flip(cot)
    cot_t = cot.T
    second_t = second_ref[0].T
    sides = (
        (wm_ref, fm_ref, accm, cot, cot_t, second_t),
        (wo_ref, fo_ref, acco, cot_turned, flip(cot_t, 0), flip(second_t, 0)),
    )
    made, pulled = [], []
    for t, (w_ref, f_ref, acc, c, c_t, s_t) in enumerate(sides):
        forward = jnp.zeros(cot.shape, F32)
        grad_second = jnp.zeros(cot.shape, F32)
        for s in range(0, wide, 512):
            span = slice(t * wide + s, t * wide + s + 512)
            fc2 = f_ref[:, s : s + 512]
            active = act_ref[0, :, span]
            forward = forward + dot(active, fc2, 1, 1)
            grad = (dot(c, fc2, 1, 0) * slope_ref[0, :, span].astype(F32)).astype(BF)
            wide_ref[:, span] += jnp.sum(grad.astype(F32), 0, keepdims=True)
            acc[:, half + wide + s : half + wide + s + 512] += dot(c_t, active, 1, 0)
            acc[:, half + s : half + s + 512] += dot(s_t, grad, 1, 0)
            grad_second = grad_second + dot(grad, w_ref[:, half + s : half + s + 512], 1, 1)
        made.append(forward)
        pulled.append(grad_second)
    out = mid_ref[0] + (made[0] + flip(made[1]) + row_pair(own_ref, got_ref, BIAS2))
    put_pieces(out.astype(BF), nearm_ref, nearo_ref, farm_ref, faro_ref)
    grad_second = pulled[0] + flip(pulled[1])
    upstream = cot.astype(F32)
    xhat, inv = normed(mid_ref[0])
    grad_mid = upstream + norm_back(grad_second, xhat, inv, row_pair(own_ref, got_ref, GAIN2))
    gm_ref[0] = grad_mid
    branch = grad_mid.astype(BF)
    branch_t = branch.T
    gr_ref[0, :half, :] = dot(branch, wm_ref[:, :half], 1, 0).astype(BF).T
    gr_ref[0, half:, :] = dot(flip(branch), wo_ref[:, :half], 1, 0).astype(BF).T
    accm[:, :half] += dot(branch_t, att_ref[0, :half, :], 1, 1)
    acco[:, :half] += dot(flip(branch_t, 0), att_ref[0, half:, :], 1, 1)
    small_ref[0:1, :] += jnp.sum(upstream, 0, keepdims=True)
    small_ref[1:2, :] += jnp.sum(grad_second * xhat, 0, keepdims=True)
    small_ref[2:3, :] += jnp.sum(grad_second, 0, keepdims=True)
    small_ref[3:4, :] += jnp.sum(branch.astype(F32), 0, keepdims=True)

    @pl.when(win == pl.num_programs(0) - 1)
    def _():
        for acc, one_ref, two_ref in ((accm, onem_ref, twom_ref), (acco, oneo_ref, twoo_ref)):
            one_ref[...] = acc[:, half : half + wide].astype(BF)
            two_ref[:, :half] = acc[:, :half].astype(BF)
            two_ref[:, half:] = acc[:, half + wide :].astype(BF)


def middle_back(cm, co, mid, second, act, slope, att, own, got, wm, wo, fm, fo, deps):
    wins, toks, half = cm.shape
    width = 2 * half
    hidden = act.shape[2]
    windows = (cm, co, mid, second, act, slope, att)
    fixed = (own, got, wm, wo, fm, fo)
    plain = jax.ShapeDtypeStruct((wins, SENT_OUT, half), BF)
    outs = [plain, plain, plain, plain, jax.ShapeDtypeStruct(mid.shape, F32), jax.ShapeDtypeStruct(att.shape, BF)]
    grads = jax.ShapeDtypeStruct((width, wm.shape[1] + fm.shape[1]), BF)
    one = jax.ShapeDtypeStruct((width, wm.shape[1] - half), BF)
    two = jax.ShapeDtypeStruct((width, half + fm.shape[1]), BF)
    sums = [one, one, two, two, jax.ShapeDtypeStruct((4, width), F32), jax.ShapeDtypeStruct((1, hidden), F32)]
    return pl.pallas_call(
        middle_back_kernel,
        grid=(wins,),
        in_specs=[window_spec(a) for a in windows] + [whole_spec(a) for a in fixed] + [ANY] * len(deps),
        out_specs=[window_spec(o) for o in outs] + [whole_spec(o) for o in sums],
        out_shape=[pltpu.HBM(o.shape, o.dtype) for o in outs + sums],
        scratch_shapes=[pltpu.VMEM(grads.shape, F32), pltpu.VMEM(grads.shape, F32)],
        compiler_params=params(28),
        cost_estimate=cost(12 * wins * toks * width * (width + 2 * hidden), wins * toks * (width * 16 + hidden * 4) + fm.size * 12),
        name="middle_back",
    )(*windows, *fixed, *deps)


def side_kernel(first_ref, dq_ref, dk_ref, dv_ref, do_ref):
    for c, ref in enumerate((dq_ref, dk_ref, dv_ref)):
        cols = ref.shape[1]
        part = sum(dot(flip(first_ref[w], 0), ref[w], 1, 1) for w in range(first_ref.shape[0]))
        do_ref[:, c * cols : (c + 1) * cols] = part.astype(BF)


def side_grads(first, grads):
    wins, width, toks = first.shape
    return pl.pallas_call(
        side_kernel,
        out_shape=jax.ShapeDtypeStruct((width, 3 * grads[0].shape[1]), BF),
        compiler_params=params(),
        cost_estimate=cost(0, 0),
        name="side_grads",
    )(first, *grads)


def back_kernel(xm_ref, xo_ref, first_ref, qm_ref, km_ref, vm_ref, qo_ref, ko_ref, vo_ref, gm_ref, own_ref, got_ref, wm_ref, wo_ref, side_ref, nearm_ref, nearo_ref, farm_ref, faro_ref, dm_ref, small_ref, acc):
    win = pl.program_id(0)

    @pl.when(win == 0)
    def _():
        acc[...] = side_ref[...].astype(F32)
        small_ref[...] = jnp.zeros_like(small_ref)

    xhat, inv = normed(jnp.concatenate([xm_ref[0], xo_ref[0]], 1).astype(F32))
    half = xm_ref.shape[2]
    mine = jnp.concatenate([qm_ref[0], km_ref[0], vm_ref[0]], 0)
    other = jnp.concatenate([qo_ref[0], ko_ref[0], vo_ref[0]], 0)
    acc[...] += dot(first_ref[0], mine, 1, 1)
    grad_first = dot(mine, wm_ref[...], 0, 1) + flip(dot(other, wo_ref[...], 0, 1))
    grad_first = grad_first.astype(BF).astype(F32)
    grad_x = gm_ref[0] + norm_back(grad_first, xhat, inv, row_pair(own_ref, got_ref, GAIN1))
    put_pieces(grad_x.astype(BF), nearm_ref, nearo_ref, farm_ref, faro_ref)
    ones = jnp.ones((8, mine.shape[1]), BF)
    for t, side in enumerate((mine, other)):
        sums = dot(ones, side, 1, 1)[0:1]
        span = slice(t * half, (t + 1) * half)
        small_ref[0:1, span] += sums[:, :half]
        small_ref[1:2, span] += sums[:, 2 * half :]
    small_ref[2:3, :] += jnp.sum(grad_first * xhat, 0, keepdims=True)
    small_ref[3:4, :] += jnp.sum(grad_first, 0, keepdims=True)

    @pl.when(win == pl.num_programs(0) - 1)
    def _():
        dm_ref[...] = acc[...].astype(BF)


def back(xm, xo, first, mine, other, gm, own, got, wm, wo, side):
    wins, toks, half = xm.shape
    windows = (xm, xo, first) + mine + other + (gm,)
    fixed = (own, got, wm, wo, side)
    plain = jax.ShapeDtypeStruct((wins, SENT_OUT, half), BF)
    grads = jax.ShapeDtypeStruct(wm.shape, BF)
    small = jax.ShapeDtypeStruct((4, 2 * half), F32)
    return pl.pallas_call(
        back_kernel,
        grid=(wins,),
        in_specs=[window_spec(a) for a in windows] + [whole_spec(a) for a in fixed],
        out_specs=[window_spec(plain)] * 4 + [whole_spec(grads), whole_spec(small)],
        out_shape=[pltpu.HBM(o.shape, o.dtype) for o in (plain, plain, plain, plain, grads, small)],
        scratch_shapes=[pltpu.VMEM(wm.shape, F32)],
        compiler_params=params(),
        cost_estimate=cost(0, 0),
        name="back",
    )(*windows, *fixed)


def one_hot_rows(picks, size):
    cells = lax.broadcasted_iota(jnp.int32, (picks.shape[0], size), 1)
    return jnp.where(cells == picks, 1.0, 0.0).astype(BF)


def select_in_kernel(core_ref, picks_ref, near_ref, far_ref, mine_ref, other_ref):
    skip = WTOK - SENT_IN
    near = jnp.concatenate([near_ref[w, skip:, :] for w in range(4)], 0)
    low = dot(one_hot_rows(picks_ref[0, : 4 * SENT_IN, :], near.shape[0]), near, 1, 0)
    high = dot(one_hot_rows(picks_ref[0, 4 * SENT_IN :, :], far_ref.shape[0]), far_ref[...], 1, 0)
    rows = lax.broadcasted_iota(jnp.int32, (SENT_IN - skip, 1), 0) + skip
    for w in range(4):
        first, last = low[w * SENT_IN : (w + 1) * SENT_IN], high[w * SENT_OUT : (w + 1) * SENT_OUT]
        over = jnp.where(rows < HELD, first[skip:], last[: SENT_IN - skip])
        whole = jnp.concatenate([first[:skip], over, last[SENT_IN - skip :]], 0).astype(BF)
        (mine_ref if w < 2 else other_ref)[w % 2] = whole


def core_block(picks):
    return pl.BlockSpec((1,) + picks.shape[1:], lambda i, core: (core[0], 0, 0))


def select_in(core, picks, near, far):
    out = jax.ShapeDtypeStruct((2, TOKS, near.shape[2]), BF)
    return pl.pallas_call(
        select_in_kernel,
        grid_spec=pltpu.PrefetchScalarGridSpec(
            num_scalar_prefetch=1,
            grid=(1,),
            in_specs=[core_block(picks), whole_spec(near), whole_spec(far)],
            out_specs=[whole_spec(out)] * 2,
        ),
        out_shape=[out, out],
        compiler_params=params(28),
        cost_estimate=cost(0, 0),
        name="select_in",
    )(core, picks, near, far)


def select_out_kernel(core_ref, picks_ref, kept_ref, beside_ref, across_ref, corner_ref, out_ref):
    skip = WTOK - SENT_IN
    near = jnp.concatenate([kept_ref[...], beside_ref[...]], 0)
    far = jnp.concatenate([across_ref[...], corner_ref[...]], 0)
    low = dot(one_hot_rows(picks_ref[0, : 4 * SENT_IN, :], far.shape[0]), far, 1, 0)
    high = dot(one_hot_rows(picks_ref[0, 4 * SENT_IN :, :], near.shape[0]), near, 1, 0)
    rows = lax.broadcasted_iota(jnp.int32, (SENT_IN - skip, 1), 0) + skip
    for w in range(4):
        first, last = [part[w * SENT_IN : (w + 1) * SENT_IN] for part in (low, high)]
        out_ref[w, :skip, :] = first[:skip]
        out_ref[w, skip:SENT_IN, :] = jnp.where(rows < HELD, first[skip:], last[: SENT_IN - skip])
        out_ref[w, SENT_IN:, :] = last[SENT_IN - skip :]


def select_out(core, picks, arrays):
    out = jax.ShapeDtypeStruct((4, WTOK, arrays[0].shape[1]), F32)
    return pl.pallas_call(
        select_out_kernel,
        grid_spec=pltpu.PrefetchScalarGridSpec(
            num_scalar_prefetch=1,
            grid=(1,),
            in_specs=[core_block(picks)] + [whole_spec(a) for a in arrays],
            out_specs=whole_spec(out),
        ),
        out_shape=out,
        compiler_params=params(28),
        cost_estimate=cost(0, 0),
        name="select_out",
    )(core, picks, *arrays)


def bits_of(axis):
    return lax.axis_size(axis).bit_length() - 1


def bit_on(axis, bit):
    return lax.shift_right_logical(lax.axis_index(axis), bit) % 2


def swap(value, axis, bit=0):
    pairs = [(source, source ^ (1 << bit)) for source in range(lax.axis_size(axis))]
    return lax.ppermute(value, axis, pairs)


def bit_order():
    count = bits_of("shard")
    return list(range(1, count)) + [0]


def row_place(bit):
    place = bit_on("shard", bit)
    if bit == bits_of("shard") - 1:
        place = jnp.bitwise_xor(place, lax.axis_index("tensor"))
    return place


def ordered(on, mine, other, axis):
    return jnp.concatenate((jnp.where(on, other, mine), jnp.where(on, mine, other)), axis)


def after(value, *deps):
    return lax.optimization_barrier((value,) + deps)[0]


def gather_start(part):
    rows, cols = part.shape
    return part.reshape((1,) * bits_of("shard") + (rows, cols))


def joint(values, deps):
    return lax.optimization_barrier(tuple(values) + tuple(deps))[: len(values)]


def gather_join(held, bit, got):
    return ordered(row_place(bit) == 1, held, got, bits_of("shard") - 1 - bit)


def gather_send(held, bits):
    for bit in bits[:-1]:
        held = gather_join(held, bit, swap(held, "shard", bit))
    return held, swap(held, "shard", bits[-1])


def choose(array, index, axis):
    return lax.dynamic_slice_in_dim(array, index, 1, axis)


def add_rounded(a, b):
    return (a.astype(F32) + b.astype(F32)).astype(BF)


def split_rows(part):
    count = bits_of("shard")
    return part.reshape((2,) * count + (part.shape[0] >> count, part.shape[1]))


def scatter_add(held, bit, got):
    axis = bits_of("shard") - 1 - bit
    return add_rounded(choose(held, row_place(bit), axis), got)


def scatter_send(held, bits):
    for bit in bits[:-1]:
        held = scatter_add(held, bit, scatter_send(held, (bit,))[1])
    axis = bits_of("shard") - 1 - bits[-1]
    return held, swap(choose(held, 1 - row_place(bits[-1]), axis), "shard", bits[-1])


def ctx_half(held, own):
    axis = held.ndim - 2
    half = held.shape[axis] // 2
    return lax.dynamic_slice_in_dim(held, own * half, half, axis)


def ctx_split_send(held):
    return swap(ctx_half(held, 1 - bit_on("ctx", 0)), "ctx")


def ctx_split_add(held, got):
    return add_rounded(ctx_half(held, bit_on("ctx", 0)), got)


def flat(held):
    return held.reshape(held.shape[-2:])


def ctx_send(held):
    held = flat(held)
    for bit in range(bits_of("ctx") - 1):
        held = add_rounded(held, swap(held, "ctx", bit))
    return held, swap(held, "ctx", bits_of("ctx") - 1)


def ctx_add(held, got):
    return held.astype(F32) + got.astype(F32)


def joint_swap(value, mask):
    size = lax.axis_size("shard") * lax.axis_size("ctx")
    return lax.ppermute(value, ("shard", "ctx"), [(i, i ^ mask) for i in range(size)])


def joint_parts(value, bits):
    value = value.astype(BF)
    low = 1 << bits[0]
    if len(bits) == 1:
        return [value, joint_swap(value, low), jnp.zeros_like(value), jnp.zeros_like(value)]
    high = 1 << bits[1]
    return [value, joint_swap(value, low), joint_swap(value, high), joint_swap(value, low | high)]


def add_parts(parts):
    a, b, c, d = [part.astype(F32) for part in parts]
    return (a + b) + (c + d)


def joint_groups():
    bits = list(range(bits_of("shard") + bits_of("ctx")))
    return [bits[i : i + 2] for i in range(0, len(bits), 2)]


def roll_axis(shaped, axis_pos, levels, backward):
    token_axis = 4 + axis_pos
    length = shaped.shape[token_axis]
    border = length - length // 2 if backward else length // 2
    before = lax.slice_in_dim(shaped, 0, border, axis=token_axis)
    after = lax.slice_in_dim(shaped, border, length, axis=token_axis)
    moving = after if backward else before
    if axis_pos < levels:
        moving = swap(moving, "ctx", levels - 1 - axis_pos)
    else:
        moving = jnp.roll(moving, 1 if backward else -1, axis=1 + axis_pos)
    return jnp.concatenate((moving, before) if backward else (after, moving), axis=token_axis)


def window_roll(windows, clips, counts, backward):
    shaped = windows.reshape((clips,) + counts + (WT, WH, WW, windows.shape[-1]))
    for axis_pos in range(3):
        shaped = roll_axis(shaped, axis_pos, bits_of("ctx"), backward)
    return shaped.reshape(windows.shape)


def frame_sources():
    source = np.zeros((4, HELD), np.int64)
    for h in range(2 * WH):
        for w in range(2 * WW):
            here = (h // WH) * 2 + w // WW
            there_h, there_w = (h + WH // 2) % (2 * WH), (w + WW // 2) % (2 * WW)
            there = (there_h // WH) * 2 + there_w // WW
            for a in range(WT // 2):
                row = (a * WH + h % WH) * WW + w % WW
                source[here, row] = there * HELD + (a * WH + there_h % WH) * WW + there_w % WW
    return source


def picks_in():
    source = frame_sources()
    there, row = source // HELD, source % HELD
    picks = np.full((4, TOKS), -1)
    picks[:, :HELD] = there * SENT_IN + row + SENT_IN - HELD
    picks[:, HELD:WTOK] = there * SENT_IN + row
    both = []
    for rows in (picks, np.concatenate((picks[2:], picks[:2]))):
        both.append(np.concatenate((rows[:, :SENT_IN].reshape(-1, 1), rows[:, WTOK - SENT_IN :].reshape(-1, 1))))
    return jnp.asarray(np.stack(both), jnp.int32)


def picks_out():
    place = np.argsort(frame_sources().reshape(-1)).reshape(4, HELD)
    there, row = place // HELD, place % HELD
    both = []
    for core in range(2):
        block = ((there // 2 + core) % 2) * 2 * SENT_OUT + (there % 2) * SENT_OUT
        picks = np.zeros((4, WTOK), np.int64)
        picks[:, HELD:] = block + row
        picks[:, :HELD] = block + row + HELD - (TOKS - SENT_OUT)
        both.append(np.concatenate((picks[:, :SENT_IN].reshape(-1, 1), picks[:, WTOK - SENT_IN :].reshape(-1, 1))))
    return jnp.asarray(np.stack(both), jnp.int32)


def plain_ring(clips):
    return bits_of("ctx") == 1 and clips == 1


def shift_start(windows, clips):
    if plain_ring(clips):
        return swap(windows[:, :SENT_IN].reshape(-1, windows.shape[-1]), "ctx")
    return windows[:1, :8]


def shift_in(windows, got, clips, counts, core_row):
    half = windows.shape[0] // 2
    if plain_ring(clips):
        mine, other = select_in(core_row, picks_in(), windows, got)
        return mine, swap(other, "tensor")
    moved = jnp.pad(window_roll(windows, clips, counts, False), ((0, 0), (0, TOKS - WTOK), (0, 0)))
    core = lax.axis_index("tensor")
    mine = lax.dynamic_slice_in_dim(moved, core * half, half, 0)
    return mine, swap(lax.dynamic_slice_in_dim(moved, (1 - core) * half, half, 0), "tensor")


def leave_start(pieces, clips):
    nearm, nearo, farm, faro = pieces
    width = nearm.shape[-1]
    if not plain_ring(clips):
        cut = TOKS - SENT_OUT
        mine, other = [jnp.concatenate((near[:, :cut], far), 1) for near, far in ((nearm, farm), (nearo, faro))]
        return mine, swap(other, "tensor")
    nearm, nearo, farm, faro = [piece.reshape(-1, width) for piece in pieces]
    corner = lax.ppermute(faro, ("ctx", "tensor"), [(i, i ^ 3) for i in range(4)])
    return nearm, swap(nearo, "tensor"), swap(farm, "ctx"), corner


def leave_end(parts, clips, counts, core_row, *deps):
    parts = (after(parts[0], *deps),) + tuple(parts[1:])
    if plain_ring(clips):
        return select_out(core_row, picks_out(), parts)
    windows = ordered(lax.axis_index("tensor") == 1, parts[0], parts[1], 0)
    return window_roll(windows[:, :WTOK], clips, counts, True).astype(F32)


def on_device(
    clip_input,
    cotangent,
    gain_one,
    shift_one,
    w_qkv,
    b_qv,
    w_proj,
    b_proj,
    bias_table,
    gain_two,
    shift_two,
    w_fc1,
    b_fc1,
    w_fc2,
    b_fc2,
    rel_index,
    regions,
):
    clips, window_count, tokens, half_width = clip_input.shape
    heads = bias_table.shape[0]
    levels = bits_of("ctx")
    counts = tuple(1 if axis_pos < levels else 2 for axis_pos in range(3))
    core = lax.axis_index("tensor")
    core_row = core.astype(jnp.int32).reshape(1)
    total_windows = clips * window_count
    held_windows = total_windows // 2
    scale = HD ** (-0.5)
    hidden = w_fc1.shape[1]

    own = pack(gain_one, shift_one, b_qv, b_proj, gain_two, shift_two, b_fc2, b_fc1, bias_table)
    got = swap(own, "tensor")
    qkv = gather_start(w_qkv.transpose(1, 0, 2).reshape(w_qkv.shape[1], -1))
    early = gather_start(jnp.concatenate((w_proj.T, w_fc1), 1))
    late = gather_start(w_fc2.T)
    index = jnp.pad(rel_index.T, ((0, TOKS - tokens), (0, TOKS - tokens)))
    index = lax.dynamic_slice_in_dim(index, core * (TOKS - HALF_ROWS), HALF_ROWS, 0)
    block = HALF_ROWS // ROWS
    cut = block // 2
    early_blocks = 5
    labels = jnp.tile(regions, (clips, 1))
    labels = lax.dynamic_slice_in_dim(labels, core * held_windows, held_windows, 0)
    labels = jnp.pad(labels, ((0, 0), (0, TOKS - tokens)))[:, None, :]

    order = bit_order()
    first, middle, last = order[0], order[1:-1], order[-1]
    clip_rows = clip_input.reshape(total_windows, tokens, half_width)
    cot_rows = cotangent.reshape(total_windows, tokens, half_width)

    clip_got = shift_start(clip_rows, clips)
    qkv = gather_join(qkv, first, swap(qkv, "shard", first))
    qkv, qkv_got = gather_send(qkv, middle)
    early, late = joint((early, late), (qkv,))
    early_got, late_got = [swap(held, "shard", first) for held in (early, late)]
    part_own = lookup(after(index, qkv), own, got, heads, 0, early_blocks)
    qkv_got, clip_got, early_got, late_got, part_own = joint((qkv_got, clip_got, early_got, late_got, part_own), ())
    qkv = gather_join(qkv, middle[-1], qkv_got)
    early, late = gather_join(early, first, early_got), gather_join(late, first, late_got)
    early, early_got = gather_send(early, middle)
    qkv_got = swap(qkv, "shard", last)
    bias_own = lookup(index, own, got, heads, early_blocks, block - early_blocks, (part_own,))
    xm, xo = shift_in(clip_rows, after(clip_got, bias_own), clips, counts, core_row)
    early_got, qkv_got, xm = joint((early_got, qkv_got, xm), ())
    early = gather_join(early, middle[-1], early_got)
    qkv = gather_join(qkv, last, qkv_got)
    bias_got = swap(after(bias_own, qkv), "tensor")
    qkv = qkv.reshape(-1, qkv.shape[-1])
    qkv_other = swap(qkv, "tensor")
    early_got = swap(early, "shard", last)
    late, late_got = gather_send(after(late, early), middle)
    cot_got = shift_start(after(cot_rows, early), clips)
    queries, keys, values, first_t = front(after(xm, early), xo, own, got, qkv, qkv_other, scale * LOG2E, ())
    att, exact, lse = attend(core_row, queries, keys, values, labels, bias_own, bias_got)
    early_got, late_got, cot_got, att = joint((early_got, late_got, cot_got, att), ())
    early = gather_join(early, last, early_got)
    early = early.reshape(-1, early.shape[-1])
    early_other = swap(early, "tensor")
    late = gather_join(late, middle[-1], late_got)
    late_got = swap(late, "shard", last)
    mid, second, act, slope = middle_forward(xm, xo, att, own, got, early, early_other, ())
    cm, co = shift_in(after(cot_rows, act), cot_got, clips, counts, core_row)
    late = gather_join(late, last, after(late_got, cm))
    late = late.reshape(-1, late.shape[-1])
    late_other = swap(late, "tensor")
    *block_pieces, grad_mid, grad_att, one_mine, one_other, two_mine, two_other, small_mid, small_wide = middle_back(cm, co, mid, second, act, slope, att, own, got, early, early_other, late, late_other, ())

    order = order[::-1]
    twice = bits_of("ctx") == 1
    args = (core_row, queries, keys, values, labels, bias_own, bias_got, exact, lse)
    block_parts = leave_start(block_pieces, clips)
    one_got, two_got = swap(one_other, "tensor"), swap(two_other, "tensor")
    qo, ko, vo, pair_o, sent_o = attend_back(*args, grad_att, scale, 1)
    one_got, two_got, qo = joint((one_got, two_got, qo), ())
    one, two = split_rows(add_rounded(one_mine, one_got)), split_rows(add_rounded(two_mine, two_got))
    one_got = scatter_send(one, order[:1])[1]
    two_got = ctx_split_send(two) if twice else scatter_send(two, order[:1])[1]
    side = side_grads(first_t, (qo, ko, vo))
    side_got, sent_o = swap(side, "tensor"), swap(sent_o, "tensor")
    qm, km, vm, pair_m, sent_m = attend_back(*args, after(grad_att, side), scale, 0)
    one_got, two_got, side, sent_o, qm, *moved = joint((one_got, two_got, side_got, sent_o, qm) + tuple(block_parts[1:]), ())
    block_parts = (block_parts[0],) + tuple(moved)
    one = scatter_add(one, order[0], one_got)
    two = ctx_split_add(two, two_got) if twice else scatter_add(two, order[0], two_got)
    one_got = scatter_send(one, order[1:2])[1]
    two_bits = order if twice else order[1:]
    two_got = scatter_send(two, two_bits[:1])[1]
    sent_m = swap(sent_m, "tensor")
    *grad_pieces, qkv_grads, small_end = back(xm, xo, first_t, (after(qm, one, two), km, vm), (qo, ko, vo), grad_mid, own, got, qkv, qkv_other, side)
    block_out = leave_end(block_parts, clips, counts, core_row, small_end)
    one_got, two_got, sent_m, block_out = joint((one_got, two_got, sent_m, block_out), ())
    one = scatter_add(one, order[1], one_got)
    two = scatter_add(two, two_bits[0], two_got)
    qkv_grads = split_rows(qkv_grads)
    qkv_got = scatter_send(qkv_grads, order[:1])[1]
    grad_parts = leave_start(grad_pieces, clips)
    two_got = scatter_send(two, two_bits[1:2])[1]
    one, one_got = scatter_send(one, order[2:])
    pairs = (pair_m, pair_o, sent_m, sent_o)
    (folded,) = fold(core_row, after(index, one, two), pairs, heads, 0, cut)
    qkv_got, two_got, one_got, folded, *moved = joint((qkv_got, two_got, one_got, folded) + tuple(grad_parts[1:]), ())
    grad_parts = (grad_parts[0],) + tuple(moved)
    qkv_grads = scatter_add(qkv_grads, order[0], qkv_got)
    two = scatter_add(two, two_bits[1], two_got)
    one = scatter_add(one, order[-1], one_got)
    qkv_got = scatter_send(qkv_grads, order[1:2])[1]
    two, two_got = scatter_send(two, two_bits[2:])
    one, one_got = ctx_send(one)
    fold_mine, fold_other = fold(core_row, after(index, one, two, qkv_grads), pairs, heads, cut, block - cut, (folded, small_mid, small_wide, small_end))
    qkv_got, two_got, one_got, fold_mine = joint((qkv_got, two_got, one_got, fold_mine), ())
    small = fold_mine + swap(fold_other, "tensor")
    qkv_grads = scatter_add(qkv_grads, order[1], qkv_got)
    qkv_grads, qkv_got = scatter_send(qkv_grads, order[2:])
    two = scatter_add(two, two_bits[-1], two_got)
    two, two_got = (two, swap(two, "ctx")) if twice else ctx_send(two)
    groups = joint_groups()
    for group in groups[:-2]:
        small = add_parts(joint_parts(small, group))
    parts = joint_parts(small, groups[-2])
    grad_input = leave_end(grad_parts, clips, counts, core_row, small)
    *parts, qkv_got, two_got, grad_input = joint(tuple(parts) + (qkv_got, two_got, grad_input), ())
    parts = joint_parts(add_parts(parts), groups[-1])
    qkv_grads = scatter_add(qkv_grads, order[-1], qkv_got)
    qkv_grads, qkv_got = ctx_send(qkv_grads)
    one = ctx_add(one, one_got)
    two = flat(ordered(bit_on("ctx", 0) == 1, two, two_got, two.ndim - 2)).astype(F32) if twice else ctx_add(two, two_got)
    qkv_grads = ctx_add(qkv_grads, qkv_got)
    d_gain1, d_shift1, d_bqv, d_bp, d_table, d_gain2, d_shift2, d_b1, d_b2 = unpack(parts, heads)
    rows = w_fc1.shape[0]
    return (
        block_out.reshape(clip_input.shape),
        grad_input.reshape(clip_input.shape),
        d_gain1,
        d_shift1,
        qkv_grads.reshape(rows, 3, half_width).transpose(1, 0, 2),
        d_bqv,
        two[:, :half_width].T,
        d_bp,
        d_table,
        d_gain2,
        d_shift2,
        one,
        d_b1,
        two[:, half_width:].T,
        d_b2,
    )


def solution(mesh):
    in_specs = (
        P("shard", "ctx", None, "tensor"),
        P("shard", "ctx", None, "tensor"),
        P("tensor"),
        P("tensor"),
        P(None, "shard", "tensor"),
        P(None, "tensor"),
        P("tensor", "shard"),
        P("tensor"),
        P("tensor", None),
        P("tensor"),
        P("tensor"),
        P("shard", "tensor"),
        P("tensor"),
        P("tensor", "shard"),
        P("tensor"),
        P(),
        P("ctx", None),
    )
    out_specs = (
        P("shard", "ctx", None, "tensor"),
        P("shard", "ctx", None, "tensor"),
        P("tensor"),
        P("tensor"),
        P(None, "shard", "tensor"),
        P(None, "tensor"),
        P("tensor", "shard"),
        P("tensor"),
        P("tensor", None),
        P("tensor"),
        P("tensor"),
        P("shard", "tensor"),
        P("tensor"),
        P("tensor", "shard"),
        P("tensor"),
    )
    return jax.shard_map(
        on_device, mesh=mesh, in_specs=in_specs, out_specs=out_specs, check_vma=False
    )
```

```python
import functools

import jax
import jax.numpy as jnp
import numpy as np
from jax import lax
from jax.experimental import pallas as pl
from jax.experimental.pallas import tpu as pltpu
from jax.sharding import PartitionSpec as P

BF = jnp.bfloat16
F32 = jnp.float32
HD = 32
WT, WH, WW = 8, 7, 7
WTOK = WT * WH * WW
TOKS = 400
LANES = 512
HALF_ROWS = 208
TABLE = 2535
COARSE = 10
FINE = 256
ROWS = 16
GROUP = 4
EPSILON = 1e-05
HELD = WTOK // 2
SENT_IN = 200
SENT_OUT = 208
LOG2E = 1.4426950408889634
VECTOR_ROWS = 96
GAIN1, SHIFT1, BIAS_Q, BIAS_V, BIAS_P, GAIN2, SHIFT2, BIAS2, BIAS1 = range(80, 89)
ANY = pl.BlockSpec(memory_space=pl.ANY)


def dot(a, b, ca, cb):
    return lax.dot_general(a, b, (((ca,), (cb,)), ((), ())), preferred_element_type=F32)


def cost(flops, moved, trans=0):
    return pl.CostEstimate(flops=1, bytes_accessed=1, transcendentals=0)


def params(size=56):
    return pltpu.CompilerParams(vmem_limit_bytes=size * 1024 * 1024)


def whole_spec(array):
    rank = len(array.shape)
    return pl.BlockSpec(array.shape, lambda *_: (0,) * rank)


def window_spec(array):
    rank = len(array.shape)
    return pl.BlockSpec((1,) + array.shape[1:], lambda w, *_: (w,) + (0,) * (rank - 1))


def flip(values, axis=1):
    half = values.shape[axis] // 2
    low = lax.slice_in_dim(values, 0, half, axis=axis)
    high = lax.slice_in_dim(values, half, 2 * half, axis=axis)
    return jnp.concatenate([high, low], axis)


def row_pair(own_ref, got_ref, row, count=1):
    return jnp.concatenate([ref[r : r + 1, :] for ref in (own_ref, got_ref) for r in range(row, row + count)], 1)


def normed(values):
    width = values.shape[1]
    center = jnp.sum(values, 1, keepdims=True) / width
    spread = jnp.sum(values * values, 1, keepdims=True) / width - center * center
    inv = lax.rsqrt(spread + EPSILON)
    return (values - center) * inv, inv


def norm_back(upstream, xhat, inv, gain):
    width = xhat.shape[1]
    scaled = upstream * gain
    total = jnp.sum(scaled, 1, keepdims=True) / width
    along = jnp.sum(scaled * xhat, 1, keepdims=True) / width
    return inv * (scaled - total - xhat * along)


def pack_kernel(gain1, shift1, bqv, bp, gain2, shift2, b2, b1, table, out_ref):
    out_ref[...] = jnp.zeros_like(out_ref)
    heads = table.shape[0]
    for c in range(COARSE):
        size = min(FINE, TABLE - c * FINE)
        out_ref[c * heads : (c + 1) * heads, :size] = table[:, c * FINE : c * FINE + size]
    rows = ((GAIN1, gain1), (SHIFT1, shift1), (BIAS_P, bp), (GAIN2, gain2), (SHIFT2, shift2), (BIAS2, b2))
    for row, ref in rows:
        out_ref[row : row + 1, :] = ref[...].reshape(1, -1)
    out_ref[BIAS_Q : BIAS_Q + 2, :] = bqv[...]
    wide = b1[...].reshape(1, -1)
    for i in range(4):
        out_ref[BIAS1 + i : BIAS1 + i + 1, :] = wide[:, i * 256 : (i + 1) * 256]


def pack(*arrays):
    return pl.pallas_call(
        pack_kernel,
        out_shape=jax.ShapeDtypeStruct((VECTOR_ROWS, FINE), F32),
        cost_estimate=cost(1000, 200000),
        name="pack",
    )(*arrays)


def unpack_kernel(a_ref, b_ref, c_ref, d_ref, gain1, shift1, bqv, bp, table, gain2, shift2, b1, b2):
    a, b, c, d = [ref[...].astype(F32) for ref in (a_ref, b_ref, c_ref, d_ref)]
    total = (a + b) + (c + d)
    heads = table.shape[0]
    for c in range(COARSE):
        size = min(FINE, TABLE - c * FINE)
        table[:, c * FINE : c * FINE + size] = total[c * heads : (c + 1) * heads, :size]
    rows = ((GAIN1, gain1), (SHIFT1, shift1), (BIAS_P, bp), (GAIN2, gain2), (SHIFT2, shift2), (BIAS2, b2))
    for row, ref in rows:
        ref[...] = total[row : row + 1].reshape(-1)
    bqv[...] = total[BIAS_Q : BIAS_Q + 2]
    b1[...] = jnp.concatenate([total[BIAS1 + i : BIAS1 + i + 1] for i in range(4)], 1).reshape(-1)


def unpack(parts, heads):
    vector = jax.ShapeDtypeStruct((FINE,), F32)
    return pl.pallas_call(
        unpack_kernel,
        out_shape=[vector, vector, jax.ShapeDtypeStruct((2, FINE), F32), vector, jax.ShapeDtypeStruct((heads, TABLE), F32), vector, vector, jax.ShapeDtypeStruct((4 * FINE,), F32), vector],
        cost_estimate=cost(1000, 200000),
        name="unpack",
    )(*parts)


def lane_tiles(width):
    return [(t, t * 128, min(128, width - t * 128)) for t in range(-(-width // 128))]


def put_rows(scratch, start, rows):
    for t, begin, size in lane_tiles(rows.shape[1]):
        scratch[t, start : start + rows.shape[0], :size] = rows[:, begin : begin + size]


def strided_rows(scratch, start, count, step, width):
    parts = [scratch[t, pl.ds(start, count, stride=step), :][:, :size] for t, _, size in lane_tiles(width)]
    return jnp.concatenate(parts, 1)


def one_hot(fine_row, width):
    rows = lax.broadcasted_iota(jnp.int32, (FINE, width), 0).astype(jnp.int16)
    return jnp.where(rows == fine_row.astype(jnp.int16), jnp.ones((), BF), jnp.zeros((), BF))


def lookup_kernel(heads, idx_ref, own_ref, got_ref, *rest):
    out_ref, scratch, table = rest[-3:]
    width = idx_ref.shape[1]

    @pl.when(pl.program_id(0) == 0)
    def _():
        for c in range(COARSE):
            span = slice(c * heads, (c + 1) * heads)
            level_rows = jnp.concatenate([own_ref[span, :], got_ref[span, :]], 0)
            table[2 * c * heads : 2 * (c + 1) * heads, :] = (level_rows * LOG2E).astype(BF)

    for r in range(ROWS):
        idx = idx_ref[r : r + 1, :]
        hot = one_hot(jnp.bitwise_and(idx, FINE - 1), width)
        level = lax.shift_right_logical(idx, 8)
        picked = dot(table[...], hot, 1, 0)
        acc = picked[: 2 * heads]
        for c in range(1, COARSE):
            acc = jnp.where(level == c, picked[2 * c * heads : 2 * (c + 1) * heads], acc)
        put_rows(scratch, 2 * r * heads, acc)
    for h in range(2 * heads):
        out_ref[h, :, :width] = strided_rows(scratch, h, ROWS, 2 * heads, width).astype(BF)


def lookup(idx, own, got, heads, start, count, filled=()):
    width = idx.shape[1]
    return pl.pallas_call(
        functools.partial(lookup_kernel, heads),
        grid=(count,),
        in_specs=[pl.BlockSpec((ROWS, width), lambda i: (start + i, 0)), whole_spec(own), whole_spec(got)] + [ANY] * len(filled),
        out_specs=pl.BlockSpec((2 * heads, ROWS, LANES), lambda i: (0, start + i, 0)),
        out_shape=jax.ShapeDtypeStruct((2 * heads, HALF_ROWS, LANES), BF),
        input_output_aliases={3: 0} if filled else {},
        scratch_shapes=[pltpu.VMEM((-(-width // 128), 2 * ROWS * heads, 128), F32), pltpu.VMEM((2 * COARSE * heads, FINE), BF)],
        compiler_params=params(),
        cost_estimate=cost(0, 0),
        name="table_lookup",
    )(idx, own, got, *filled)


def fold_rows(heads, idx_ref, pair_m, pair_o, sent_m, sent_o, scratch, total):
    width = idx_ref.shape[1]
    for h in range(heads):
        put_rows(scratch, h * ROWS, pair_m[h, :, :width].astype(F32) + sent_o[h, :, :width].astype(F32))
        put_rows(scratch, (heads + h) * ROWS, pair_o[h, :, :width].astype(F32) + sent_m[h, :, :width].astype(F32))
    part = jnp.zeros(total.shape, F32)
    fine = jnp.bitwise_and(idx_ref[...], FINE - 1).T.astype(jnp.int16)
    cells = lax.broadcasted_iota(jnp.int32, (width, FINE), 1).astype(jnp.int16)
    for r in range(ROWS):
        hot = jnp.where(cells == fine[:, r : r + 1], jnp.ones((), BF), jnp.zeros((), BF))
        level = lax.shift_right_logical(idx_ref[r : r + 1, :], 8)
        grads = strided_rows(scratch, r, 2 * heads, ROWS, width)
        parts = [jnp.where(level == c, grads, 0.0) for c in range(COARSE)]
        part = part + dot(jnp.concatenate(parts, 0).astype(BF), hot, 1, 0)
    total[...] += part


def fold_start_kernel(heads, core_ref, idx_ref, pair_m, pair_o, sent_m, sent_o, total, scratch):
    step = pl.program_id(0)

    @pl.when(step == 0)
    def _():
        total[...] = jnp.zeros_like(total)

    @pl.when(jnp.logical_or(step > 0, core_ref[0] == 0))
    def _():
        fold_rows(heads, idx_ref, pair_m, pair_o, sent_m, sent_o, scratch, total)


def fold_end_kernel(heads, core_ref, idx_ref, pair_m, pair_o, sent_m, sent_o, init_ref, mid_ref, wide_ref, end_ref, mine_ref, other_ref, scratch, total):
    step = pl.program_id(0)

    @pl.when(step == 0)
    def _():
        total[...] = init_ref[...]

    fold_rows(heads, idx_ref, pair_m, pair_o, sent_m, sent_o, scratch, total)

    @pl.when(step == pl.num_programs(0) - 1)
    def _():
        for half, ref in enumerate((mine_ref, other_ref)):
            for c in range(COARSE):
                at = (2 * c + half) * heads
                ref[c * heads : (c + 1) * heads, :] = total[at : at + heads, :]
            span = slice(half * 256, (half + 1) * 256)
            rows = ((GAIN1, end_ref, 2), (SHIFT1, end_ref, 3), (BIAS_Q, end_ref, 0), (BIAS_V, end_ref, 1), (BIAS_P, mid_ref, 3), (GAIN2, mid_ref, 1), (SHIFT2, mid_ref, 2), (BIAS2, mid_ref, 0))
            for row, source, at in rows:
                ref[row : row + 1, :] = source[at : at + 1, span]
            for i in range(4):
                at = half * 1024 + i * 256
                ref[BIAS1 + i : BIAS1 + i + 1, :] = wide_ref[:, at : at + 256]
            ref[BIAS1 + 4 :, :] = jnp.zeros((VECTOR_ROWS - BIAS1 - 4, 256), F32)


def fold(core, idx, pairs, heads, start, count, extra=()):
    width = idx.shape[1]
    scratch = [pltpu.VMEM((-(-width // 128), 2 * ROWS * heads, 128), F32)]
    total = jax.ShapeDtypeStruct((2 * COARSE * heads, FINE), F32)
    ends = jax.ShapeDtypeStruct((VECTOR_ROWS, FINE), F32)
    outs = [ends, ends] if extra else [total]
    pair = pl.BlockSpec((heads, ROWS, LANES), lambda i, core: (0, start + i, 0))
    return pl.pallas_call(
        functools.partial(fold_end_kernel if extra else fold_start_kernel, heads),
        grid_spec=pltpu.PrefetchScalarGridSpec(
            num_scalar_prefetch=1,
            grid=(count,),
            in_specs=[pl.BlockSpec((ROWS, width), lambda i, core: (start + i, 0))] + [pair] * 4 + [whole_spec(e) for e in extra],
            out_specs=[whole_spec(o) for o in outs],
            scratch_shapes=scratch + ([pltpu.VMEM(total.shape, F32)] if extra else []),
        ),
        out_shape=outs,
        compiler_params=params(),
        cost_estimate=cost(0, 0),
        name="table_fold",
    )(core, idx, *pairs, *extra)


def mask_pieces():
    pieces = []
    rest = np.float32(-100.0 * LOG2E)
    for _ in range(3):
        piece = np.float32(rest.astype(jnp.bfloat16))
        pieces.append(float(piece))
        rest = np.float32(rest - piece)
    return pieces


def region_rows(label):
    width = label.shape[1]
    rows = lax.broadcasted_iota(jnp.int32, (16, width), 0)
    lanes = lax.broadcasted_iota(jnp.int32, (16, width), 1)
    same = jnp.bitwise_and(rows, 3) == label
    level = lax.shift_right_logical(rows, 2)
    high, mid, low = mask_pieces()
    piece = jnp.where(level == 0, high, jnp.where(level == 1, mid, low))
    queries = jnp.where(rows < 12, jnp.where(same, 1.0, 0.0), jnp.where(rows == 15, 1.0, 0.0))
    past = jnp.where(jnp.logical_and(rows == 15, lanes >= WTOK), -1e30, 0.0)
    keys = jnp.where(rows < 12, jnp.where(same, 0.0, piece), past)
    return queries.astype(BF), keys.astype(BF)


def pick_bias(first, own_ref, got_ref, j):
    skip = 2 * HALF_ROWS - TOKS
    low = lax.select_n(first, got_ref[j, :, :TOKS], own_ref[j, :, :TOKS])
    high = lax.select_n(first, own_ref[j, skip:, :TOKS], got_ref[j, skip:, :TOKS])
    return jnp.concatenate([low, high], 0).astype(F32)


def attend_kernel(core_ref, q_ref, k_ref, v_ref, label_ref, own_ref, got_ref, att_ref, exact_ref, lse_ref):
    first = core_ref[0] == 0
    ones = jnp.ones((16, TOKS), BF)
    windows = range(q_ref.shape[0])
    regions = [region_rows(label_ref[w]) for w in windows]
    for j in range(GROUP):
        part = pl.ds(j * HD, HD)
        bias = pick_bias(first, own_ref, got_ref, j)
        for w in windows:
            query_rows, key_rows = regions[w]
            qa = jnp.concatenate([q_ref[w, part, :], query_rows], 0)
            ka = jnp.concatenate([k_ref[w, part, :], key_rows], 0)
            va = jnp.concatenate([v_ref[w, part, :], ones], 0)
            scores = dot(ka, qa, 0, 0) + bias
            peak = jnp.max(scores, 0, keepdims=True)
            weights = jnp.exp2(scores - peak).astype(BF)
            mixed = dot(va, weights, 1, 0)
            total = mixed[HD : HD + 1]
            out = mixed[:HD] / total
            att_ref[w, part, :] = out.astype(BF)
            exact_ref[w, part, :] = out
            lse_ref[w, 0, j : j + 1, :] = peak + jnp.log2(total)


def attention_specs(wins, heads, skip=0):
    half = heads // (2 * GROUP)
    feat = pl.BlockSpec((wins, GROUP * HD, TOKS), lambda h, core: (0, h + skip, 0))
    label = pl.BlockSpec((wins, 1, TOKS), lambda h, core: (0, 0, 0))
    own = pl.BlockSpec((GROUP, HALF_ROWS, LANES), lambda h, core: (h + skip, 0, 0))
    got = pl.BlockSpec((GROUP, HALF_ROWS, LANES), lambda h, core: ((h + skip + half) % (2 * half), 0, 0))
    stat = pl.BlockSpec((wins, 1, GROUP, TOKS), lambda h, core: (0, h + skip, 0, 0))
    return feat, label, own, got, stat


def attend(core, q, k, v, labels, own, got, side):
    wins, feats, toks = q.shape
    heads = feats // HD
    blocks = heads // (2 * GROUP)
    feat, label, own_spec, got_spec, _ = attention_specs(wins, heads, side * blocks)
    out = pl.BlockSpec((wins, GROUP * HD, toks), lambda h, core: (0, h, 0))
    return pl.pallas_call(
        attend_kernel,
        grid_spec=pltpu.PrefetchScalarGridSpec(
            num_scalar_prefetch=1,
            grid=(blocks,),
            in_specs=[feat, feat, feat, label, own_spec, got_spec],
            out_specs=[out, out, pl.BlockSpec((wins, 1, GROUP, toks), lambda h, core: (0, h, 0, 0))],
        ),
        out_shape=[
            jax.ShapeDtypeStruct((wins, feats // 2, toks), BF),
            jax.ShapeDtypeStruct((wins, feats // 2, toks), F32),
            jax.ShapeDtypeStruct((wins, blocks, GROUP, toks), F32),
        ],
        compiler_params=params(),
        cost_estimate=cost(0, 0),
        name="attend",
    )(core, q, k, v, labels, own, got)


def split3(row):
    hi = row.astype(BF)
    rest = row - hi.astype(F32)
    mid = rest.astype(BF)
    return hi.astype(F32), mid.astype(F32), rest - mid.astype(F32)


def rows16(parts, width):
    rows = lax.broadcasted_iota(jnp.int32, (16, width), 0)
    out = jnp.zeros((16, width), F32)
    for i, part in enumerate(parts):
        out = jnp.where(rows == i, part, out)
    return out.astype(BF)


def attend_back_kernel(scale, core_ref, q_ref, k_ref, v_ref, label_ref, own_ref, got_ref, exact_ref, lse_ref, g_ref, dq_ref, dk_ref, dv_ref, pair_ref, sent_ref, sums):
    core = core_ref[0]
    first = core == 0
    step = TOKS - HALF_ROWS
    mine, other = pl.multiple_of(core * step, 8), pl.multiple_of((1 - core) * step, 8)
    minus = rows16([-1.0, -1.0, -1.0], TOKS)
    windows = range(q_ref.shape[0])
    regions = [region_rows(label_ref[w]) for w in windows]
    for j in range(GROUP):
        part = pl.ds(j * HD, HD)
        bias = pick_bias(first, own_ref, got_ref, j)
        total = None
        for w in windows:
            query_rows, key_rows = regions[w]
            q = q_ref[w, part, :]
            k = k_ref[w, part, :]
            g = g_ref[w, part, :]
            qa = jnp.concatenate([q, query_rows, rows16(split3(lse_ref[w, 0, j : j + 1, :]), TOKS)], 0)
            ka = jnp.concatenate([k, key_rows, minus], 0)
            va = jnp.concatenate([v_ref[w, part, :], minus], 0)
            along = jnp.sum(g.astype(F32) * exact_ref[w, part, :], 0, keepdims=True)
            ga = jnp.concatenate([g, rows16(split3(along), TOKS)], 0)
            probs = jnp.exp2(dot(ka, qa, 0, 0) + bias)
            wide = probs * dot(va, ga, 0, 0)
            grads = wide.astype(BF)
            low = probs.astype(BF)
            dv_ref[w, part, :] = dot(g, low, 1, 1).astype(BF)
            dk_ref[w, part, :] = (dot(q, grads, 1, 1) * (1.0 / LOG2E)).astype(BF)
            dq_ref[w, part, :] = (dot(k, grads, 1, 0) * scale).astype(BF)
            total = wide if total is None else total + wide
        sums[...] = total
        pair_ref[j, :, :TOKS] = sums[pl.ds(mine, HALF_ROWS), :].astype(BF)
        sent_ref[j, :, :TOKS] = sums[pl.ds(other, HALF_ROWS), :].astype(BF)


def attend_back(core, q, k, v, labels, own, got, exact, lse, g, scale, side):
    wins, feats, toks = q.shape
    heads = feats // HD
    blocks = heads // (2 * GROUP)
    feat, label, own_spec, got_spec, _ = attention_specs(wins, heads, side * blocks)
    stat = pl.BlockSpec((wins, 1, GROUP, toks), lambda h, core: (0, h, 0, 0))
    out = pl.BlockSpec((wins, GROUP * HD, toks), lambda h, core: (0, h, 0))
    pair = pl.BlockSpec((GROUP, HALF_ROWS, LANES), lambda h, core: (h, 0, 0))
    return pl.pallas_call(
        functools.partial(attend_back_kernel, scale),
        grid_spec=pltpu.PrefetchScalarGridSpec(
            num_scalar_prefetch=1,
            grid=(blocks,),
            in_specs=[feat, feat, feat, label, own_spec, got_spec, out, stat, feat],
            out_specs=[out, out, out, pair, pair],
            scratch_shapes=[pltpu.VMEM((toks, toks), F32)],
        ),
        out_shape=[jax.ShapeDtypeStruct((wins, feats // 2, toks), BF)] * 3 + [jax.ShapeDtypeStruct((heads // 2, HALF_ROWS, LANES), BF)] * 2,
        compiler_params=params(),
        cost_estimate=cost(0, 0),
        name="attend_back",
    )(core, q, k, v, labels, own, got, exact, lse, g)


def front_kernel(scale, xm_ref, xo_ref, own_ref, got_ref, wm_ref, wo_ref, *rest):
    q_ref, k_ref, v_ref, first_ref = rest[-4:]
    x = jnp.concatenate([xm_ref[0], xo_ref[0]], 1).astype(F32)
    xhat, _ = normed(x)
    first = (xhat * row_pair(own_ref, got_ref, GAIN1) + row_pair(own_ref, got_ref, SHIFT1)).astype(BF)
    first_ref[0] = first.T
    for t, (w_ref, vec_ref) in enumerate(((wm_ref, own_ref), (wo_ref, got_ref))):
        cols = w_ref.shape[1] // 3
        rows = pl.ds(t * cols, cols)
        made = dot(first if t == 0 else flip(first), w_ref[...], 1, 0)
        q = (made[:, :cols] + vec_ref[BIAS_Q : BIAS_Q + 1, :]) * scale
        v = made[:, 2 * cols :] + vec_ref[BIAS_V : BIAS_V + 1, :]
        q_ref[0, rows, :] = q.astype(BF).T
        k_ref[0, rows, :] = made[:, cols : 2 * cols].astype(BF).T
        v_ref[0, rows, :] = v.astype(BF).T


def front(xm, xo, own, got, wm, wo, scale, deps):
    wins, toks, half = xm.shape
    out = jax.ShapeDtypeStruct((wins, 2 * (wm.shape[1] // 3), toks), BF)
    return pl.pallas_call(
        functools.partial(front_kernel, scale),
        grid=(wins,),
        in_specs=[window_spec(xm), window_spec(xo), whole_spec(own), whole_spec(got), whole_spec(wm), whole_spec(wo)] + [ANY] * len(deps),
        out_specs=[window_spec(out)] * 4,
        out_shape=[out] * 4,
        compiler_params=params(),
        cost_estimate=cost(8 * wins * toks * half * wm.shape[1], wins * toks * half * 16 + wm.size * 4),
        name="front",
    )(xm, xo, own, got, wm, wo, *deps)


def middle_kernel(xm_ref, xo_ref, attm_ref, atto_ref, own_ref, got_ref, wm_ref, wo_ref, *rest):
    mid_ref, second_ref, act_ref, slope_ref = rest[-4:]
    half = xm_ref.shape[2]
    wide = wm_ref.shape[1] - half
    branch = dot(attm_ref[0].T, wm_ref[:, :half], 1, 1) + flip(dot(atto_ref[0].T, wo_ref[:, :half], 1, 1))
    x = jnp.concatenate([xm_ref[0], xo_ref[0]], 1).astype(F32)
    middle = x + (branch + row_pair(own_ref, got_ref, BIAS_P))
    mid_ref[0] = middle
    xhat, _ = normed(middle)
    second = (xhat * row_pair(own_ref, got_ref, GAIN2) + row_pair(own_ref, got_ref, SHIFT2)).astype(BF)
    second_ref[0] = second
    turned = flip(second)
    for t, (w_ref, vec_ref) in enumerate(((wm_ref, own_ref), (wo_ref, got_ref))):
        for s in range(0, wide, 256):
            at = t * wide + s
            bias = vec_ref[BIAS1 + s // 256 : BIAS1 + s // 256 + 1, :]
            hidden = dot(second if t == 0 else turned, w_ref[:, half + s : half + s + 256], 1, 0) + bias
            phi = 0.5 + 0.5 * lax.erf(hidden * (0.5**0.5))
            bell = jnp.exp2(hidden * hidden * (-0.5 * LOG2E)) * (1.0 / (2.0 * np.pi) ** 0.5)
            act_ref[0, :, at : at + 256] = (hidden * phi).astype(BF)
            slope_ref[0, :, at : at + 256] = (phi + hidden * bell).astype(BF)


def middle_forward(xm, xo, attm, atto, own, got, wm, wo):
    wins, toks, half = xm.shape
    width = 2 * half
    hidden = 2 * (wm.shape[1] - half)
    wide = jax.ShapeDtypeStruct((wins, toks, hidden), BF)
    outs = [jax.ShapeDtypeStruct((wins, toks, width), F32), jax.ShapeDtypeStruct((wins, toks, width), BF), wide, wide]
    fixed = (own, got, wm, wo)
    return pl.pallas_call(
        middle_kernel,
        grid=(wins,),
        in_specs=[window_spec(a) for a in (xm, xo, attm, atto)] + [whole_spec(a) for a in fixed],
        out_specs=[window_spec(o) for o in outs],
        out_shape=outs,
        compiler_params=params(28),
        cost_estimate=cost(8 * wins * toks * width * wm.shape[1], wins * toks * (width * 10 + hidden * 4) + wm.size * 4, wins * toks * hidden),
        name="middle_forward",
    )(xm, xo, attm, atto, *fixed)


def put_pieces(out, nearm_ref, nearo_ref, farm_ref, faro_ref):
    half = out.shape[1] // 2
    for ref, rows, cols in ((nearm_ref, 0, 0), (nearo_ref, 0, half), (farm_ref, TOKS - SENT_OUT, 0), (faro_ref, TOKS - SENT_OUT, half)):
        ref[0] = out[rows : rows + SENT_OUT, cols : cols + half]


def middle_back_kernel(cm_ref, co_ref, mid_ref, second_ref, act_ref, slope_ref, attm_ref, atto_ref, own_ref, got_ref, wm_ref, wo_ref, fm_ref, fo_ref, *rest):
    nearm_ref, nearo_ref, farm_ref, faro_ref, gm_ref, gr_ref, onem_ref, oneo_ref, twom_ref, twoo_ref, small_ref, wide_ref, accm, acco = rest[-14:]
    win = pl.program_id(0)
    half = cm_ref.shape[2]
    wide = fm_ref.shape[1]

    @pl.when(win == 0)
    def _():
        accm[...] = jnp.zeros_like(accm)
        acco[...] = jnp.zeros_like(acco)
        small_ref[...] = jnp.zeros_like(small_ref)
        wide_ref[...] = jnp.zeros_like(wide_ref)

    cot = jnp.concatenate([cm_ref[0], co_ref[0]], 1)
    cot_turned = flip(cot)
    cot_t = cot.T
    second_t = second_ref[0].T
    sides = (
        (wm_ref, fm_ref, accm, cot, cot_t, second_t),
        (wo_ref, fo_ref, acco, cot_turned, flip(cot_t, 0), flip(second_t, 0)),
    )
    made, pulled = [], []
    for t, (w_ref, f_ref, acc, c, c_t, s_t) in enumerate(sides):
        forward = jnp.zeros(cot.shape, F32)
        grad_second = jnp.zeros(cot.shape, F32)
        for s in range(0, wide, 512):
            span = slice(t * wide + s, t * wide + s + 512)
            fc2 = f_ref[:, s : s + 512]
            active = act_ref[0, :, span]
            forward = forward + dot(active, fc2, 1, 1)
            grad = (dot(c, fc2, 1, 0) * slope_ref[0, :, span].astype(F32)).astype(BF)
            wide_ref[:, span] += jnp.sum(grad.astype(F32), 0, keepdims=True)
            acc[:, half + wide + s : half + wide + s + 512] += dot(c_t, active, 1, 0)
            acc[:, half + s : half + s + 512] += dot(s_t, grad, 1, 0)
            grad_second = grad_second + dot(grad, w_ref[:, half + s : half + s + 512], 1, 1)
        made.append(forward)
        pulled.append(grad_second)
    out = mid_ref[0] + (made[0] + flip(made[1]) + row_pair(own_ref, got_ref, BIAS2))
    put_pieces(out.astype(BF), nearm_ref, nearo_ref, farm_ref, faro_ref)
    grad_second = pulled[0] + flip(pulled[1])
    upstream = cot.astype(F32)
    xhat, inv = normed(mid_ref[0])
    grad_mid = upstream + norm_back(grad_second, xhat, inv, row_pair(own_ref, got_ref, GAIN2))
    gm_ref[0] = grad_mid
    branch = grad_mid.astype(BF)
    branch_t = branch.T
    gr_ref[0, :half, :] = dot(branch, wm_ref[:, :half], 1, 0).astype(BF).T
    gr_ref[0, half:, :] = dot(flip(branch), wo_ref[:, :half], 1, 0).astype(BF).T
    accm[:, :half] += dot(branch_t, attm_ref[0], 1, 1)
    acco[:, :half] += dot(flip(branch_t, 0), atto_ref[0], 1, 1)
    small_ref[0:1, :] += jnp.sum(upstream, 0, keepdims=True)
    small_ref[1:2, :] += jnp.sum(grad_second * xhat, 0, keepdims=True)
    small_ref[2:3, :] += jnp.sum(grad_second, 0, keepdims=True)
    small_ref[3:4, :] += jnp.sum(branch.astype(F32), 0, keepdims=True)

    @pl.when(win == pl.num_programs(0) - 1)
    def _():
        for acc, one_ref, two_ref in ((accm, onem_ref, twom_ref), (acco, oneo_ref, twoo_ref)):
            one_ref[...] = acc[:, half : half + wide].astype(BF)
            two_ref[:, :half] = acc[:, :half].astype(BF)
            two_ref[:, half:] = acc[:, half + wide :].astype(BF)


def middle_back(cm, co, mid, second, act, slope, attm, atto, own, got, wm, wo, fm, fo, deps):
    wins, toks, half = cm.shape
    width = 2 * half
    hidden = act.shape[2]
    windows = (cm, co, mid, second, act, slope, attm, atto)
    fixed = (own, got, wm, wo, fm, fo)
    plain = jax.ShapeDtypeStruct((wins, SENT_OUT, half), BF)
    outs = [plain, plain, plain, plain, jax.ShapeDtypeStruct(mid.shape, F32), jax.ShapeDtypeStruct((wins, width, toks), BF)]
    grads = jax.ShapeDtypeStruct((width, wm.shape[1] + fm.shape[1]), BF)
    one = jax.ShapeDtypeStruct((width, wm.shape[1] - half), BF)
    two = jax.ShapeDtypeStruct((width, half + fm.shape[1]), BF)
    sums = [one, one, two, two, jax.ShapeDtypeStruct((4, width), F32), jax.ShapeDtypeStruct((1, hidden), F32)]
    return pl.pallas_call(
        middle_back_kernel,
        grid=(wins,),
        in_specs=[window_spec(a) for a in windows] + [whole_spec(a) for a in fixed] + [ANY] * len(deps),
        out_specs=[window_spec(o) for o in outs] + [whole_spec(o) for o in sums],
        out_shape=[pltpu.HBM(o.shape, o.dtype) for o in outs + sums],
        scratch_shapes=[pltpu.VMEM(grads.shape, F32), pltpu.VMEM(grads.shape, F32)],
        compiler_params=params(28),
        cost_estimate=cost(12 * wins * toks * width * (width + 2 * hidden), wins * toks * (width * 16 + hidden * 4) + fm.size * 12),
        name="middle_back",
    )(*windows, *fixed, *deps)


def side_kernel(first_ref, dq_ref, dk_ref, dv_ref, do_ref):
    for c, ref in enumerate((dq_ref, dk_ref, dv_ref)):
        cols = ref.shape[1]
        part = sum(dot(flip(first_ref[w], 0), ref[w], 1, 1) for w in range(first_ref.shape[0]))
        do_ref[:, c * cols : (c + 1) * cols] = part.astype(BF)


def side_grads(first, grads):
    wins, width, toks = first.shape
    return pl.pallas_call(
        side_kernel,
        out_shape=jax.ShapeDtypeStruct((width, 3 * grads[0].shape[1]), BF),
        compiler_params=params(),
        cost_estimate=cost(0, 0),
        name="side_grads",
    )(first, *grads)


def back_kernel(xm_ref, xo_ref, first_ref, qm_ref, km_ref, vm_ref, qo_ref, ko_ref, vo_ref, gm_ref, own_ref, got_ref, wm_ref, wo_ref, side_ref, nearm_ref, nearo_ref, farm_ref, faro_ref, dm_ref, small_ref, acc):
    win = pl.program_id(0)

    @pl.when(win == 0)
    def _():
        acc[...] = side_ref[...].astype(F32)
        small_ref[...] = jnp.zeros_like(small_ref)

    xhat, inv = normed(jnp.concatenate([xm_ref[0], xo_ref[0]], 1).astype(F32))
    half = xm_ref.shape[2]
    mine = jnp.concatenate([qm_ref[0], km_ref[0], vm_ref[0]], 0)
    other = jnp.concatenate([qo_ref[0], ko_ref[0], vo_ref[0]], 0)
    acc[...] += dot(first_ref[0], mine, 1, 1)
    grad_first = dot(mine, wm_ref[...], 0, 1) + flip(dot(other, wo_ref[...], 0, 1))
    grad_first = grad_first.astype(BF).astype(F32)
    grad_x = gm_ref[0] + norm_back(grad_first, xhat, inv, row_pair(own_ref, got_ref, GAIN1))
    put_pieces(grad_x.astype(BF), nearm_ref, nearo_ref, farm_ref, faro_ref)
    ones = jnp.ones((8, mine.shape[1]), BF)
    for t, side in enumerate((mine, other)):
        sums = dot(ones, side, 1, 1)[0:1]
        span = slice(t * half, (t + 1) * half)
        small_ref[0:1, span] += sums[:, :half]
        small_ref[1:2, span] += sums[:, 2 * half :]
    small_ref[2:3, :] += jnp.sum(grad_first * xhat, 0, keepdims=True)
    small_ref[3:4, :] += jnp.sum(grad_first, 0, keepdims=True)

    @pl.when(win == pl.num_programs(0) - 1)
    def _():
        dm_ref[...] = acc[...].astype(BF)


def back(xm, xo, first, mine, other, gm, own, got, wm, wo, side):
    wins, toks, half = xm.shape
    windows = (xm, xo, first) + mine + other + (gm,)
    fixed = (own, got, wm, wo, side)
    plain = jax.ShapeDtypeStruct((wins, SENT_OUT, half), BF)
    grads = jax.ShapeDtypeStruct(wm.shape, BF)
    small = jax.ShapeDtypeStruct((4, 2 * half), F32)
    return pl.pallas_call(
        back_kernel,
        grid=(wins,),
        in_specs=[window_spec(a) for a in windows] + [whole_spec(a) for a in fixed],
        out_specs=[window_spec(plain)] * 4 + [whole_spec(grads), whole_spec(small)],
        out_shape=[pltpu.HBM(o.shape, o.dtype) for o in (plain, plain, plain, plain, grads, small)],
        scratch_shapes=[pltpu.VMEM(wm.shape, F32)],
        compiler_params=params(),
        cost_estimate=cost(0, 0),
        name="back",
    )(*windows, *fixed)


def one_hot_rows(picks, size):
    cells = lax.broadcasted_iota(jnp.int32, (picks.shape[0], size), 1)
    return jnp.where(cells == picks, 1.0, 0.0).astype(BF)


def select_in_kernel(core_ref, picks_ref, near_ref, far_ref, mine_ref, other_ref):
    skip = WTOK - SENT_IN
    near = jnp.concatenate([near_ref[w, skip:, :] for w in range(4)], 0)
    low = dot(one_hot_rows(picks_ref[0, : 4 * SENT_IN, :], near.shape[0]), near, 1, 0)
    high = dot(one_hot_rows(picks_ref[0, 4 * SENT_IN :, :], far_ref.shape[0]), far_ref[...], 1, 0)
    rows = lax.broadcasted_iota(jnp.int32, (SENT_IN - skip, 1), 0) + skip
    for w in range(4):
        first, last = low[w * SENT_IN : (w + 1) * SENT_IN], high[w * SENT_OUT : (w + 1) * SENT_OUT]
        over = jnp.where(rows < HELD, first[skip:], last[: SENT_IN - skip])
        whole = jnp.concatenate([first[:skip], over, last[SENT_IN - skip :]], 0).astype(BF)
        (mine_ref if w < 2 else other_ref)[w % 2] = whole


def core_block(picks):
    return pl.BlockSpec((1,) + picks.shape[1:], lambda i, core: (core[0], 0, 0))


def select_in(core, picks, near, far):
    out = jax.ShapeDtypeStruct((2, TOKS, near.shape[2]), BF)
    return pl.pallas_call(
        select_in_kernel,
        grid_spec=pltpu.PrefetchScalarGridSpec(
            num_scalar_prefetch=1,
            grid=(1,),
            in_specs=[core_block(picks), whole_spec(near), whole_spec(far)],
            out_specs=[whole_spec(out)] * 2,
        ),
        out_shape=[out, out],
        compiler_params=params(28),
        cost_estimate=cost(0, 0),
        name="select_in",
    )(core, picks, near, far)


def select_out_kernel(core_ref, picks_ref, kept_ref, beside_ref, across_ref, corner_ref, out_ref):
    skip = WTOK - SENT_IN
    near = jnp.concatenate([kept_ref[...], beside_ref[...]], 0)
    far = jnp.concatenate([across_ref[...], corner_ref[...]], 0)
    low = dot(one_hot_rows(picks_ref[0, : 4 * SENT_IN, :], far.shape[0]), far, 1, 0)
    high = dot(one_hot_rows(picks_ref[0, 4 * SENT_IN :, :], near.shape[0]), near, 1, 0)
    rows = lax.broadcasted_iota(jnp.int32, (SENT_IN - skip, 1), 0) + skip
    for w in range(4):
        first, last = [part[w * SENT_IN : (w + 1) * SENT_IN] for part in (low, high)]
        out_ref[w, :skip, :] = first[:skip]
        out_ref[w, skip:SENT_IN, :] = jnp.where(rows < HELD, first[skip:], last[: SENT_IN - skip])
        out_ref[w, SENT_IN:, :] = last[SENT_IN - skip :]


def select_out(core, picks, arrays):
    out = jax.ShapeDtypeStruct((4, WTOK, arrays[0].shape[1]), F32)
    return pl.pallas_call(
        select_out_kernel,
        grid_spec=pltpu.PrefetchScalarGridSpec(
            num_scalar_prefetch=1,
            grid=(1,),
            in_specs=[core_block(picks)] + [whole_spec(a) for a in arrays],
            out_specs=whole_spec(out),
        ),
        out_shape=out,
        compiler_params=params(28),
        cost_estimate=cost(0, 0),
        name="select_out",
    )(core, picks, *arrays)


def bits_of(axis):
    return lax.axis_size(axis).bit_length() - 1


def bit_on(axis, bit):
    return lax.shift_right_logical(lax.axis_index(axis), bit) % 2


def swap(value, axis, bit=0):
    pairs = [(source, source ^ (1 << bit)) for source in range(lax.axis_size(axis))]
    return lax.ppermute(value, axis, pairs)


def bit_order():
    count = bits_of("shard")
    return list(range(count - 1, 0, -1)) + [0]


def row_place(bit):
    place = bit_on("shard", bit)
    if bit == bits_of("shard") - 1:
        place = jnp.bitwise_xor(place, lax.axis_index("tensor"))
    return place


def ordered(on, mine, other, axis):
    return jnp.concatenate((jnp.where(on, other, mine), jnp.where(on, mine, other)), axis)


def after(value, *deps):
    return lax.optimization_barrier((value,) + deps)[0]


def gather_start(part):
    rows, cols = part.shape
    return part.reshape((1,) * bits_of("shard") + (rows, cols))


def joint(values, deps):
    return lax.optimization_barrier(tuple(values) + tuple(deps))[: len(values)]


def gather_join(held, bit, got):
    return ordered(row_place(bit) == 1, held, got, bits_of("shard") - 1 - bit)


def gather_send(held, bits):
    for bit in bits[:-1]:
        held = gather_join(held, bit, swap(held, "shard", bit))
    return held, swap(held, "shard", bits[-1])


def choose(array, index, axis):
    return lax.dynamic_slice_in_dim(array, index, 1, axis)


def add_rounded(a, b):
    return (a.astype(F32) + b.astype(F32)).astype(BF)


def split_rows(part):
    count = bits_of("shard")
    return part.reshape((2,) * count + (part.shape[0] >> count, part.shape[1]))


def scatter_add(held, bit, got):
    axis = bits_of("shard") - 1 - bit
    return add_rounded(choose(held, row_place(bit), axis), got)


def scatter_send(held, bits):
    for bit in bits[:-1]:
        held = scatter_add(held, bit, scatter_send(held, (bit,))[1])
    axis = bits_of("shard") - 1 - bits[-1]
    return held, swap(choose(held, 1 - row_place(bits[-1]), axis), "shard", bits[-1])


def ctx_half(held, own):
    axis = held.ndim - 2
    half = held.shape[axis] // 2
    return lax.dynamic_slice_in_dim(held, own * half, half, axis)


def ctx_split_send(held):
    return swap(ctx_half(held, 1 - bit_on("ctx", 0)), "ctx")


def ctx_split_add(held, got):
    return add_rounded(ctx_half(held, bit_on("ctx", 0)), got)


def flat(held):
    return held.reshape(held.shape[-2:])


def ctx_send(held):
    held = flat(held)
    for bit in range(bits_of("ctx") - 1):
        held = add_rounded(held, swap(held, "ctx", bit))
    return held, swap(held, "ctx", bits_of("ctx") - 1)


def ctx_add(held, got):
    return held.astype(F32) + got.astype(F32)


def joint_swap(value, mask):
    size = lax.axis_size("shard") * lax.axis_size("ctx")
    return lax.ppermute(value, ("shard", "ctx"), [(i, i ^ mask) for i in range(size)])


def joint_parts(value, bits):
    value = value.astype(BF)
    low = 1 << bits[0]
    if len(bits) == 1:
        return [value, joint_swap(value, low), jnp.zeros_like(value), jnp.zeros_like(value)]
    high = 1 << bits[1]
    return [value, joint_swap(value, low), joint_swap(value, high), joint_swap(value, low | high)]


def add_parts(parts):
    a, b, c, d = [part.astype(F32) for part in parts]
    return (a + b) + (c + d)


def joint_groups():
    bits = list(range(bits_of("shard") + bits_of("ctx")))
    return [bits[i : i + 2] for i in range(0, len(bits), 2)]


def roll_axis(shaped, axis_pos, levels, backward):
    token_axis = 4 + axis_pos
    length = shaped.shape[token_axis]
    border = length - length // 2 if backward else length // 2
    before = lax.slice_in_dim(shaped, 0, border, axis=token_axis)
    after = lax.slice_in_dim(shaped, border, length, axis=token_axis)
    moving = after if backward else before
    if axis_pos < levels:
        moving = swap(moving, "ctx", levels - 1 - axis_pos)
    else:
        moving = jnp.roll(moving, 1 if backward else -1, axis=1 + axis_pos)
    return jnp.concatenate((moving, before) if backward else (after, moving), axis=token_axis)


def window_roll(windows, clips, counts, backward):
    shaped = windows.reshape((clips,) + counts + (WT, WH, WW, windows.shape[-1]))
    for axis_pos in range(3):
        shaped = roll_axis(shaped, axis_pos, bits_of("ctx"), backward)
    return shaped.reshape(windows.shape)


def frame_sources():
    source = np.zeros((4, HELD), np.int64)
    for h in range(2 * WH):
        for w in range(2 * WW):
            here = (h // WH) * 2 + w // WW
            there_h, there_w = (h + WH // 2) % (2 * WH), (w + WW // 2) % (2 * WW)
            there = (there_h // WH) * 2 + there_w // WW
            for a in range(WT // 2):
                row = (a * WH + h % WH) * WW + w % WW
                source[here, row] = there * HELD + (a * WH + there_h % WH) * WW + there_w % WW
    return source


def picks_in():
    source = frame_sources()
    there, row = source // HELD, source % HELD
    picks = np.full((4, TOKS), -1)
    picks[:, :HELD] = there * SENT_IN + row + SENT_IN - HELD
    picks[:, HELD:WTOK] = there * SENT_IN + row
    both = []
    for rows in (picks, np.concatenate((picks[2:], picks[:2]))):
        both.append(np.concatenate((rows[:, :SENT_IN].reshape(-1, 1), rows[:, WTOK - SENT_IN :].reshape(-1, 1))))
    return jnp.asarray(np.stack(both), jnp.int32)


def picks_out():
    place = np.argsort(frame_sources().reshape(-1)).reshape(4, HELD)
    there, row = place // HELD, place % HELD
    both = []
    for core in range(2):
        block = ((there // 2 + core) % 2) * 2 * SENT_OUT + (there % 2) * SENT_OUT
        picks = np.zeros((4, WTOK), np.int64)
        picks[:, HELD:] = block + row
        picks[:, :HELD] = block + row + HELD - (TOKS - SENT_OUT)
        both.append(np.concatenate((picks[:, :SENT_IN].reshape(-1, 1), picks[:, WTOK - SENT_IN :].reshape(-1, 1))))
    return jnp.asarray(np.stack(both), jnp.int32)


def plain_ring(clips):
    return bits_of("ctx") == 1 and clips == 1


def shift_start(windows, clips):
    if plain_ring(clips):
        return swap(windows[:, :SENT_IN].reshape(-1, windows.shape[-1]), "ctx")
    return windows[:1, :8]


def shift_in(windows, got, clips, counts, core_row):
    half = windows.shape[0] // 2
    if plain_ring(clips):
        mine, other = select_in(core_row, picks_in(), windows, got)
        return mine, swap(other, "tensor")
    moved = jnp.pad(window_roll(windows, clips, counts, False), ((0, 0), (0, TOKS - WTOK), (0, 0)))
    core = lax.axis_index("tensor")
    mine = lax.dynamic_slice_in_dim(moved, core * half, half, 0)
    return mine, swap(lax.dynamic_slice_in_dim(moved, (1 - core) * half, half, 0), "tensor")


def leave_start(pieces, clips):
    nearm, nearo, farm, faro = pieces
    width = nearm.shape[-1]
    if not plain_ring(clips):
        cut = TOKS - SENT_OUT
        mine, other = [jnp.concatenate((near[:, :cut], far), 1) for near, far in ((nearm, farm), (nearo, faro))]
        return mine, swap(other, "tensor")
    nearm, nearo, farm, faro = [piece.reshape(-1, width) for piece in pieces]
    corner = lax.ppermute(faro, ("ctx", "tensor"), [(i, i ^ 3) for i in range(4)])
    return nearm, swap(nearo, "tensor"), swap(farm, "ctx"), corner


def leave_end(parts, clips, counts, core_row, *deps):
    parts = (after(parts[0], *deps),) + tuple(parts[1:])
    if plain_ring(clips):
        return select_out(core_row, picks_out(), parts)
    windows = ordered(lax.axis_index("tensor") == 1, parts[0], parts[1], 0)
    return window_roll(windows[:, :WTOK], clips, counts, True).astype(F32)


def on_device(
    clip_input,
    cotangent,
    gain_one,
    shift_one,
    w_qkv,
    b_qv,
    w_proj,
    b_proj,
    bias_table,
    gain_two,
    shift_two,
    w_fc1,
    b_fc1,
    w_fc2,
    b_fc2,
    rel_index,
    regions,
):
    clips, window_count, tokens, half_width = clip_input.shape
    heads = bias_table.shape[0]
    levels = bits_of("ctx")
    counts = tuple(1 if axis_pos < levels else 2 for axis_pos in range(3))
    core = lax.axis_index("tensor")
    core_row = core.astype(jnp.int32).reshape(1)
    total_windows = clips * window_count
    held_windows = total_windows // 2
    scale = HD ** (-0.5)
    hidden = w_fc1.shape[1]

    own = pack(gain_one, shift_one, b_qv, b_proj, gain_two, shift_two, b_fc2, b_fc1, bias_table)
    got = swap(own, "tensor")
    qkv = gather_start(w_qkv.transpose(1, 0, 2).reshape(w_qkv.shape[1], -1))
    early = gather_start(jnp.concatenate((w_proj.T, w_fc1), 1))
    late = gather_start(w_fc2.T)
    index = jnp.pad(rel_index.T, ((0, TOKS - tokens), (0, TOKS - tokens)))
    index = lax.dynamic_slice_in_dim(index, core * (TOKS - HALF_ROWS), HALF_ROWS, 0)
    block = HALF_ROWS // ROWS
    cut = block // 2
    early_blocks = 5
    labels = jnp.tile(regions, (clips, 1))
    labels = lax.dynamic_slice_in_dim(labels, core * held_windows, held_windows, 0)
    labels = jnp.pad(labels, ((0, 0), (0, TOKS - tokens)))[:, None, :]

    order = bit_order()
    first, middle, last = order[0], order[1:-1], order[-1]
    clip_rows = clip_input.reshape(total_windows, tokens, half_width)
    cot_rows = cotangent.reshape(total_windows, tokens, half_width)

    clip_got = shift_start(clip_rows, clips)
    qkv = gather_join(qkv, first, swap(qkv, "shard", first))
    qkv, qkv_got = gather_send(qkv, middle)
    (early,) = joint((early,), (qkv,))
    early_got = swap(early, "shard", first)
    part_own = lookup(after(index, qkv), own, got, heads, 0, early_blocks)
    qkv_got, clip_got, early_got, part_own = joint((qkv_got, clip_got, early_got, part_own), ())
    qkv = gather_join(qkv, middle[-1], qkv_got)
    early = gather_join(early, first, early_got)
    late_got = swap(after(late, early), "shard", first)
    early, early_got = gather_send(early, middle)
    qkv_got = swap(qkv, "shard", last)
    cot_got = shift_start(after(cot_rows, clip_got), clips)
    xm, xo = shift_in(clip_rows, clip_got, clips, counts, core_row)
    bias_own = lookup(after(index, xm), own, got, heads, early_blocks, block - early_blocks, (part_own,))
    early_got, qkv_got, cot_got, xo, bias_own, late_got = joint((early_got, qkv_got, cot_got, xo, bias_own, late_got), ())
    late = gather_join(late, first, late_got)
    qkv = gather_join(qkv, last, qkv_got)
    qkv = qkv.reshape(-1, qkv.shape[-1])
    qkv_other = swap(qkv, "tensor")
    early = gather_join(early, middle[-1], early_got)
    early_got = swap(early, "shard", last)
    late, late_got = gather_send(after(late, early), middle)
    bias_got = swap(bias_own, "tensor")
    queries, keys, values, first_t = front(xm, xo, own, got, qkv, qkv_other, scale * LOG2E, ())
    cm, co = shift_in(after(cot_rows, queries), cot_got, clips, counts, core_row)
    attm, exactm, lsem = attend(core_row, after(queries, cm), keys, values, labels, bias_own, bias_got, 0)
    late_got, attm = joint((late_got, attm), ())
    late = gather_join(late, middle[-1], late_got)
    late_got = swap(late, "shard", last)
    atto, exacto, lseo = attend(core_row, after(queries, late), keys, values, labels, bias_own, bias_got, 1)
    early_got, late_got, atto, co = joint((early_got, late_got, atto, co), ())
    early = gather_join(early, last, early_got)
    early = early.reshape(-1, early.shape[-1])
    early_other = swap(early, "tensor")
    mid, second, act, slope = middle_forward(xm, xo, attm, atto, own, got, early, early_other)
    late = gather_join(late, last, late_got)
    late = late.reshape(-1, late.shape[-1])
    late_other = swap(late, "tensor")
    *block_pieces, grad_mid, grad_att, one_mine, one_other, two_mine, two_other, small_mid, small_wide = middle_back(cm, co, mid, second, act, slope, attm, atto, own, got, early, early_other, late, late_other, ())

    order = order[::-1]
    twice = bits_of("ctx") == 1
    args = (core_row, queries, keys, values, labels, bias_own, bias_got)
    block_parts = leave_start(block_pieces, clips)
    one_got, two_got = swap(one_other, "tensor"), swap(two_other, "tensor")
    qo, ko, vo, pair_o, sent_o = attend_back(*args, exacto, lseo, grad_att, scale, 1)
    one_got, two_got, qo, sent_o, *moved = joint((one_got, two_got, qo, sent_o) + tuple(block_parts[1:]), ())
    block_parts = (block_parts[0],) + tuple(moved)
    one, two = split_rows(add_rounded(one_mine, one_got)), split_rows(add_rounded(two_mine, two_got))
    one_got = scatter_send(one, order[:1])[1]
    two_got = ctx_split_send(two) if twice else scatter_send(two, order[:1])[1]
    side = side_grads(first_t, (qo, ko, vo))
    side_got, sent_o = swap(side, "tensor"), swap(sent_o, "tensor")
    qm, km, vm, pair_m, sent_m = attend_back(*args, exactm, lsem, after(grad_att, side), scale, 0)
    one_got, two_got, side, sent_o, qm, sent_m = joint((one_got, two_got, side_got, sent_o, qm, sent_m), ())
    one = scatter_add(one, order[0], one_got)
    two = ctx_split_add(two, two_got) if twice else scatter_add(two, order[0], two_got)
    one_got = scatter_send(one, order[1:2])[1]
    two_bits = order if twice else order[1:]
    two_got = scatter_send(two, two_bits[:1])[1]
    sent_m = swap(sent_m, "tensor")
    *grad_pieces, qkv_grads, small_end = back(xm, xo, first_t, (after(qm, one, two), km, vm), (qo, ko, vo), grad_mid, own, got, qkv, qkv_other, side)
    block_out = leave_end(block_parts, clips, counts, core_row, small_end)
    one_got, two_got, sent_m, block_out = joint((one_got, two_got, sent_m, block_out), ())
    one = scatter_add(one, order[1], one_got)
    two = scatter_add(two, two_bits[0], two_got)
    qkv_grads = split_rows(qkv_grads)
    qkv_got = scatter_send(qkv_grads, order[:1])[1]
    grad_parts = leave_start(grad_pieces, clips)
    two_got = scatter_send(two, two_bits[1:2])[1]
    one, one_got = scatter_send(one, order[2:])
    pairs = (pair_m, pair_o, sent_m, sent_o)
    (folded,) = fold(core_row, after(index, one, two), pairs, heads, 0, cut)
    qkv_got, two_got, one_got, folded, *moved = joint((qkv_got, two_got, one_got, folded) + tuple(grad_parts[1:]), ())
    grad_parts = (grad_parts[0],) + tuple(moved)
    qkv_grads = scatter_add(qkv_grads, order[0], qkv_got)
    two = scatter_add(two, two_bits[1], two_got)
    one = scatter_add(one, order[-1], one_got)
    qkv_got = scatter_send(qkv_grads, order[1:2])[1]
    two, two_got = scatter_send(two, two_bits[2:])
    one, one_got = ctx_send(one)
    fold_mine, fold_other = fold(core_row, after(index, one, two, qkv_grads), pairs, heads, cut, block - cut, (folded, small_mid, small_wide, small_end))
    qkv_got, two_got, one_got, fold_mine, fold_other = joint((qkv_got, two_got, one_got, fold_mine, fold_other), ())
    small = fold_mine + swap(fold_other, "tensor")
    qkv_grads = scatter_add(qkv_grads, order[1], qkv_got)
    qkv_grads, qkv_got = scatter_send(qkv_grads, order[2:])
    two = scatter_add(two, two_bits[-1], two_got)
    two, two_got = (two, swap(two, "ctx")) if twice else ctx_send(two)
    groups = joint_groups()
    for group in groups[:-2]:
        small = add_parts(joint_parts(small, group))
    parts = joint_parts(small, groups[-2])
    grad_input = leave_end(grad_parts, clips, counts, core_row, small)
    *parts, grad_input = joint(tuple(parts) + (grad_input,), ())
    small = add_parts(parts)
    parts = joint_parts(small, groups[-1])
    qkv_got, two_got, one_got = joint((qkv_got, two_got, one_got), (small,))
    qkv_grads = scatter_add(qkv_grads, order[-1], qkv_got)
    qkv_grads, qkv_got = ctx_send(qkv_grads)
    one = ctx_add(one, one_got)
    two = flat(ordered(bit_on("ctx", 0) == 1, two, two_got, two.ndim - 2)).astype(F32) if twice else ctx_add(two, two_got)
    qkv_grads = ctx_add(qkv_grads, qkv_got)
    d_gain1, d_shift1, d_bqv, d_bp, d_table, d_gain2, d_shift2, d_b1, d_b2 = unpack(parts, heads)
    rows = w_fc1.shape[0]
    return (
        block_out.reshape(clip_input.shape),
        grad_input.reshape(clip_input.shape),
        d_gain1,
        d_shift1,
        qkv_grads.reshape(rows, 3, half_width).transpose(1, 0, 2),
        d_bqv,
        two[:, :half_width].T,
        d_bp,
        d_table,
        d_gain2,
        d_shift2,
        one,
        d_b1,
        two[:, half_width:].T,
        d_b2,
    )


def solution(mesh):
    in_specs = (
        P("shard", "ctx", None, "tensor"),
        P("shard", "ctx", None, "tensor"),
        P("tensor"),
        P("tensor"),
        P(None, "shard", "tensor"),
        P(None, "tensor"),
        P("tensor", "shard"),
        P("tensor"),
        P("tensor", None),
        P("tensor"),
        P("tensor"),
        P("shard", "tensor"),
        P("tensor"),
        P("tensor", "shard"),
        P("tensor"),
        P(),
        P("ctx", None),
    )
    out_specs = (
        P("shard", "ctx", None, "tensor"),
        P("shard", "ctx", None, "tensor"),
        P("tensor"),
        P("tensor"),
        P(None, "shard", "tensor"),
        P(None, "tensor"),
        P("tensor", "shard"),
        P("tensor"),
        P("tensor", None),
        P("tensor"),
        P("tensor"),
        P("shard", "tensor"),
        P("tensor"),
        P("tensor", "shard"),
        P("tensor"),
    )
    return jax.shard_map(
        on_device, mesh=mesh, in_specs=in_specs, out_specs=out_specs, check_vma=False
    )
```

```python
import functools

import jax
import jax.numpy as jnp
import numpy as np
from jax import lax
from jax.experimental import pallas as pl
from jax.experimental.pallas import tpu as pltpu
from jax.sharding import PartitionSpec as P

BF = jnp.bfloat16
F32 = jnp.float32
HD = 32
WT, WH, WW = 8, 7, 7
WTOK = WT * WH * WW
TOKS = 400
LANES = 512
HALF_ROWS = 208
TABLE = 2535
COARSE = 10
FINE = 256
ROWS = 16
GROUP = 4
EPSILON = 1e-05
HELD = WTOK // 2
SENT_IN = 200
SENT_OUT = 208
LOG2E = 1.4426950408889634
VECTOR_ROWS = 96
GAIN1, SHIFT1, BIAS_Q, BIAS_V, BIAS_P, GAIN2, SHIFT2, BIAS2, BIAS1 = range(80, 89)
ANY = pl.BlockSpec(memory_space=pl.ANY)


def dot(a, b, ca, cb):
    return lax.dot_general(a, b, (((ca,), (cb,)), ((), ())), preferred_element_type=F32)


def cost(flops, moved, trans=0):
    return pl.CostEstimate(flops=1, bytes_accessed=1, transcendentals=0)


def params(size=56):
    return pltpu.CompilerParams(vmem_limit_bytes=size * 1024 * 1024)


def whole_spec(array):
    rank = len(array.shape)
    return pl.BlockSpec(array.shape, lambda *_: (0,) * rank)


def window_spec(array, skip=0):
    rank = len(array.shape)
    return pl.BlockSpec((1,) + array.shape[1:], lambda w, *_: (w + skip,) + (0,) * (rank - 1))


def flip(values, axis=1):
    half = values.shape[axis] // 2
    low = lax.slice_in_dim(values, 0, half, axis=axis)
    high = lax.slice_in_dim(values, half, 2 * half, axis=axis)
    return jnp.concatenate([high, low], axis)


def row_pair(own_ref, got_ref, row, count=1):
    return jnp.concatenate([ref[r : r + 1, :] for ref in (own_ref, got_ref) for r in range(row, row + count)], 1)


def normed(values):
    width = values.shape[1]
    center = jnp.sum(values, 1, keepdims=True) / width
    spread = jnp.sum(values * values, 1, keepdims=True) / width - center * center
    inv = lax.rsqrt(spread + EPSILON)
    return (values - center) * inv, inv


def norm_back(upstream, xhat, inv, gain):
    width = xhat.shape[1]
    scaled = upstream * gain
    total = jnp.sum(scaled, 1, keepdims=True) / width
    along = jnp.sum(scaled * xhat, 1, keepdims=True) / width
    return inv * (scaled - total - xhat * along)


def pack_kernel(gain1, shift1, bqv, bp, gain2, shift2, b2, b1, table, out_ref):
    out_ref[...] = jnp.zeros_like(out_ref)
    heads = table.shape[0]
    for c in range(COARSE):
        size = min(FINE, TABLE - c * FINE)
        out_ref[c * heads : (c + 1) * heads, :size] = table[:, c * FINE : c * FINE + size]
    rows = ((GAIN1, gain1), (SHIFT1, shift1), (BIAS_P, bp), (GAIN2, gain2), (SHIFT2, shift2), (BIAS2, b2))
    for row, ref in rows:
        out_ref[row : row + 1, :] = ref[...].reshape(1, -1)
    out_ref[BIAS_Q : BIAS_Q + 2, :] = bqv[...]
    wide = b1[...].reshape(1, -1)
    for i in range(4):
        out_ref[BIAS1 + i : BIAS1 + i + 1, :] = wide[:, i * 256 : (i + 1) * 256]


def pack(*arrays):
    return pl.pallas_call(
        pack_kernel,
        out_shape=jax.ShapeDtypeStruct((VECTOR_ROWS, FINE), F32),
        cost_estimate=cost(1000, 200000),
        name="pack",
    )(*arrays)


def unpack_kernel(a_ref, b_ref, c_ref, d_ref, gain1, shift1, bqv, bp, table, gain2, shift2, b1, b2):
    a, b, c, d = [ref[...].astype(F32) for ref in (a_ref, b_ref, c_ref, d_ref)]
    total = (a + b) + (c + d)
    heads = table.shape[0]
    for c in range(COARSE):
        size = min(FINE, TABLE - c * FINE)
        table[:, c * FINE : c * FINE + size] = total[c * heads : (c + 1) * heads, :size]
    rows = ((GAIN1, gain1), (SHIFT1, shift1), (BIAS_P, bp), (GAIN2, gain2), (SHIFT2, shift2), (BIAS2, b2))
    for row, ref in rows:
        ref[...] = total[row : row + 1].reshape(-1)
    bqv[...] = total[BIAS_Q : BIAS_Q + 2]
    b1[...] = jnp.concatenate([total[BIAS1 + i : BIAS1 + i + 1] for i in range(4)], 1).reshape(-1)


def unpack(parts, heads):
    vector = jax.ShapeDtypeStruct((FINE,), F32)
    return pl.pallas_call(
        unpack_kernel,
        out_shape=[vector, vector, jax.ShapeDtypeStruct((2, FINE), F32), vector, jax.ShapeDtypeStruct((heads, TABLE), F32), vector, vector, jax.ShapeDtypeStruct((4 * FINE,), F32), vector],
        cost_estimate=cost(1000, 200000),
        name="unpack",
    )(*parts)


def lane_tiles(width):
    return [(t, t * 128, min(128, width - t * 128)) for t in range(-(-width // 128))]


def put_rows(scratch, start, rows):
    for t, begin, size in lane_tiles(rows.shape[1]):
        scratch[t, start : start + rows.shape[0], :size] = rows[:, begin : begin + size]


def strided_rows(scratch, start, count, step, width):
    parts = [scratch[t, pl.ds(start, count, stride=step), :][:, :size] for t, _, size in lane_tiles(width)]
    return jnp.concatenate(parts, 1)


def one_hot(fine_row, width):
    rows = lax.broadcasted_iota(jnp.int32, (FINE, width), 0).astype(jnp.int16)
    return jnp.where(rows == fine_row.astype(jnp.int16), jnp.ones((), BF), jnp.zeros((), BF))


def lookup_kernel(heads, idx_ref, own_ref, got_ref, *rest):
    out_ref, scratch, table = rest[-3:]
    width = idx_ref.shape[1]

    @pl.when(pl.program_id(0) == 0)
    def _():
        for c in range(COARSE):
            span = slice(c * heads, (c + 1) * heads)
            level_rows = jnp.concatenate([own_ref[span, :], got_ref[span, :]], 0)
            table[2 * c * heads : 2 * (c + 1) * heads, :] = (level_rows * LOG2E).astype(BF)

    for r in range(ROWS):
        idx = idx_ref[r : r + 1, :]
        hot = one_hot(jnp.bitwise_and(idx, FINE - 1), width)
        level = lax.shift_right_logical(idx, 8)
        picked = dot(table[...], hot, 1, 0)
        acc = picked[: 2 * heads]
        for c in range(1, COARSE):
            acc = jnp.where(level == c, picked[2 * c * heads : 2 * (c + 1) * heads], acc)
        put_rows(scratch, 2 * r * heads, acc)
    for h in range(2 * heads):
        out_ref[h, :, :width] = strided_rows(scratch, h, ROWS, 2 * heads, width).astype(BF)


def lookup(idx, own, got, heads, start, count, filled=()):
    width = idx.shape[1]
    return pl.pallas_call(
        functools.partial(lookup_kernel, heads),
        grid=(count,),
        in_specs=[pl.BlockSpec((ROWS, width), lambda i: (start + i, 0)), whole_spec(own), whole_spec(got)] + [ANY] * len(filled),
        out_specs=pl.BlockSpec((2 * heads, ROWS, LANES), lambda i: (0, start + i, 0)),
        out_shape=jax.ShapeDtypeStruct((2 * heads, HALF_ROWS, LANES), BF),
        input_output_aliases={3: 0} if filled else {},
        scratch_shapes=[pltpu.VMEM((-(-width // 128), 2 * ROWS * heads, 128), F32), pltpu.VMEM((2 * COARSE * heads, FINE), BF)],
        compiler_params=params(),
        cost_estimate=cost(0, 0),
        name="table_lookup",
    )(idx, own, got, *filled)


def fold_rows(heads, idx_ref, pair_m, pair_o, sent_m, sent_o, scratch, total):
    width = idx_ref.shape[1]
    for h in range(heads):
        put_rows(scratch, h * ROWS, pair_m[h, :, :width].astype(F32) + sent_o[h, :, :width].astype(F32))
        put_rows(scratch, (heads + h) * ROWS, pair_o[h, :, :width].astype(F32) + sent_m[h, :, :width].astype(F32))
    part = jnp.zeros(total.shape, F32)
    fine = jnp.bitwise_and(idx_ref[...], FINE - 1).T.astype(jnp.int16)
    cells = lax.broadcasted_iota(jnp.int32, (width, FINE), 1).astype(jnp.int16)
    for r in range(ROWS):
        hot = jnp.where(cells == fine[:, r : r + 1], jnp.ones((), BF), jnp.zeros((), BF))
        level = lax.shift_right_logical(idx_ref[r : r + 1, :], 8)
        grads = strided_rows(scratch, r, 2 * heads, ROWS, width)
        parts = [jnp.where(level == c, grads, 0.0) for c in range(COARSE)]
        part = part + dot(jnp.concatenate(parts, 0).astype(BF), hot, 1, 0)
    total[...] += part


def fold_start_kernel(heads, core_ref, idx_ref, pair_m, pair_o, sent_m, sent_o, total, scratch):
    step = pl.program_id(0)

    @pl.when(step == 0)
    def _():
        total[...] = jnp.zeros_like(total)

    @pl.when(jnp.logical_or(step > 0, core_ref[0] == 0))
    def _():
        fold_rows(heads, idx_ref, pair_m, pair_o, sent_m, sent_o, scratch, total)


def fold_end_kernel(heads, core_ref, idx_ref, pair_m, pair_o, sent_m, sent_o, init_ref, mid_ref, wide_ref, end_ref, mine_ref, other_ref, scratch, total):
    step = pl.program_id(0)

    @pl.when(step == 0)
    def _():
        total[...] = init_ref[...]

    fold_rows(heads, idx_ref, pair_m, pair_o, sent_m, sent_o, scratch, total)

    @pl.when(step == pl.num_programs(0) - 1)
    def _():
        for half, ref in enumerate((mine_ref, other_ref)):
            for c in range(COARSE):
                at = (2 * c + half) * heads
                ref[c * heads : (c + 1) * heads, :] = total[at : at + heads, :]
            span = slice(half * 256, (half + 1) * 256)
            rows = ((GAIN1, end_ref, 2), (SHIFT1, end_ref, 3), (BIAS_Q, end_ref, 0), (BIAS_V, end_ref, 1), (BIAS_P, mid_ref, 3), (GAIN2, mid_ref, 1), (SHIFT2, mid_ref, 2), (BIAS2, mid_ref, 0))
            for row, source, at in rows:
                ref[row : row + 1, :] = source[at : at + 1, span]
            for i in range(4):
                at = half * 1024 + i * 256
                ref[BIAS1 + i : BIAS1 + i + 1, :] = wide_ref[:, at : at + 256]
            ref[BIAS1 + 4 :, :] = jnp.zeros((VECTOR_ROWS - BIAS1 - 4, 256), F32)


def fold(core, idx, pairs, heads, start, count, extra=()):
    width = idx.shape[1]
    scratch = [pltpu.VMEM((-(-width // 128), 2 * ROWS * heads, 128), F32)]
    total = jax.ShapeDtypeStruct((2 * COARSE * heads, FINE), F32)
    ends = jax.ShapeDtypeStruct((VECTOR_ROWS, FINE), F32)
    outs = [ends, ends] if extra else [total]
    pair = pl.BlockSpec((heads, ROWS, LANES), lambda i, core: (0, start + i, 0))
    return pl.pallas_call(
        functools.partial(fold_end_kernel if extra else fold_start_kernel, heads),
        grid_spec=pltpu.PrefetchScalarGridSpec(
            num_scalar_prefetch=1,
            grid=(count,),
            in_specs=[pl.BlockSpec((ROWS, width), lambda i, core: (start + i, 0))] + [pair] * 4 + [whole_spec(e) for e in extra],
            out_specs=[whole_spec(o) for o in outs],
            scratch_shapes=scratch + ([pltpu.VMEM(total.shape, F32)] if extra else []),
        ),
        out_shape=outs,
        compiler_params=params(),
        cost_estimate=cost(0, 0),
        name="table_fold",
    )(core, idx, *pairs, *extra)


def mask_pieces():
    pieces = []
    rest = np.float32(-100.0 * LOG2E)
    for _ in range(3):
        piece = np.float32(rest.astype(jnp.bfloat16))
        pieces.append(float(piece))
        rest = np.float32(rest - piece)
    return pieces


def region_rows(label):
    width = label.shape[1]
    rows = lax.broadcasted_iota(jnp.int32, (16, width), 0)
    lanes = lax.broadcasted_iota(jnp.int32, (16, width), 1)
    same = jnp.bitwise_and(rows, 3) == label
    level = lax.shift_right_logical(rows, 2)
    high, mid, low = mask_pieces()
    piece = jnp.where(level == 0, high, jnp.where(level == 1, mid, low))
    queries = jnp.where(rows < 12, jnp.where(same, 1.0, 0.0), jnp.where(rows == 15, 1.0, 0.0))
    past = jnp.where(jnp.logical_and(rows == 15, lanes >= WTOK), -1e30, 0.0)
    keys = jnp.where(rows < 12, jnp.where(same, 0.0, piece), past)
    return queries.astype(BF), keys.astype(BF)


def pick_bias(first, own_ref, got_ref, j):
    skip = 2 * HALF_ROWS - TOKS
    low = lax.select_n(first, got_ref[j, :, :TOKS], own_ref[j, :, :TOKS])
    high = lax.select_n(first, own_ref[j, skip:, :TOKS], got_ref[j, skip:, :TOKS])
    return jnp.concatenate([low, high], 0).astype(F32)


def attend_kernel(core_ref, q_ref, k_ref, v_ref, label_ref, own_ref, got_ref, att_ref, exact_ref, lse_ref):
    first = core_ref[0] == 0
    ones = jnp.ones((16, TOKS), BF)
    windows = range(q_ref.shape[0])
    regions = [region_rows(label_ref[w]) for w in windows]
    for j in range(GROUP):
        part = pl.ds(j * HD, HD)
        bias = pick_bias(first, own_ref, got_ref, j)
        for w in windows:
            query_rows, key_rows = regions[w]
            qa = jnp.concatenate([q_ref[w, part, :], query_rows], 0)
            ka = jnp.concatenate([k_ref[w, part, :], key_rows], 0)
            va = jnp.concatenate([v_ref[w, part, :], ones], 0)
            scores = dot(ka, qa, 0, 0) + bias
            peak = jnp.max(scores, 0, keepdims=True)
            weights = jnp.exp2(scores - peak).astype(BF)
            mixed = dot(va, weights, 1, 0)
            total = mixed[HD : HD + 1]
            out = mixed[:HD] / total
            att_ref[w, part, :] = out.astype(BF)
            exact_ref[w, part, :] = out
            lse_ref[w, 0, j : j + 1, :] = peak + jnp.log2(total)


def attention_specs(wins, heads, skip=0):
    half = heads // (2 * GROUP)
    feat = pl.BlockSpec((wins, GROUP * HD, TOKS), lambda h, core: (0, h + skip, 0))
    label = pl.BlockSpec((wins, 1, TOKS), lambda h, core: (0, 0, 0))
    own = pl.BlockSpec((GROUP, HALF_ROWS, LANES), lambda h, core: (h + skip, 0, 0))
    got = pl.BlockSpec((GROUP, HALF_ROWS, LANES), lambda h, core: ((h + skip + half) % (2 * half), 0, 0))
    stat = pl.BlockSpec((wins, 1, GROUP, TOKS), lambda h, core: (0, h + skip, 0, 0))
    return feat, label, own, got, stat


def attend(core, q, k, v, labels, own, got):
    wins, feats, toks = q.shape
    heads = feats // HD
    feat, label, own_spec, got_spec, stat = attention_specs(wins, heads)
    return pl.pallas_call(
        attend_kernel,
        grid_spec=pltpu.PrefetchScalarGridSpec(
            num_scalar_prefetch=1,
            grid=(heads // GROUP,),
            in_specs=[feat, feat, feat, label, own_spec, got_spec],
            out_specs=[feat, feat, stat],
        ),
        out_shape=[
            jax.ShapeDtypeStruct(q.shape, BF),
            jax.ShapeDtypeStruct(q.shape, F32),
            jax.ShapeDtypeStruct((wins, heads // GROUP, GROUP, toks), F32),
        ],
        compiler_params=params(),
        cost_estimate=cost(0, 0),
        name="attend",
    )(core, q, k, v, labels, own, got)


def split3(row):
    hi = row.astype(BF)
    rest = row - hi.astype(F32)
    mid = rest.astype(BF)
    return hi.astype(F32), mid.astype(F32), rest - mid.astype(F32)


def rows16(parts, width):
    rows = lax.broadcasted_iota(jnp.int32, (16, width), 0)
    out = jnp.zeros((16, width), F32)
    for i, part in enumerate(parts):
        out = jnp.where(rows == i, part, out)
    return out.astype(BF)


def attend_back_kernel(scale, core_ref, q_ref, k_ref, v_ref, label_ref, own_ref, got_ref, exact_ref, lse_ref, g_ref, dq_ref, dk_ref, dv_ref, pair_ref, sent_ref, sums):
    core = core_ref[0]
    first = core == 0
    step = TOKS - HALF_ROWS
    mine, other = pl.multiple_of(core * step, 8), pl.multiple_of((1 - core) * step, 8)
    minus = rows16([-1.0, -1.0, -1.0], TOKS)
    windows = range(q_ref.shape[0])
    regions = [region_rows(label_ref[w]) for w in windows]
    for j in range(GROUP):
        part = pl.ds(j * HD, HD)
        bias = pick_bias(first, own_ref, got_ref, j)
        total = None
        for w in windows:
            query_rows, key_rows = regions[w]
            q = q_ref[w, part, :]
            k = k_ref[w, part, :]
            g = g_ref[w, part, :]
            qa = jnp.concatenate([q, query_rows, rows16(split3(lse_ref[w, 0, j : j + 1, :]), TOKS)], 0)
            ka = jnp.concatenate([k, key_rows, minus], 0)
            va = jnp.concatenate([v_ref[w, part, :], minus], 0)
            along = jnp.sum(g.astype(F32) * exact_ref[w, part, :], 0, keepdims=True)
            ga = jnp.concatenate([g, rows16(split3(along), TOKS)], 0)
            probs = jnp.exp2(dot(ka, qa, 0, 0) + bias)
            wide = probs * dot(va, ga, 0, 0)
            grads = wide.astype(BF)
            low = probs.astype(BF)
            dv_ref[w, part, :] = dot(g, low, 1, 1).astype(BF)
            dk_ref[w, part, :] = (dot(q, grads, 1, 1) * (1.0 / LOG2E)).astype(BF)
            dq_ref[w, part, :] = (dot(k, grads, 1, 0) * scale).astype(BF)
            total = wide if total is None else total + wide
        sums[...] = total
        pair_ref[j, :, :TOKS] = sums[pl.ds(mine, HALF_ROWS), :].astype(BF)
        sent_ref[j, :, :TOKS] = sums[pl.ds(other, HALF_ROWS), :].astype(BF)


def attend_back(core, q, k, v, labels, own, got, exact, lse, g, scale, side):
    wins, feats, toks = q.shape
    heads = feats // HD
    blocks = heads // (2 * GROUP)
    feat, label, own_spec, got_spec, stat = attention_specs(wins, heads, side * blocks)
    out = pl.BlockSpec((wins, GROUP * HD, toks), lambda h, core: (0, h, 0))
    pair = pl.BlockSpec((GROUP, HALF_ROWS, LANES), lambda h, core: (h, 0, 0))
    return pl.pallas_call(
        functools.partial(attend_back_kernel, scale),
        grid_spec=pltpu.PrefetchScalarGridSpec(
            num_scalar_prefetch=1,
            grid=(blocks,),
            in_specs=[feat, feat, feat, label, own_spec, got_spec, feat, stat, feat],
            out_specs=[out, out, out, pair, pair],
            scratch_shapes=[pltpu.VMEM((toks, toks), F32)],
        ),
        out_shape=[jax.ShapeDtypeStruct((wins, feats // 2, toks), BF)] * 3 + [jax.ShapeDtypeStruct((heads // 2, HALF_ROWS, LANES), BF)] * 2,
        compiler_params=params(),
        cost_estimate=cost(0, 0),
        name="attend_back",
    )(core, q, k, v, labels, own, got, exact, lse, g)


def front_kernel(scale, xm_ref, xo_ref, own_ref, got_ref, wm_ref, wo_ref, *rest):
    q_ref, k_ref, v_ref, first_ref = rest[-4:]
    x = jnp.concatenate([xm_ref[0], xo_ref[0]], 1).astype(F32)
    xhat, _ = normed(x)
    first = (xhat * row_pair(own_ref, got_ref, GAIN1) + row_pair(own_ref, got_ref, SHIFT1)).astype(BF)
    first_ref[0] = first.T
    for t, (w_ref, vec_ref) in enumerate(((wm_ref, own_ref), (wo_ref, got_ref))):
        cols = w_ref.shape[1] // 3
        rows = pl.ds(t * cols, cols)
        made = dot(first if t == 0 else flip(first), w_ref[...], 1, 0)
        q = (made[:, :cols] + vec_ref[BIAS_Q : BIAS_Q + 1, :]) * scale
        v = made[:, 2 * cols :] + vec_ref[BIAS_V : BIAS_V + 1, :]
        q_ref[0, rows, :] = q.astype(BF).T
        k_ref[0, rows, :] = made[:, cols : 2 * cols].astype(BF).T
        v_ref[0, rows, :] = v.astype(BF).T


def front(xm, xo, own, got, wm, wo, scale, deps):
    wins, toks, half = xm.shape
    out = jax.ShapeDtypeStruct((wins, 2 * (wm.shape[1] // 3), toks), BF)
    return pl.pallas_call(
        functools.partial(front_kernel, scale),
        grid=(wins,),
        in_specs=[window_spec(xm), window_spec(xo), whole_spec(own), whole_spec(got), whole_spec(wm), whole_spec(wo)] + [ANY] * len(deps),
        out_specs=[window_spec(out)] * 4,
        out_shape=[out] * 4,
        compiler_params=params(),
        cost_estimate=cost(8 * wins * toks * half * wm.shape[1], wins * toks * half * 16 + wm.size * 4),
        name="front",
    )(xm, xo, own, got, wm, wo, *deps)


def middle_kernel(xm_ref, xo_ref, att_ref, own_ref, got_ref, wm_ref, wo_ref, *rest):
    mid_ref, second_ref, act_ref, slope_ref = rest[-4:]
    half = xm_ref.shape[2]
    wide = wm_ref.shape[1] - half
    branch = dot(att_ref[0, :half, :].T, wm_ref[:, :half], 1, 1) + flip(dot(att_ref[0, half:, :].T, wo_ref[:, :half], 1, 1))
    x = jnp.concatenate([xm_ref[0], xo_ref[0]], 1).astype(F32)
    middle = x + (branch + row_pair(own_ref, got_ref, BIAS_P))
    mid_ref[0] = middle
    xhat, _ = normed(middle)
    second = (xhat * row_pair(own_ref, got_ref, GAIN2) + row_pair(own_ref, got_ref, SHIFT2)).astype(BF)
    second_ref[0] = second
    turned = flip(second)
    for t, (w_ref, vec_ref) in enumerate(((wm_ref, own_ref), (wo_ref, got_ref))):
        for s in range(0, wide, 256):
            at = t * wide + s
            bias = vec_ref[BIAS1 + s // 256 : BIAS1 + s // 256 + 1, :]
            hidden = dot(second if t == 0 else turned, w_ref[:, half + s : half + s + 256], 1, 0) + bias
            phi = 0.5 + 0.5 * lax.erf(hidden * (0.5**0.5))
            bell = jnp.exp2(hidden * hidden * (-0.5 * LOG2E)) * (1.0 / (2.0 * np.pi) ** 0.5)
            act_ref[0, :, at : at + 256] = (hidden * phi).astype(BF)
            slope_ref[0, :, at : at + 256] = (phi + hidden * bell).astype(BF)


def middle_forward(xm, xo, att, own, got, wm, wo):
    wins, toks, half = xm.shape
    width = 2 * half
    hidden = 2 * (wm.shape[1] - half)
    wide = jax.ShapeDtypeStruct((wins, toks, hidden), BF)
    outs = [jax.ShapeDtypeStruct((wins, toks, width), F32), jax.ShapeDtypeStruct((wins, toks, width), BF), wide, wide]
    fixed = (own, got, wm, wo)
    return pl.pallas_call(
        middle_kernel,
        grid=(wins,),
        in_specs=[window_spec(a) for a in (xm, xo, att)] + [whole_spec(a) for a in fixed],
        out_specs=[window_spec(o) for o in outs],
        out_shape=outs,
        compiler_params=params(28),
        cost_estimate=cost(8 * wins * toks * width * wm.shape[1], wins * toks * (width * 10 + hidden * 4) + wm.size * 4, wins * toks * hidden),
        name="middle_forward",
    )(xm, xo, att, *fixed)


def put_pieces(out, nearm_ref, nearo_ref, farm_ref, faro_ref):
    half = out.shape[1] // 2
    for ref, rows, cols in ((nearm_ref, 0, 0), (nearo_ref, 0, half), (farm_ref, TOKS - SENT_OUT, 0), (faro_ref, TOKS - SENT_OUT, half)):
        ref[0] = out[rows : rows + SENT_OUT, cols : cols + half]


def middle_back_kernel(cm_ref, co_ref, mid_ref, second_ref, act_ref, slope_ref, att_ref, own_ref, got_ref, wm_ref, wo_ref, fm_ref, fo_ref, *rest):
    nearm_ref, nearo_ref, farm_ref, faro_ref, gm_ref, gr_ref, onem_ref, oneo_ref, twom_ref, twoo_ref, small_ref, wide_ref, accm, acco = rest[-14:]
    win = pl.program_id(0)
    half = cm_ref.shape[2]
    wide = fm_ref.shape[1]

    @pl.when(win == 0)
    def _():
        accm[...] = jnp.zeros_like(accm)
        acco[...] = jnp.zeros_like(acco)
        small_ref[...] = jnp.zeros_like(small_ref)
        wide_ref[...] = jnp.zeros_like(wide_ref)

    cot = jnp.concatenate([cm_ref[0], co_ref[0]], 1)
    cot_turned = flip(cot)
    cot_t = cot.T
    second_t = second_ref[0].T
    sides = (
        (wm_ref, fm_ref, accm, cot, cot_t, second_t),
        (wo_ref, fo_ref, acco, cot_turned, flip(cot_t, 0), flip(second_t, 0)),
    )
    made, pulled = [], []
    for t, (w_ref, f_ref, acc, c, c_t, s_t) in enumerate(sides):
        forward = jnp.zeros(cot.shape, F32)
        grad_second = jnp.zeros(cot.shape, F32)
        for s in range(0, wide, 512):
            span = slice(t * wide + s, t * wide + s + 512)
            fc2 = f_ref[:, s : s + 512]
            active = act_ref[0, :, span]
            forward = forward + dot(active, fc2, 1, 1)
            grad = (dot(c, fc2, 1, 0) * slope_ref[0, :, span].astype(F32)).astype(BF)
            wide_ref[:, span] += jnp.sum(grad.astype(F32), 0, keepdims=True)
            acc[:, half + wide + s : half + wide + s + 512] += dot(c_t, active, 1, 0)
            acc[:, half + s : half + s + 512] += dot(s_t, grad, 1, 0)
            grad_second = grad_second + dot(grad, w_ref[:, half + s : half + s + 512], 1, 1)
        made.append(forward)
        pulled.append(grad_second)
    out = mid_ref[0] + (made[0] + flip(made[1]) + row_pair(own_ref, got_ref, BIAS2))
    put_pieces(out.astype(BF), nearm_ref, nearo_ref, farm_ref, faro_ref)
    grad_second = pulled[0] + flip(pulled[1])
    upstream = cot.astype(F32)
    xhat, inv = normed(mid_ref[0])
    grad_mid = upstream + norm_back(grad_second, xhat, inv, row_pair(own_ref, got_ref, GAIN2))
    gm_ref[0] = grad_mid
    branch = grad_mid.astype(BF)
    branch_t = branch.T
    gr_ref[0, :half, :] = dot(branch, wm_ref[:, :half], 1, 0).astype(BF).T
    gr_ref[0, half:, :] = dot(flip(branch), wo_ref[:, :half], 1, 0).astype(BF).T
    accm[:, :half] += dot(branch_t, att_ref[0, :half, :], 1, 1)
    acco[:, :half] += dot(flip(branch_t, 0), att_ref[0, half:, :], 1, 1)
    small_ref[0:1, :] += jnp.sum(upstream, 0, keepdims=True)
    small_ref[1:2, :] += jnp.sum(grad_second * xhat, 0, keepdims=True)
    small_ref[2:3, :] += jnp.sum(grad_second, 0, keepdims=True)
    small_ref[3:4, :] += jnp.sum(branch.astype(F32), 0, keepdims=True)

    @pl.when(win == pl.num_programs(0) - 1)
    def _():
        for acc, one_ref, two_ref in ((accm, onem_ref, twom_ref), (acco, oneo_ref, twoo_ref)):
            one_ref[...] = acc[:, half : half + wide].astype(BF)
            two_ref[:, :half] = acc[:, :half].astype(BF)
            two_ref[:, half:] = acc[:, half + wide :].astype(BF)


def middle_back(cm, co, mid, second, act, slope, att, own, got, wm, wo, fm, fo, deps):
    wins, toks, half = cm.shape
    width = 2 * half
    hidden = act.shape[2]
    windows = (cm, co, mid, second, act, slope, att)
    fixed = (own, got, wm, wo, fm, fo)
    plain = jax.ShapeDtypeStruct((wins, SENT_OUT, half), BF)
    outs = [plain, plain, plain, plain, jax.ShapeDtypeStruct(mid.shape, F32), jax.ShapeDtypeStruct((wins, width, toks), BF)]
    grads = jax.ShapeDtypeStruct((width, wm.shape[1] + fm.shape[1]), BF)
    one = jax.ShapeDtypeStruct((width, wm.shape[1] - half), BF)
    two = jax.ShapeDtypeStruct((width, half + fm.shape[1]), BF)
    sums = [one, one, two, two, jax.ShapeDtypeStruct((4, width), F32), jax.ShapeDtypeStruct((1, hidden), F32)]
    return pl.pallas_call(
        middle_back_kernel,
        grid=(wins,),
        in_specs=[window_spec(a, wins if a is co else 0) for a in windows] + [whole_spec(a) for a in fixed] + [ANY] * len(deps),
        out_specs=[window_spec(o) for o in outs] + [whole_spec(o) for o in sums],
        out_shape=[pltpu.HBM(o.shape, o.dtype) for o in outs + sums],
        scratch_shapes=[pltpu.VMEM(grads.shape, F32), pltpu.VMEM(grads.shape, F32)],
        compiler_params=params(28),
        cost_estimate=cost(12 * wins * toks * width * (width + 2 * hidden), wins * toks * (width * 16 + hidden * 4) + fm.size * 12),
        name="middle_back",
    )(*windows, *fixed, *deps)


def side_kernel(first_ref, dq_ref, dk_ref, dv_ref, do_ref):
    for c, ref in enumerate((dq_ref, dk_ref, dv_ref)):
        cols = ref.shape[1]
        part = sum(dot(flip(first_ref[w], 0), ref[w], 1, 1) for w in range(first_ref.shape[0]))
        do_ref[:, c * cols : (c + 1) * cols] = part.astype(BF)


def side_grads(first, grads):
    wins, width, toks = first.shape
    return pl.pallas_call(
        side_kernel,
        out_shape=jax.ShapeDtypeStruct((width, 3 * grads[0].shape[1]), BF),
        compiler_params=params(),
        cost_estimate=cost(0, 0),
        name="side_grads",
    )(first, *grads)


def back_kernel(xm_ref, xo_ref, first_ref, qm_ref, km_ref, vm_ref, qo_ref, ko_ref, vo_ref, gm_ref, own_ref, got_ref, wm_ref, wo_ref, side_ref, nearm_ref, nearo_ref, farm_ref, faro_ref, dm_ref, small_ref, acc):
    win = pl.program_id(0)

    @pl.when(win == 0)
    def _():
        acc[...] = side_ref[...].astype(F32)
        small_ref[...] = jnp.zeros_like(small_ref)

    xhat, inv = normed(jnp.concatenate([xm_ref[0], xo_ref[0]], 1).astype(F32))
    half = xm_ref.shape[2]
    mine = jnp.concatenate([qm_ref[0], km_ref[0], vm_ref[0]], 0)
    other = jnp.concatenate([qo_ref[0], ko_ref[0], vo_ref[0]], 0)
    acc[...] += dot(first_ref[0], mine, 1, 1)
    grad_first = dot(mine, wm_ref[...], 0, 1) + flip(dot(other, wo_ref[...], 0, 1))
    grad_first = grad_first.astype(BF).astype(F32)
    grad_x = gm_ref[0] + norm_back(grad_first, xhat, inv, row_pair(own_ref, got_ref, GAIN1))
    put_pieces(grad_x.astype(BF), nearm_ref, nearo_ref, farm_ref, faro_ref)
    ones = jnp.ones((8, mine.shape[1]), BF)
    for t, side in enumerate((mine, other)):
        sums = dot(ones, side, 1, 1)[0:1]
        span = slice(t * half, (t + 1) * half)
        small_ref[0:1, span] += sums[:, :half]
        small_ref[1:2, span] += sums[:, 2 * half :]
    small_ref[2:3, :] += jnp.sum(grad_first * xhat, 0, keepdims=True)
    small_ref[3:4, :] += jnp.sum(grad_first, 0, keepdims=True)

    @pl.when(win == pl.num_programs(0) - 1)
    def _():
        dm_ref[...] = acc[...].astype(BF)


def back(xm, xo, first, mine, other, gm, own, got, wm, wo, side):
    wins, toks, half = xm.shape
    windows = (xm, xo, first) + mine + other + (gm,)
    fixed = (own, got, wm, wo, side)
    plain = jax.ShapeDtypeStruct((wins, SENT_OUT, half), BF)
    grads = jax.ShapeDtypeStruct(wm.shape, BF)
    small = jax.ShapeDtypeStruct((4, 2 * half), F32)
    return pl.pallas_call(
        back_kernel,
        grid=(wins,),
        in_specs=[window_spec(a) for a in windows] + [whole_spec(a) for a in fixed],
        out_specs=[window_spec(plain)] * 4 + [whole_spec(grads), whole_spec(small)],
        out_shape=[pltpu.HBM(o.shape, o.dtype) for o in (plain, plain, plain, plain, grads, small)],
        scratch_shapes=[pltpu.VMEM(wm.shape, F32)],
        compiler_params=params(),
        cost_estimate=cost(0, 0),
        name="back",
    )(*windows, *fixed)


def one_hot_rows(picks, size):
    cells = lax.broadcasted_iota(jnp.int32, (picks.shape[0], size), 1)
    return jnp.where(cells == picks, 1.0, 0.0).astype(BF)


def select_in_kernel(core_ref, picks_ref, x_ref, cot_ref, far_ref, xm_ref, cm_ref, other_ref):
    skip = WTOK - SENT_IN
    near = jnp.concatenate([jnp.concatenate([ref[w, skip:, :] for ref in (x_ref, cot_ref)], 1) for w in range(4)], 0)
    rows = far_ref.shape[0] // 2
    far = jnp.concatenate([far_ref[:rows, :], far_ref[rows:, :]], 1)
    low = dot(one_hot_rows(picks_ref[0, : 4 * SENT_IN, :], near.shape[0]), near, 1, 0)
    high = dot(one_hot_rows(picks_ref[0, 4 * SENT_IN :, :], far.shape[0]), far, 1, 0)
    places = lax.broadcasted_iota(jnp.int32, (SENT_IN - skip, 1), 0) + skip
    half = x_ref.shape[2]
    for w in range(4):
        first, last = low[w * SENT_IN : (w + 1) * SENT_IN], high[w * SENT_OUT : (w + 1) * SENT_OUT]
        over = jnp.where(places < HELD, first[skip:], last[: SENT_IN - skip])
        whole = jnp.concatenate([first[:skip], over, last[SENT_IN - skip :]], 0).astype(BF)
        if w < 2:
            xm_ref[w] = whole[:, :half]
            cm_ref[w] = whole[:, half:]
        else:
            other_ref[w - 2] = whole[:, :half]
            other_ref[w] = whole[:, half:]


def core_block(picks):
    return pl.BlockSpec((1,) + picks.shape[1:], lambda i, core: (core[0], 0, 0))


def select_in(core, picks, x, cot, far):
    out = jax.ShapeDtypeStruct((2, TOKS, x.shape[2]), BF)
    other = jax.ShapeDtypeStruct((4, TOKS, x.shape[2]), BF)
    return pl.pallas_call(
        select_in_kernel,
        grid_spec=pltpu.PrefetchScalarGridSpec(
            num_scalar_prefetch=1,
            grid=(1,),
            in_specs=[core_block(picks), whole_spec(x), whole_spec(cot), whole_spec(far)],
            out_specs=[whole_spec(out), whole_spec(out), whole_spec(other)],
        ),
        out_shape=[out, out, other],
        compiler_params=params(28),
        cost_estimate=cost(0, 0),
        name="select_in",
    )(core, picks, x, cot, far)


def select_out_kernel(core_ref, picks_ref, kept_ref, beside_ref, across_ref, corner_ref, out_ref):
    skip = WTOK - SENT_IN
    near = jnp.concatenate([kept_ref[...], beside_ref[...]], 0)
    far = jnp.concatenate([across_ref[...], corner_ref[...]], 0)
    low = dot(one_hot_rows(picks_ref[0, : 4 * SENT_IN, :], far.shape[0]), far, 1, 0)
    high = dot(one_hot_rows(picks_ref[0, 4 * SENT_IN :, :], near.shape[0]), near, 1, 0)
    rows = lax.broadcasted_iota(jnp.int32, (SENT_IN - skip, 1), 0) + skip
    for w in range(4):
        first, last = [part[w * SENT_IN : (w + 1) * SENT_IN] for part in (low, high)]
        out_ref[w, :skip, :] = first[:skip]
        out_ref[w, skip:SENT_IN, :] = jnp.where(rows < HELD, first[skip:], last[: SENT_IN - skip])
        out_ref[w, SENT_IN:, :] = last[SENT_IN - skip :]


def select_out(core, picks, arrays):
    out = jax.ShapeDtypeStruct((4, WTOK, arrays[0].shape[1]), F32)
    return pl.pallas_call(
        select_out_kernel,
        grid_spec=pltpu.PrefetchScalarGridSpec(
            num_scalar_prefetch=1,
            grid=(1,),
            in_specs=[core_block(picks)] + [whole_spec(a) for a in arrays],
            out_specs=whole_spec(out),
        ),
        out_shape=out,
        compiler_params=params(28),
        cost_estimate=cost(0, 0),
        name="select_out",
    )(core, picks, *arrays)


def bits_of(axis):
    return lax.axis_size(axis).bit_length() - 1


def bit_on(axis, bit):
    return lax.shift_right_logical(lax.axis_index(axis), bit) % 2


def swap(value, axis, bit=0):
    pairs = [(source, source ^ (1 << bit)) for source in range(lax.axis_size(axis))]
    return lax.ppermute(value, axis, pairs)


def bit_order():
    count = bits_of("shard")
    return list(range(count - 1, 0, -1)) + [0]


def row_place(bit):
    place = bit_on("shard", bit)
    if bit == bits_of("shard") - 1:
        place = jnp.bitwise_xor(place, lax.axis_index("tensor"))
    return place


def ordered(on, mine, other, axis):
    return jnp.concatenate((jnp.where(on, other, mine), jnp.where(on, mine, other)), axis)


def after(value, *deps):
    return lax.optimization_barrier((value,) + deps)[0]


def gather_start(part):
    rows, cols = part.shape
    return part.reshape((1,) * bits_of("shard") + (rows, cols))


def joint(values, deps):
    return lax.optimization_barrier(tuple(values) + tuple(deps))[: len(values)]


def gather_join(held, bit, got):
    return ordered(row_place(bit) == 1, held, got, bits_of("shard") - 1 - bit)


def gather_send(held, bits):
    for bit in bits[:-1]:
        held = gather_join(held, bit, swap(held, "shard", bit))
    return held, swap(held, "shard", bits[-1])


def choose(array, index, axis):
    return lax.dynamic_slice_in_dim(array, index, 1, axis)


def add_rounded(a, b):
    return (a.astype(F32) + b.astype(F32)).astype(BF)


def split_rows(part):
    count = bits_of("shard")
    return part.reshape((2,) * count + (part.shape[0] >> count, part.shape[1]))


def scatter_add(held, bit, got):
    axis = bits_of("shard") - 1 - bit
    return add_rounded(choose(held, row_place(bit), axis), got)


def scatter_send(held, bits):
    for bit in bits[:-1]:
        held = scatter_add(held, bit, scatter_send(held, (bit,))[1])
    axis = bits_of("shard") - 1 - bits[-1]
    return held, swap(choose(held, 1 - row_place(bits[-1]), axis), "shard", bits[-1])


def ctx_half(held, own):
    axis = held.ndim - 2
    half = held.shape[axis] // 2
    return lax.dynamic_slice_in_dim(held, own * half, half, axis)


def ctx_split_send(held):
    return swap(ctx_half(held, 1 - bit_on("ctx", 0)), "ctx")


def ctx_split_add(held, got):
    return add_rounded(ctx_half(held, bit_on("ctx", 0)), got)


def flat(held):
    return held.reshape(held.shape[-2:])


def ctx_send(held):
    held = flat(held)
    for bit in range(bits_of("ctx") - 1):
        held = add_rounded(held, swap(held, "ctx", bit))
    return held, swap(held, "ctx", bits_of("ctx") - 1)


def ctx_add(held, got):
    return held.astype(F32) + got.astype(F32)


def joint_swap(value, mask):
    size = lax.axis_size("shard") * lax.axis_size("ctx")
    return lax.ppermute(value, ("shard", "ctx"), [(i, i ^ mask) for i in range(size)])


def joint_parts(value, bits):
    value = value.astype(BF)
    low = 1 << bits[0]
    if len(bits) == 1:
        return [value, joint_swap(value, low), jnp.zeros_like(value), jnp.zeros_like(value)]
    high = 1 << bits[1]
    return [value, joint_swap(value, low), joint_swap(value, high), joint_swap(value, low | high)]


def add_parts(parts):
    a, b, c, d = [part.astype(F32) for part in parts]
    return (a + b) + (c + d)


def joint_groups():
    bits = list(range(bits_of("shard") + bits_of("ctx")))
    return [bits[i : i + 2] for i in range(0, len(bits), 2)]


def roll_axis(shaped, axis_pos, levels, backward):
    token_axis = 4 + axis_pos
    length = shaped.shape[token_axis]
    border = length - length // 2 if backward else length // 2
    before = lax.slice_in_dim(shaped, 0, border, axis=token_axis)
    after = lax.slice_in_dim(shaped, border, length, axis=token_axis)
    moving = after if backward else before
    if axis_pos < levels:
        moving = swap(moving, "ctx", levels - 1 - axis_pos)
    else:
        moving = jnp.roll(moving, 1 if backward else -1, axis=1 + axis_pos)
    return jnp.concatenate((moving, before) if backward else (after, moving), axis=token_axis)


def window_roll(windows, clips, counts, backward):
    shaped = windows.reshape((clips,) + counts + (WT, WH, WW, windows.shape[-1]))
    for axis_pos in range(3):
        shaped = roll_axis(shaped, axis_pos, bits_of("ctx"), backward)
    return shaped.reshape(windows.shape)


def frame_sources():
    source = np.zeros((4, HELD), np.int64)
    for h in range(2 * WH):
        for w in range(2 * WW):
            here = (h // WH) * 2 + w // WW
            there_h, there_w = (h + WH // 2) % (2 * WH), (w + WW // 2) % (2 * WW)
            there = (there_h // WH) * 2 + there_w // WW
            for a in range(WT // 2):
                row = (a * WH + h % WH) * WW + w % WW
                source[here, row] = there * HELD + (a * WH + there_h % WH) * WW + there_w % WW
    return source


def picks_in():
    source = frame_sources()
    there, row = source // HELD, source % HELD
    picks = np.full((4, TOKS), -1)
    picks[:, :HELD] = there * SENT_IN + row + SENT_IN - HELD
    picks[:, HELD:WTOK] = there * SENT_IN + row
    both = []
    for rows in (picks, np.concatenate((picks[2:], picks[:2]))):
        both.append(np.concatenate((rows[:, :SENT_IN].reshape(-1, 1), rows[:, WTOK - SENT_IN :].reshape(-1, 1))))
    return jnp.asarray(np.stack(both), jnp.int32)


def picks_out():
    place = np.argsort(frame_sources().reshape(-1)).reshape(4, HELD)
    there, row = place // HELD, place % HELD
    both = []
    for core in range(2):
        block = ((there // 2 + core) % 2) * 2 * SENT_OUT + (there % 2) * SENT_OUT
        picks = np.zeros((4, WTOK), np.int64)
        picks[:, HELD:] = block + row
        picks[:, :HELD] = block + row + HELD - (TOKS - SENT_OUT)
        both.append(np.concatenate((picks[:, :SENT_IN].reshape(-1, 1), picks[:, WTOK - SENT_IN :].reshape(-1, 1))))
    return jnp.asarray(np.stack(both), jnp.int32)


def plain_ring(clips):
    return bits_of("ctx") == 1 and clips == 1


def shift_start(arrays, clips):
    if plain_ring(clips):
        sent = jnp.concatenate([a[:, :SENT_IN] for a in arrays], 0)
        return swap(sent.reshape(-1, sent.shape[-1]), "ctx")
    return arrays[0][:1, :8]


def shift_in(arrays, got, clips, counts, core_row):
    if plain_ring(clips):
        xm, cm, other = select_in(core_row, picks_in(), *arrays, got)
        return xm, cm, swap(other, "tensor")
    half = arrays[0].shape[0] // 2
    core = lax.axis_index("tensor")
    mine, sent = [], []
    for array in arrays:
        moved = jnp.pad(window_roll(array, clips, counts, False), ((0, 0), (0, TOKS - WTOK), (0, 0)))
        mine.append(lax.dynamic_slice_in_dim(moved, core * half, half, 0))
        sent.append(lax.dynamic_slice_in_dim(moved, (1 - core) * half, half, 0))
    return mine[0], mine[1], swap(jnp.concatenate(sent, 0), "tensor")


def leave_start(pieces, clips):
    nearm, nearo, farm, faro = pieces
    width = nearm.shape[-1]
    if not plain_ring(clips):
        cut = TOKS - SENT_OUT
        mine, other = [jnp.concatenate((near[:, :cut], far), 1) for near, far in ((nearm, farm), (nearo, faro))]
        return mine, swap(other, "tensor")
    nearm, nearo, farm, faro = [piece.reshape(-1, width) for piece in pieces]
    corner = lax.ppermute(faro, ("ctx", "tensor"), [(i, i ^ 3) for i in range(4)])
    return nearm, swap(nearo, "tensor"), swap(farm, "ctx"), corner


def leave_end(parts, clips, counts, core_row, *deps):
    parts = (after(parts[0], *deps),) + tuple(parts[1:])
    if plain_ring(clips):
        return select_out(core_row, picks_out(), parts)
    windows = ordered(lax.axis_index("tensor") == 1, parts[0], parts[1], 0)
    return window_roll(windows[:, :WTOK], clips, counts, True).astype(F32)


def on_device(
    clip_input,
    cotangent,
    gain_one,
    shift_one,
    w_qkv,
    b_qv,
    w_proj,
    b_proj,
    bias_table,
    gain_two,
    shift_two,
    w_fc1,
    b_fc1,
    w_fc2,
    b_fc2,
    rel_index,
    regions,
):
    clips, window_count, tokens, half_width = clip_input.shape
    heads = bias_table.shape[0]
    levels = bits_of("ctx")
    counts = tuple(1 if axis_pos < levels else 2 for axis_pos in range(3))
    core = lax.axis_index("tensor")
    core_row = core.astype(jnp.int32).reshape(1)
    total_windows = clips * window_count
    held_windows = total_windows // 2
    scale = HD ** (-0.5)
    hidden = w_fc1.shape[1]

    own = pack(gain_one, shift_one, b_qv, b_proj, gain_two, shift_two, b_fc2, b_fc1, bias_table)
    got = swap(own, "tensor")
    qkv = gather_start(w_qkv.transpose(1, 0, 2).reshape(w_qkv.shape[1], -1))
    rest = gather_start(jnp.concatenate((w_proj.T, w_fc1, w_fc2.T), 1))
    index = jnp.pad(rel_index.T, ((0, TOKS - tokens), (0, TOKS - tokens)))
    index = lax.dynamic_slice_in_dim(index, core * (TOKS - HALF_ROWS), HALF_ROWS, 0)
    block = HALF_ROWS // ROWS
    cut = block // 2
    early_blocks = 5
    labels = jnp.tile(regions, (clips, 1))
    labels = lax.dynamic_slice_in_dim(labels, core * held_windows, held_windows, 0)
    labels = jnp.pad(labels, ((0, 0), (0, TOKS - tokens)))[:, None, :]

    order = bit_order()
    first, middle, last = order[0], order[1:-1], order[-1]
    clip_rows = clip_input.reshape(total_windows, tokens, half_width)
    cot_rows = cotangent.reshape(total_windows, tokens, half_width)

    pair_rows = (clip_rows, cot_rows)
    pair_got = shift_start(pair_rows, clips)
    qkv = gather_join(qkv, first, swap(qkv, "shard", first))
    qkv, qkv_got = gather_send(qkv, middle)
    rest = after(rest, qkv)
    rest_got = swap(rest, "shard", first)
    part_own = lookup(after(index, qkv), own, got, heads, 0, early_blocks)
    qkv_got, pair_got, rest_got, part_own = joint((qkv_got, pair_got, rest_got, part_own), ())
    qkv = gather_join(qkv, middle[-1], qkv_got)
    rest = gather_join(rest, first, rest_got)
    rest, rest_got = gather_send(rest, middle)
    qkv_got = swap(qkv, "shard", last)
    xm, cm, other = shift_in(pair_rows, pair_got, clips, counts, core_row)
    bias_own = lookup(after(index, xm), own, got, heads, early_blocks, block - early_blocks, (part_own,))
    rest_got, qkv_got, other, bias_own = joint((rest_got, qkv_got, other, bias_own), ())
    qkv = gather_join(qkv, last, qkv_got)
    qkv = qkv.reshape(-1, qkv.shape[-1])
    qkv_other = swap(qkv, "tensor")
    rest = gather_join(rest, middle[-1], rest_got)
    rest_got = swap(rest, "shard", last)
    bias_got = swap(bias_own, "tensor")
    queries, keys, values, first_t = front(xm, other, own, got, qkv, qkv_other, scale * LOG2E, ())
    att, exact, lse = attend(core_row, queries, keys, values, labels, bias_own, bias_got)
    rest_got, att = joint((rest_got, att), ())
    edge = half_width + hidden
    early, late = [gather_join(rest[..., span], last, rest_got[..., span]) for span in (slice(0, edge), slice(edge, None))]
    early, late = [w.reshape(-1, w.shape[-1]) for w in (early, late)]
    early_other, late_other = swap(early, "tensor"), swap(late, "tensor")
    mid, second, act, slope = middle_forward(xm, other, att, own, got, early, early_other)
    *block_pieces, grad_mid, grad_att, one_mine, one_other, two_mine, two_other, small_mid, small_wide = middle_back(cm, other, mid, second, act, slope, att, own, got, early, early_other, late, late_other, ())

    order = order[::-1]
    twice = bits_of("ctx") == 1
    args = (core_row, queries, keys, values, labels, bias_own, bias_got)
    block_parts = leave_start(block_pieces, clips)
    one_got, two_got = swap(one_other, "tensor"), swap(two_other, "tensor")
    qo, ko, vo, pair_o, sent_o = attend_back(*args, exact, lse, grad_att, scale, 1)
    one_got, two_got, qo, sent_o, *moved = joint((one_got, two_got, qo, sent_o) + tuple(block_parts[1:]), ())
    block_parts = (block_parts[0],) + tuple(moved)
    one, two = split_rows(add_rounded(one_mine, one_got)), split_rows(add_rounded(two_mine, two_got))
    one_got = scatter_send(one, order[:1])[1]
    two_got = ctx_split_send(two) if twice else scatter_send(two, order[:1])[1]
    side = side_grads(first_t, (qo, ko, vo))
    side_got, sent_o = swap(side, "tensor"), swap(sent_o, "tensor")
    qm, km, vm, pair_m, sent_m = attend_back(*args, exact, lse, after(grad_att, side), scale, 0)
    one_got, two_got, side, sent_o, qm, sent_m = joint((one_got, two_got, side_got, sent_o, qm, sent_m), ())
    one = scatter_add(one, order[0], one_got)
    two = ctx_split_add(two, two_got) if twice else scatter_add(two, order[0], two_got)
    one_got = scatter_send(one, order[1:2])[1]
    two_bits = order if twice else order[1:]
    two_got = scatter_send(two, two_bits[:1])[1]
    sent_m = swap(sent_m, "tensor")
    *grad_pieces, qkv_grads, small_end = back(xm, other, first_t, (after(qm, one, two), km, vm), (qo, ko, vo), grad_mid, own, got, qkv, qkv_other, side)
    block_out = leave_end(block_parts, clips, counts, core_row, small_end)
    one_got, two_got, sent_m, block_out = joint((one_got, two_got, sent_m, block_out), ())
    one = scatter_add(one, order[1], one_got)
    two = scatter_add(two, two_bits[0], two_got)
    qkv_grads = split_rows(qkv_grads)
    qkv_got = scatter_send(qkv_grads, order[:1])[1]
    grad_parts = leave_start(grad_pieces, clips)
    two_got = scatter_send(two, two_bits[1:2])[1]
    one, one_got = scatter_send(one, order[2:])
    pairs = (pair_m, pair_o, sent_m, sent_o)
    (folded,) = fold(core_row, after(index, one, two), pairs, heads, 0, cut)
    qkv_got, two_got, one_got, folded, *moved = joint((qkv_got, two_got, one_got, folded) + tuple(grad_parts[1:]), ())
    grad_parts = (grad_parts[0],) + tuple(moved)
    qkv_grads = scatter_add(qkv_grads, order[0], qkv_got)
    two = scatter_add(two, two_bits[1], two_got)
    one = scatter_add(one, order[-1], one_got)
    qkv_got = scatter_send(qkv_grads, order[1:2])[1]
    two, two_got = scatter_send(two, two_bits[2:])
    one, one_got = ctx_send(one)
    fold_mine, fold_other = fold(core_row, after(index, one, two, qkv_grads), pairs, heads, cut, block - cut, (folded, small_mid, small_wide, small_end))
    qkv_got, two_got, one_got, fold_mine, fold_other = joint((qkv_got, two_got, one_got, fold_mine, fold_other), ())
    small = fold_mine + swap(fold_other, "tensor")
    qkv_grads = scatter_add(qkv_grads, order[1], qkv_got)
    qkv_grads, qkv_got = scatter_send(qkv_grads, order[2:])
    two = scatter_add(two, two_bits[-1], two_got)
    two, two_got = (two, swap(two, "ctx")) if twice else ctx_send(two)
    groups = joint_groups()
    for group in groups[:-2]:
        small = add_parts(joint_parts(small, group))
    parts = joint_parts(small, groups[-2])
    grad_input = leave_end(grad_parts, clips, counts, core_row, small)
    *parts, grad_input = joint(tuple(parts) + (grad_input,), ())
    small = add_parts(parts)
    parts = joint_parts(small, groups[-1])
    qkv_got, two_got, one_got = joint((qkv_got, two_got, one_got), (small,))
    qkv_grads = scatter_add(qkv_grads, order[-1], qkv_got)
    qkv_grads, qkv_got = ctx_send(qkv_grads)
    one = ctx_add(one, one_got)
    two = flat(ordered(bit_on("ctx", 0) == 1, two, two_got, two.ndim - 2)).astype(F32) if twice else ctx_add(two, two_got)
    qkv_grads = ctx_add(qkv_grads, qkv_got)
    d_gain1, d_shift1, d_bqv, d_bp, d_table, d_gain2, d_shift2, d_b1, d_b2 = unpack(parts, heads)
    rows = w_fc1.shape[0]
    return (
        block_out.reshape(clip_input.shape),
        grad_input.reshape(clip_input.shape),
        d_gain1,
        d_shift1,
        qkv_grads.reshape(rows, 3, half_width).transpose(1, 0, 2),
        d_bqv,
        two[:, :half_width].T,
        d_bp,
        d_table,
        d_gain2,
        d_shift2,
        one,
        d_b1,
        two[:, half_width:].T,
        d_b2,
    )


def solution(mesh):
    in_specs = (
        P("shard", "ctx", None, "tensor"),
        P("shard", "ctx", None, "tensor"),
        P("tensor"),
        P("tensor"),
        P(None, "shard", "tensor"),
        P(None, "tensor"),
        P("tensor", "shard"),
        P("tensor"),
        P("tensor", None),
        P("tensor"),
        P("tensor"),
        P("shard", "tensor"),
        P("tensor"),
        P("tensor", "shard"),
        P("tensor"),
        P(),
        P("ctx", None),
    )
    out_specs = (
        P("shard", "ctx", None, "tensor"),
        P("shard", "ctx", None, "tensor"),
        P("tensor"),
        P("tensor"),
        P(None, "shard", "tensor"),
        P(None, "tensor"),
        P("tensor", "shard"),
        P("tensor"),
        P("tensor", None),
        P("tensor"),
        P("tensor"),
        P("shard", "tensor"),
        P("tensor"),
        P("tensor", "shard"),
        P("tensor"),
    )
    return jax.shard_map(
        on_device, mesh=mesh, in_specs=in_specs, out_specs=out_specs, check_vma=False
    )
```

```python
import functools

import jax
import jax.numpy as jnp
import numpy as np
from jax import lax
from jax.experimental import pallas as pl
from jax.experimental.pallas import tpu as pltpu
from jax.sharding import PartitionSpec as P

BF = jnp.bfloat16
F32 = jnp.float32
HD = 32
WT, WH, WW = 8, 7, 7
WTOK = WT * WH * WW
TOKS = 400
LANES = 512
HALF_ROWS = 208
TABLE = 2535
COARSE = 10
FINE = 256
ROWS = 16
GROUP = 4
BACK_GROUP = 2
EPSILON = 1e-05
HELD = WTOK // 2
SENT_IN = 200
SENT_OUT = 208
LOG2E = 1.4426950408889634
VECTOR_ROWS = 96
GAIN1, SHIFT1, BIAS_Q, BIAS_V, BIAS_P, GAIN2, SHIFT2, BIAS2, BIAS1 = range(80, 89)
ANY = pl.BlockSpec(memory_space=pl.ANY)


def dot(a, b, ca, cb):
    return lax.dot_general(a, b, (((ca,), (cb,)), ((), ())), preferred_element_type=F32)


def cost(flops, moved, trans=0):
    return pl.CostEstimate(flops=1, bytes_accessed=1, transcendentals=0)


def params(size=56):
    return pltpu.CompilerParams(vmem_limit_bytes=size * 1024 * 1024)


def whole_spec(array):
    rank = len(array.shape)
    return pl.BlockSpec(array.shape, lambda *_: (0,) * rank)


def window_spec(array, skip=0):
    rank = len(array.shape)
    return pl.BlockSpec((1,) + array.shape[1:], lambda w, *_: (w + skip,) + (0,) * (rank - 1))


def flip(values, axis=1):
    half = values.shape[axis] // 2
    low = lax.slice_in_dim(values, 0, half, axis=axis)
    high = lax.slice_in_dim(values, half, 2 * half, axis=axis)
    return jnp.concatenate([high, low], axis)


def row_pair(own_ref, got_ref, row, count=1):
    return jnp.concatenate([ref[r : r + 1, :] for ref in (own_ref, got_ref) for r in range(row, row + count)], 1)


def normed(values):
    width = values.shape[1]
    center = jnp.sum(values, 1, keepdims=True) / width
    spread = jnp.sum(values * values, 1, keepdims=True) / width - center * center
    inv = lax.rsqrt(spread + EPSILON)
    return (values - center) * inv, inv


def norm_back(upstream, xhat, inv, gain):
    width = xhat.shape[1]
    scaled = upstream * gain
    total = jnp.sum(scaled, 1, keepdims=True) / width
    along = jnp.sum(scaled * xhat, 1, keepdims=True) / width
    return inv * (scaled - total - xhat * along)


def pack_kernel(gain1, shift1, bqv, bp, gain2, shift2, b2, b1, table, out_ref):
    out_ref[...] = jnp.zeros_like(out_ref)
    heads = table.shape[0]
    for c in range(COARSE):
        size = min(FINE, TABLE - c * FINE)
        out_ref[c * heads : (c + 1) * heads, :size] = table[:, c * FINE : c * FINE + size]
    rows = ((GAIN1, gain1), (SHIFT1, shift1), (BIAS_P, bp), (GAIN2, gain2), (SHIFT2, shift2), (BIAS2, b2))
    for row, ref in rows:
        out_ref[row : row + 1, :] = ref[...].reshape(1, -1)
    out_ref[BIAS_Q : BIAS_Q + 2, :] = bqv[...]
    wide = b1[...].reshape(1, -1)
    for i in range(4):
        out_ref[BIAS1 + i : BIAS1 + i + 1, :] = wide[:, i * 256 : (i + 1) * 256]


def pack(*arrays):
    return pl.pallas_call(
        pack_kernel,
        out_shape=jax.ShapeDtypeStruct((VECTOR_ROWS, FINE), F32),
        cost_estimate=cost(1000, 200000),
        name="pack",
    )(*arrays)


def unpack_kernel(a_ref, b_ref, c_ref, d_ref, gain1, shift1, bqv, bp, table, gain2, shift2, b1, b2):
    a, b, c, d = [ref[...].astype(F32) for ref in (a_ref, b_ref, c_ref, d_ref)]
    total = (a + b) + (c + d)
    heads = table.shape[0]
    for c in range(COARSE):
        size = min(FINE, TABLE - c * FINE)
        table[:, c * FINE : c * FINE + size] = total[c * heads : (c + 1) * heads, :size]
    rows = ((GAIN1, gain1), (SHIFT1, shift1), (BIAS_P, bp), (GAIN2, gain2), (SHIFT2, shift2), (BIAS2, b2))
    for row, ref in rows:
        ref[...] = total[row : row + 1].reshape(-1)
    bqv[...] = total[BIAS_Q : BIAS_Q + 2]
    b1[...] = jnp.concatenate([total[BIAS1 + i : BIAS1 + i + 1] for i in range(4)], 1).reshape(-1)


def unpack(parts, heads):
    vector = jax.ShapeDtypeStruct((FINE,), F32)
    return pl.pallas_call(
        unpack_kernel,
        out_shape=[vector, vector, jax.ShapeDtypeStruct((2, FINE), F32), vector, jax.ShapeDtypeStruct((heads, TABLE), F32), vector, vector, jax.ShapeDtypeStruct((4 * FINE,), F32), vector],
        cost_estimate=cost(1000, 200000),
        name="unpack",
    )(*parts)


def lane_tiles(width):
    return [(t, t * 128, min(128, width - t * 128)) for t in range(-(-width // 128))]


def put_rows(scratch, start, rows):
    for t, begin, size in lane_tiles(rows.shape[1]):
        scratch[t, start : start + rows.shape[0], :size] = rows[:, begin : begin + size]


def strided_rows(scratch, start, count, step, width):
    parts = [scratch[t, pl.ds(start, count, stride=step), :][:, :size] for t, _, size in lane_tiles(width)]
    return jnp.concatenate(parts, 1)


def one_hot(fine_row, width):
    rows = lax.broadcasted_iota(jnp.int32, (FINE, width), 0).astype(jnp.int16)
    return jnp.where(rows == fine_row.astype(jnp.int16), jnp.ones((), BF), jnp.zeros((), BF))


def lookup_kernel(heads, idx_ref, own_ref, got_ref, *rest):
    out_ref, scratch, table = rest[-3:]
    width = idx_ref.shape[1]

    @pl.when(pl.program_id(0) == 0)
    def _():
        for c in range(COARSE):
            span = slice(c * heads, (c + 1) * heads)
            level_rows = jnp.concatenate([own_ref[span, :], got_ref[span, :]], 0)
            table[2 * c * heads : 2 * (c + 1) * heads, :] = (level_rows * LOG2E).astype(BF)

    for r in range(ROWS):
        idx = idx_ref[r : r + 1, :]
        hot = one_hot(jnp.bitwise_and(idx, FINE - 1), width)
        level = lax.shift_right_logical(idx, 8)
        picked = dot(table[...], hot, 1, 0)
        acc = picked[: 2 * heads]
        for c in range(1, COARSE):
            acc = jnp.where(level == c, picked[2 * c * heads : 2 * (c + 1) * heads], acc)
        put_rows(scratch, 2 * r * heads, acc)
    for h in range(2 * heads):
        out_ref[h, :, :width] = strided_rows(scratch, h, ROWS, 2 * heads, width).astype(BF)


def lookup(idx, own, got, heads, start, count, filled=()):
    width = idx.shape[1]
    return pl.pallas_call(
        functools.partial(lookup_kernel, heads),
        grid=(count,),
        in_specs=[pl.BlockSpec((ROWS, width), lambda i: (start + i, 0)), whole_spec(own), whole_spec(got)] + [ANY] * len(filled),
        out_specs=pl.BlockSpec((2 * heads, ROWS, LANES), lambda i: (0, start + i, 0)),
        out_shape=jax.ShapeDtypeStruct((2 * heads, HALF_ROWS, LANES), BF),
        input_output_aliases={3: 0} if filled else {},
        scratch_shapes=[pltpu.VMEM((-(-width // 128), 2 * ROWS * heads, 128), F32), pltpu.VMEM((2 * COARSE * heads, FINE), BF)],
        compiler_params=params(),
        cost_estimate=cost(0, 0),
        name="table_lookup",
    )(idx, own, got, *filled)


def fold_rows(heads, idx_ref, pair_m, pair_o, sent_m, sent_o, scratch, total):
    width = idx_ref.shape[1]
    for h in range(heads):
        put_rows(scratch, h * ROWS, pair_m[h, :, :width].astype(F32) + sent_o[h, :, :width].astype(F32))
        put_rows(scratch, (heads + h) * ROWS, pair_o[h, :, :width].astype(F32) + sent_m[h, :, :width].astype(F32))
    part = jnp.zeros(total.shape, F32)
    fine = jnp.bitwise_and(idx_ref[...], FINE - 1).T.astype(jnp.int16)
    cells = lax.broadcasted_iota(jnp.int32, (width, FINE), 1).astype(jnp.int16)
    for r in range(ROWS):
        hot = jnp.where(cells == fine[:, r : r + 1], jnp.ones((), BF), jnp.zeros((), BF))
        level = lax.shift_right_logical(idx_ref[r : r + 1, :], 8)
        grads = strided_rows(scratch, r, 2 * heads, ROWS, width)
        parts = [jnp.where(level == c, grads, 0.0) for c in range(COARSE)]
        part = part + dot(jnp.concatenate(parts, 0).astype(BF), hot, 1, 0)
    total[...] += part


def fold_start_kernel(heads, core_ref, idx_ref, pair_m, pair_o, sent_m, sent_o, total, scratch):
    step = pl.program_id(0)

    @pl.when(step == 0)
    def _():
        total[...] = jnp.zeros_like(total)

    @pl.when(jnp.logical_or(step > 0, core_ref[0] == 0))
    def _():
        fold_rows(heads, idx_ref, pair_m, pair_o, sent_m, sent_o, scratch, total)


def fold_end_kernel(heads, core_ref, idx_ref, pair_m, pair_o, sent_m, sent_o, init_ref, mid_ref, wide_ref, end_ref, mine_ref, other_ref, scratch, total):
    step = pl.program_id(0)

    @pl.when(step == 0)
    def _():
        total[...] = init_ref[...]

    fold_rows(heads, idx_ref, pair_m, pair_o, sent_m, sent_o, scratch, total)

    @pl.when(step == pl.num_programs(0) - 1)
    def _():
        for half, ref in enumerate((mine_ref, other_ref)):
            for c in range(COARSE):
                at = (2 * c + half) * heads
                ref[c * heads : (c + 1) * heads, :] = total[at : at + heads, :]
            span = slice(half * 256, (half + 1) * 256)
            rows = ((GAIN1, end_ref, 2), (SHIFT1, end_ref, 3), (BIAS_Q, end_ref, 0), (BIAS_V, end_ref, 1), (BIAS_P, mid_ref, 3), (GAIN2, mid_ref, 1), (SHIFT2, mid_ref, 2), (BIAS2, mid_ref, 0))
            for row, source, at in rows:
                ref[row : row + 1, :] = source[at : at + 1, span]
            for i in range(4):
                at = half * 1024 + i * 256
                ref[BIAS1 + i : BIAS1 + i + 1, :] = wide_ref[:, at : at + 256]
            ref[BIAS1 + 4 :, :] = jnp.zeros((VECTOR_ROWS - BIAS1 - 4, 256), F32)


def fold(core, idx, pairs, heads, start, count, extra=()):
    width = idx.shape[1]
    scratch = [pltpu.VMEM((-(-width // 128), 2 * ROWS * heads, 128), F32)]
    total = jax.ShapeDtypeStruct((2 * COARSE * heads, FINE), F32)
    ends = jax.ShapeDtypeStruct((VECTOR_ROWS, FINE), F32)
    outs = [ends, ends] if extra else [total]
    pair = pl.BlockSpec((heads, ROWS, LANES), lambda i, core: (0, start + i, 0))
    return pl.pallas_call(
        functools.partial(fold_end_kernel if extra else fold_start_kernel, heads),
        grid_spec=pltpu.PrefetchScalarGridSpec(
            num_scalar_prefetch=1,
            grid=(count,),
            in_specs=[pl.BlockSpec((ROWS, width), lambda i, core: (start + i, 0))] + [pair] * 4 + [whole_spec(e) for e in extra],
            out_specs=[whole_spec(o) for o in outs],
            scratch_shapes=scratch + ([pltpu.VMEM(total.shape, F32)] if extra else []),
        ),
        out_shape=outs,
        compiler_params=params(),
        cost_estimate=cost(0, 0),
        name="table_fold",
    )(core, idx, *pairs, *extra)


def mask_pieces():
    pieces = []
    rest = np.float32(-100.0 * LOG2E)
    for _ in range(3):
        piece = np.float32(rest.astype(jnp.bfloat16))
        pieces.append(float(piece))
        rest = np.float32(rest - piece)
    return pieces


def region_rows(label):
    width = label.shape[1]
    rows = lax.broadcasted_iota(jnp.int32, (16, width), 0)
    lanes = lax.broadcasted_iota(jnp.int32, (16, width), 1)
    same = jnp.bitwise_and(rows, 3) == label
    level = lax.shift_right_logical(rows, 2)
    high, mid, low = mask_pieces()
    piece = jnp.where(level == 0, high, jnp.where(level == 1, mid, low))
    queries = jnp.where(rows < 12, jnp.where(same, 1.0, 0.0), jnp.where(rows == 15, 1.0, 0.0))
    past = jnp.where(jnp.logical_and(rows == 15, lanes >= WTOK), -1e30, 0.0)
    keys = jnp.where(rows < 12, jnp.where(same, 0.0, piece), past)
    return queries.astype(BF), keys.astype(BF)


def pick_bias(first, own_ref, got_ref, j):
    skip = 2 * HALF_ROWS - TOKS
    low = lax.select_n(first, got_ref[j, :, :TOKS], own_ref[j, :, :TOKS])
    high = lax.select_n(first, own_ref[j, skip:, :TOKS], got_ref[j, skip:, :TOKS])
    return jnp.concatenate([low, high], 0).astype(F32)


def attend_kernel(core_ref, q_ref, k_ref, v_ref, label_ref, own_ref, got_ref, att_ref, exact_ref, lse_ref):
    first = core_ref[0] == 0
    ones = jnp.ones((16, TOKS), BF)
    windows = range(q_ref.shape[0])
    regions = [region_rows(label_ref[w]) for w in windows]
    for j in range(GROUP):
        part = pl.ds(j * HD, HD)
        bias = pick_bias(first, own_ref, got_ref, j)
        for w in windows:
            query_rows, key_rows = regions[w]
            qa = jnp.concatenate([q_ref[w, part, :], query_rows], 0)
            ka = jnp.concatenate([k_ref[w, part, :], key_rows], 0)
            va = jnp.concatenate([v_ref[w, part, :], ones], 0)
            scores = dot(ka, qa, 0, 0) + bias
            peak = jnp.max(scores, 0, keepdims=True)
            weights = jnp.exp2(scores - peak).astype(BF)
            mixed = dot(va, weights, 1, 0)
            total = mixed[HD : HD + 1]
            out = mixed[:HD] / total
            att_ref[w, part, :] = out.astype(BF)
            exact_ref[w, part, :] = out
            lse_ref[w, 0, j : j + 1, :] = peak + jnp.log2(total)


def attention_specs(wins, heads, skip=0, group=GROUP):
    half = heads // (2 * group)
    ratio = GROUP // group
    feat = pl.BlockSpec((wins, group * HD, TOKS), lambda h, core: (0, h + skip, 0))
    label = pl.BlockSpec((wins, 1, TOKS), lambda h, core: (0, 0, 0))
    own = pl.BlockSpec((group, HALF_ROWS, LANES), lambda h, core: (h + skip, 0, 0))
    got = pl.BlockSpec((group, HALF_ROWS, LANES), lambda h, core: ((h + skip + half) % (2 * half), 0, 0))
    stat = pl.BlockSpec((wins, 1, GROUP, TOKS), lambda h, core: (0, (h + skip) // ratio, 0, 0))
    return feat, label, own, got, stat


def attend(core, q, k, v, labels, own, got):
    wins, feats, toks = q.shape
    heads = feats // HD
    feat, label, own_spec, got_spec, stat = attention_specs(wins, heads)
    return pl.pallas_call(
        attend_kernel,
        grid_spec=pltpu.PrefetchScalarGridSpec(
            num_scalar_prefetch=1,
            grid=(heads // GROUP,),
            in_specs=[feat, feat, feat, label, own_spec, got_spec],
            out_specs=[feat, feat, stat],
        ),
        out_shape=[
            jax.ShapeDtypeStruct(q.shape, BF),
            jax.ShapeDtypeStruct(q.shape, F32),
            jax.ShapeDtypeStruct((wins, heads // GROUP, GROUP, toks), F32),
        ],
        compiler_params=params(),
        cost_estimate=cost(0, 0),
        name="attend",
    )(core, q, k, v, labels, own, got)


def split3(row):
    hi = row.astype(BF)
    rest = row - hi.astype(F32)
    mid = rest.astype(BF)
    return hi.astype(F32), mid.astype(F32), rest - mid.astype(F32)


def rows16(parts, width):
    rows = lax.broadcasted_iota(jnp.int32, (16, width), 0)
    out = jnp.zeros((16, width), F32)
    for i, part in enumerate(parts):
        out = jnp.where(rows == i, part, out)
    return out.astype(BF)


def attend_back_kernel(scale, core_ref, q_ref, k_ref, v_ref, label_ref, own_ref, got_ref, exact_ref, lse_ref, g_ref, dq_ref, dk_ref, dv_ref, pair_ref, sent_ref, sums):
    core = core_ref[0]
    first = core == 0
    step = TOKS - HALF_ROWS
    mine, other = pl.multiple_of(core * step, 8), pl.multiple_of((1 - core) * step, 8)
    minus = rows16([-1.0, -1.0, -1.0], TOKS)
    windows = range(q_ref.shape[0])
    regions = [region_rows(label_ref[w]) for w in windows]
    base = lax.rem(pl.program_id(0), GROUP // BACK_GROUP) * BACK_GROUP
    for j in range(BACK_GROUP):
        part = pl.ds(j * HD, HD)
        bias = pick_bias(first, own_ref, got_ref, j)
        total = None
        for w in windows:
            query_rows, key_rows = regions[w]
            q = q_ref[w, part, :]
            k = k_ref[w, part, :]
            g = g_ref[w, part, :]
            qa = jnp.concatenate([q, query_rows, rows16(split3(lse_ref[w, 0, pl.ds(base + j, 1), :]), TOKS)], 0)
            ka = jnp.concatenate([k, key_rows, minus], 0)
            va = jnp.concatenate([v_ref[w, part, :], minus], 0)
            along = jnp.sum(g.astype(F32) * exact_ref[w, part, :], 0, keepdims=True)
            ga = jnp.concatenate([g, rows16(split3(along), TOKS)], 0)
            probs = jnp.exp2(dot(ka, qa, 0, 0) + bias)
            wide = probs * dot(va, ga, 0, 0)
            grads = wide.astype(BF)
            low = probs.astype(BF)
            dv_ref[w, part, :] = dot(g, low, 1, 1).astype(BF)
            dk_ref[w, part, :] = (dot(q, grads, 1, 1) * (1.0 / LOG2E)).astype(BF)
            dq_ref[w, part, :] = (dot(k, grads, 1, 0) * scale).astype(BF)
            total = wide if total is None else total + wide
        sums[...] = total
        pair_ref[j, :, :TOKS] = sums[pl.ds(mine, HALF_ROWS), :].astype(BF)
        sent_ref[j, :, :TOKS] = sums[pl.ds(other, HALF_ROWS), :].astype(BF)


def attend_back(core, q, k, v, labels, own, got, exact, lse, g, scale, side):
    wins, feats, toks = q.shape
    heads = feats // HD
    blocks = heads // (2 * BACK_GROUP)
    feat, label, own_spec, got_spec, stat = attention_specs(wins, heads, side * blocks, BACK_GROUP)
    out = pl.BlockSpec((wins, BACK_GROUP * HD, toks), lambda h, core: (0, h, 0))
    pair = pl.BlockSpec((BACK_GROUP, HALF_ROWS, LANES), lambda h, core: (h, 0, 0))
    return pl.pallas_call(
        functools.partial(attend_back_kernel, scale),
        grid_spec=pltpu.PrefetchScalarGridSpec(
            num_scalar_prefetch=1,
            grid=(blocks,),
            in_specs=[feat, feat, feat, label, own_spec, got_spec, feat, stat, feat],
            out_specs=[out, out, out, pair, pair],
            scratch_shapes=[pltpu.VMEM((toks, toks), F32)],
        ),
        out_shape=[jax.ShapeDtypeStruct((wins, feats // 2, toks), BF)] * 3 + [jax.ShapeDtypeStruct((heads // 2, HALF_ROWS, LANES), BF)] * 2,
        compiler_params=params(),
        cost_estimate=cost(0, 0),
        name="attend_back",
    )(core, q, k, v, labels, own, got, exact, lse, g)


def front_kernel(scale, xm_ref, xo_ref, own_ref, got_ref, wm_ref, wo_ref, *rest):
    q_ref, k_ref, v_ref, first_ref = rest[-4:]
    x = jnp.concatenate([xm_ref[0], xo_ref[0]], 1).astype(F32)
    xhat, _ = normed(x)
    first = (xhat * row_pair(own_ref, got_ref, GAIN1) + row_pair(own_ref, got_ref, SHIFT1)).astype(BF)
    first_ref[0] = first.T
    for t, (w_ref, vec_ref) in enumerate(((wm_ref, own_ref), (wo_ref, got_ref))):
        cols = w_ref.shape[1] // 3
        rows = pl.ds(t * cols, cols)
        made = dot(first if t == 0 else flip(first), w_ref[...], 1, 0)
        q = (made[:, :cols] + vec_ref[BIAS_Q : BIAS_Q + 1, :]) * scale
        v = made[:, 2 * cols :] + vec_ref[BIAS_V : BIAS_V + 1, :]
        q_ref[0, rows, :] = q.astype(BF).T
        k_ref[0, rows, :] = made[:, cols : 2 * cols].astype(BF).T
        v_ref[0, rows, :] = v.astype(BF).T


def front(xm, xo, own, got, wm, wo, scale, deps):
    wins, toks, half = xm.shape
    out = jax.ShapeDtypeStruct((wins, 2 * (wm.shape[1] // 3), toks), BF)
    return pl.pallas_call(
        functools.partial(front_kernel, scale),
        grid=(wins,),
        in_specs=[window_spec(xm), window_spec(xo), whole_spec(own), whole_spec(got), whole_spec(wm), whole_spec(wo)] + [ANY] * len(deps),
        out_specs=[window_spec(out)] * 4,
        out_shape=[out] * 4,
        compiler_params=params(),
        cost_estimate=cost(8 * wins * toks * half * wm.shape[1], wins * toks * half * 16 + wm.size * 4),
        name="front",
    )(xm, xo, own, got, wm, wo, *deps)


def middle_kernel(xm_ref, xo_ref, att_ref, own_ref, got_ref, wm_ref, wo_ref, *rest):
    mid_ref, second_ref, act_ref, slope_ref = rest[-4:]
    half = xm_ref.shape[2]
    wide = wm_ref.shape[1] - half
    branch = dot(att_ref[0, :half, :].T, wm_ref[:, :half], 1, 1) + flip(dot(att_ref[0, half:, :].T, wo_ref[:, :half], 1, 1))
    x = jnp.concatenate([xm_ref[0], xo_ref[0]], 1).astype(F32)
    middle = x + (branch + row_pair(own_ref, got_ref, BIAS_P))
    mid_ref[0] = middle
    xhat, _ = normed(middle)
    second = (xhat * row_pair(own_ref, got_ref, GAIN2) + row_pair(own_ref, got_ref, SHIFT2)).astype(BF)
    second_ref[0] = second
    turned = flip(second)
    for t, (w_ref, vec_ref) in enumerate(((wm_ref, own_ref), (wo_ref, got_ref))):
        for s in range(0, wide, 256):
            at = t * wide + s
            bias = vec_ref[BIAS1 + s // 256 : BIAS1 + s // 256 + 1, :]
            hidden = dot(second if t == 0 else turned, w_ref[:, half + s : half + s + 256], 1, 0) + bias
            phi = 0.5 + 0.5 * lax.erf(hidden * (0.5**0.5))
            bell = jnp.exp2(hidden * hidden * (-0.5 * LOG2E)) * (1.0 / (2.0 * np.pi) ** 0.5)
            act_ref[0, :, at : at + 256] = (hidden * phi).astype(BF)
            slope_ref[0, :, at : at + 256] = (phi + hidden * bell).astype(BF)


def middle_forward(xm, xo, att, own, got, wm, wo):
    wins, toks, half = xm.shape
    width = 2 * half
    hidden = 2 * (wm.shape[1] - half)
    wide = jax.ShapeDtypeStruct((wins, toks, hidden), BF)
    outs = [jax.ShapeDtypeStruct((wins, toks, width), F32), jax.ShapeDtypeStruct((wins, toks, width), BF), wide, wide]
    fixed = (own, got, wm, wo)
    return pl.pallas_call(
        middle_kernel,
        grid=(wins,),
        in_specs=[window_spec(a) for a in (xm, xo, att)] + [whole_spec(a) for a in fixed],
        out_specs=[window_spec(o) for o in outs],
        out_shape=outs,
        compiler_params=params(28),
        cost_estimate=cost(8 * wins * toks * width * wm.shape[1], wins * toks * (width * 10 + hidden * 4) + wm.size * 4, wins * toks * hidden),
        name="middle_forward",
    )(xm, xo, att, *fixed)


def put_pieces(out, nearm_ref, nearo_ref, farm_ref, faro_ref):
    half = out.shape[1] // 2
    for ref, rows, cols in ((nearm_ref, 0, 0), (nearo_ref, 0, half), (farm_ref, TOKS - SENT_OUT, 0), (faro_ref, TOKS - SENT_OUT, half)):
        ref[0] = out[rows : rows + SENT_OUT, cols : cols + half]


def middle_back_kernel(cm_ref, co_ref, mid_ref, second_ref, act_ref, slope_ref, att_ref, own_ref, got_ref, wm_ref, wo_ref, fm_ref, fo_ref, *rest):
    nearm_ref, nearo_ref, farm_ref, faro_ref, gm_ref, gr_ref, onem_ref, oneo_ref, twom_ref, twoo_ref, small_ref, wide_ref, accm, acco = rest[-14:]
    win = pl.program_id(0)
    half = cm_ref.shape[2]
    wide = fm_ref.shape[1]

    @pl.when(win == 0)
    def _():
        accm[...] = jnp.zeros_like(accm)
        acco[...] = jnp.zeros_like(acco)
        small_ref[...] = jnp.zeros_like(small_ref)
        wide_ref[...] = jnp.zeros_like(wide_ref)

    cot = jnp.concatenate([cm_ref[0], co_ref[0]], 1)
    cot_turned = flip(cot)
    cot_t = cot.T
    second_t = second_ref[0].T
    sides = (
        (wm_ref, fm_ref, accm, cot, cot_t, second_t),
        (wo_ref, fo_ref, acco, cot_turned, flip(cot_t, 0), flip(second_t, 0)),
    )
    made, pulled = [], []
    for t, (w_ref, f_ref, acc, c, c_t, s_t) in enumerate(sides):
        forward = jnp.zeros(cot.shape, F32)
        grad_second = jnp.zeros(cot.shape, F32)
        for s in range(0, wide, 512):
            span = slice(t * wide + s, t * wide + s + 512)
            fc2 = f_ref[:, s : s + 512]
            active = act_ref[0, :, span]
            forward = forward + dot(active, fc2, 1, 1)
            grad = (dot(c, fc2, 1, 0) * slope_ref[0, :, span].astype(F32)).astype(BF)
            wide_ref[:, span] += jnp.sum(grad.astype(F32), 0, keepdims=True)
            acc[:, half + wide + s : half + wide + s + 512] += dot(c_t, active, 1, 0)
            acc[:, half + s : half + s + 512] += dot(s_t, grad, 1, 0)
            grad_second = grad_second + dot(grad, w_ref[:, half + s : half + s + 512], 1, 1)
        made.append(forward)
        pulled.append(grad_second)
    out = mid_ref[0] + (made[0] + flip(made[1]) + row_pair(own_ref, got_ref, BIAS2))
    put_pieces(out.astype(BF), nearm_ref, nearo_ref, farm_ref, faro_ref)
    grad_second = pulled[0] + flip(pulled[1])
    upstream = cot.astype(F32)
    xhat, inv = normed(mid_ref[0])
    grad_mid = upstream + norm_back(grad_second, xhat, inv, row_pair(own_ref, got_ref, GAIN2))
    gm_ref[0] = grad_mid
    branch = grad_mid.astype(BF)
    branch_t = branch.T
    gr_ref[0, :half, :] = dot(branch, wm_ref[:, :half], 1, 0).astype(BF).T
    gr_ref[0, half:, :] = dot(flip(branch), wo_ref[:, :half], 1, 0).astype(BF).T
    accm[:, :half] += dot(branch_t, att_ref[0, :half, :], 1, 1)
    acco[:, :half] += dot(flip(branch_t, 0), att_ref[0, half:, :], 1, 1)
    small_ref[0:1, :] += jnp.sum(upstream, 0, keepdims=True)
    small_ref[1:2, :] += jnp.sum(grad_second * xhat, 0, keepdims=True)
    small_ref[2:3, :] += jnp.sum(grad_second, 0, keepdims=True)
    small_ref[3:4, :] += jnp.sum(branch.astype(F32), 0, keepdims=True)

    @pl.when(win == pl.num_programs(0) - 1)
    def _():
        for acc, one_ref, two_ref in ((accm, onem_ref, twom_ref), (acco, oneo_ref, twoo_ref)):
            one_ref[...] = acc[:, half : half + wide].astype(BF)
            two_ref[:, :half] = acc[:, :half].astype(BF)
            two_ref[:, half:] = acc[:, half + wide :].astype(BF)


def middle_back(cm, co, mid, second, act, slope, att, own, got, wm, wo, fm, fo, deps):
    wins, toks, half = cm.shape
    width = 2 * half
    hidden = act.shape[2]
    windows = (cm, co, mid, second, act, slope, att)
    fixed = (own, got, wm, wo, fm, fo)
    plain = jax.ShapeDtypeStruct((wins, SENT_OUT, half), BF)
    outs = [plain, plain, plain, plain, jax.ShapeDtypeStruct(mid.shape, F32), jax.ShapeDtypeStruct((wins, width, toks), BF)]
    grads = jax.ShapeDtypeStruct((width, wm.shape[1] + fm.shape[1]), BF)
    one = jax.ShapeDtypeStruct((width, wm.shape[1] - half), BF)
    two = jax.ShapeDtypeStruct((width, half + fm.shape[1]), BF)
    sums = [one, one, two, two, jax.ShapeDtypeStruct((4, width), F32), jax.ShapeDtypeStruct((1, hidden), F32)]
    return pl.pallas_call(
        middle_back_kernel,
        grid=(wins,),
        in_specs=[window_spec(a, wins if a is co else 0) for a in windows] + [whole_spec(a) for a in fixed] + [ANY] * len(deps),
        out_specs=[window_spec(o) for o in outs] + [whole_spec(o) for o in sums],
        out_shape=[pltpu.HBM(o.shape, o.dtype) for o in outs + sums],
        scratch_shapes=[pltpu.VMEM(grads.shape, F32), pltpu.VMEM(grads.shape, F32)],
        compiler_params=params(28),
        cost_estimate=cost(12 * wins * toks * width * (width + 2 * hidden), wins * toks * (width * 16 + hidden * 4) + fm.size * 12),
        name="middle_back",
    )(*windows, *fixed, *deps)


def side_kernel(first_ref, dq_ref, dk_ref, dv_ref, do_ref):
    for c, ref in enumerate((dq_ref, dk_ref, dv_ref)):
        cols = ref.shape[1]
        part = sum(dot(flip(first_ref[w], 0), ref[w], 1, 1) for w in range(first_ref.shape[0]))
        do_ref[:, c * cols : (c + 1) * cols] = part.astype(BF)


def side_grads(first, grads):
    wins, width, toks = first.shape
    return pl.pallas_call(
        side_kernel,
        out_shape=jax.ShapeDtypeStruct((width, 3 * grads[0].shape[1]), BF),
        compiler_params=params(),
        cost_estimate=cost(0, 0),
        name="side_grads",
    )(first, *grads)


def back_kernel(place_ref, xm_ref, xo_ref, first_ref, qm_ref, km_ref, vm_ref, qo_ref, ko_ref, vo_ref, gm_ref, own_ref, got_ref, wm_ref, wo_ref, side_ref, nearm_ref, nearo_ref, farm_ref, faro_ref, keep_ref, send_ref, small_ref, acc):
    win = pl.program_id(0)

    @pl.when(win == 0)
    def _():
        acc[...] = side_ref[...].astype(F32)
        small_ref[...] = jnp.zeros_like(small_ref)

    xhat, inv = normed(jnp.concatenate([xm_ref[0], xo_ref[0]], 1).astype(F32))
    half = xm_ref.shape[2]
    mine = jnp.concatenate([qm_ref[0], km_ref[0], vm_ref[0]], 0)
    other = jnp.concatenate([qo_ref[0], ko_ref[0], vo_ref[0]], 0)
    acc[...] += dot(first_ref[0], mine, 1, 1)
    grad_first = dot(mine, wm_ref[...], 0, 1) + flip(dot(other, wo_ref[...], 0, 1))
    grad_first = grad_first.astype(BF).astype(F32)
    grad_x = gm_ref[0] + norm_back(grad_first, xhat, inv, row_pair(own_ref, got_ref, GAIN1))
    put_pieces(grad_x.astype(BF), nearm_ref, nearo_ref, farm_ref, faro_ref)
    ones = jnp.ones((8, mine.shape[1]), BF)
    for t, side in enumerate((mine, other)):
        sums = dot(ones, side, 1, 1)[0:1]
        span = slice(t * half, (t + 1) * half)
        small_ref[0:1, span] += sums[:, :half]
        small_ref[1:2, span] += sums[:, 2 * half :]
    small_ref[2:3, :] += jnp.sum(grad_first * xhat, 0, keepdims=True)
    small_ref[3:4, :] += jnp.sum(grad_first, 0, keepdims=True)

    @pl.when(win == pl.num_programs(0) - 1)
    def _():
        rows = keep_ref.shape[-2]
        own = place_ref[0]
        for i in range(keep_ref.shape[0]):
            for ref, side in ((keep_ref, own), (send_ref, 1 - own)):
                at = pl.multiple_of((2 * i + side) * rows, 16)
                ref[i] = acc[pl.ds(at, rows), :].astype(BF)


def back(place, blocks, xm, xo, first, mine, other, gm, own, got, wm, wo, side):
    wins, toks, half = xm.shape
    windows = (xm, xo, first) + mine + other + (gm,)
    fixed = (own, got, wm, wo, side)
    plain = jax.ShapeDtypeStruct((wins, SENT_OUT, half), BF)
    grads = jax.ShapeDtypeStruct((blocks // 2, 2 * half // blocks, wm.shape[1]), BF)
    small = jax.ShapeDtypeStruct((4, 2 * half), F32)
    outs = [plain] * 4 + [grads, grads, small]
    return pl.pallas_call(
        back_kernel,
        grid_spec=pltpu.PrefetchScalarGridSpec(
            num_scalar_prefetch=1,
            grid=(wins,),
            in_specs=[window_spec(a) for a in windows] + [whole_spec(a) for a in fixed],
            out_specs=[window_spec(plain)] * 4 + [whole_spec(grads), whole_spec(grads), whole_spec(small)],
            scratch_shapes=[pltpu.VMEM(wm.shape, F32)],
        ),
        out_shape=[pltpu.HBM(o.shape, o.dtype) for o in outs],
        compiler_params=params(),
        cost_estimate=cost(0, 0),
        name="back",
    )(place, *windows, *fixed)


def one_hot_rows(picks, size):
    cells = lax.broadcasted_iota(jnp.int32, (picks.shape[0], size), 1)
    return jnp.where(cells == picks, 1.0, 0.0).astype(BF)


def select_in_kernel(core_ref, picks_ref, x_ref, cot_ref, far_ref, xm_ref, cm_ref, other_ref):
    skip = WTOK - SENT_IN
    near = jnp.concatenate([jnp.concatenate([ref[w, skip:, :] for ref in (x_ref, cot_ref)], 1) for w in range(4)], 0)
    rows = far_ref.shape[0] // 2
    far = jnp.concatenate([far_ref[:rows, :], far_ref[rows:, :]], 1)
    low = dot(one_hot_rows(picks_ref[0, : 4 * SENT_IN, :], near.shape[0]), near, 1, 0)
    high = dot(one_hot_rows(picks_ref[0, 4 * SENT_IN :, :], far.shape[0]), far, 1, 0)
    places = lax.broadcasted_iota(jnp.int32, (SENT_IN - skip, 1), 0) + skip
    half = x_ref.shape[2]
    for w in range(4):
        first, last = low[w * SENT_IN : (w + 1) * SENT_IN], high[w * SENT_OUT : (w + 1) * SENT_OUT]
        over = jnp.where(places < HELD, first[skip:], last[: SENT_IN - skip])
        whole = jnp.concatenate([first[:skip], over, last[SENT_IN - skip :]], 0).astype(BF)
        if w < 2:
            xm_ref[w] = whole[:, :half]
            cm_ref[w] = whole[:, half:]
        else:
            other_ref[w - 2] = whole[:, :half]
            other_ref[w] = whole[:, half:]


def core_block(picks):
    return pl.BlockSpec((1,) + picks.shape[1:], lambda i, core: (core[0], 0, 0))


def select_in(core, picks, x, cot, far):
    out = jax.ShapeDtypeStruct((2, TOKS, x.shape[2]), BF)
    other = jax.ShapeDtypeStruct((4, TOKS, x.shape[2]), BF)
    return pl.pallas_call(
        select_in_kernel,
        grid_spec=pltpu.PrefetchScalarGridSpec(
            num_scalar_prefetch=1,
            grid=(1,),
            in_specs=[core_block(picks), whole_spec(x), whole_spec(cot), whole_spec(far)],
            out_specs=[whole_spec(out), whole_spec(out), whole_spec(other)],
        ),
        out_shape=[out, out, other],
        compiler_params=params(28),
        cost_estimate=cost(0, 0),
        name="select_in",
    )(core, picks, x, cot, far)


def select_out_kernel(core_ref, picks_ref, kept_ref, beside_ref, across_ref, corner_ref, out_ref):
    skip = WTOK - SENT_IN
    near = jnp.concatenate([kept_ref[...], beside_ref[...]], 0)
    far = jnp.concatenate([across_ref[...], corner_ref[...]], 0)
    low = dot(one_hot_rows(picks_ref[0, : 4 * SENT_IN, :], far.shape[0]), far, 1, 0)
    high = dot(one_hot_rows(picks_ref[0, 4 * SENT_IN :, :], near.shape[0]), near, 1, 0)
    rows = lax.broadcasted_iota(jnp.int32, (SENT_IN - skip, 1), 0) + skip
    for w in range(4):
        first, last = [part[w * SENT_IN : (w + 1) * SENT_IN] for part in (low, high)]
        out_ref[w, :skip, :] = first[:skip]
        out_ref[w, skip:SENT_IN, :] = jnp.where(rows < HELD, first[skip:], last[: SENT_IN - skip])
        out_ref[w, SENT_IN:, :] = last[SENT_IN - skip :]


def select_out(core, picks, arrays):
    out = jax.ShapeDtypeStruct((4, WTOK, arrays[0].shape[1]), F32)
    return pl.pallas_call(
        select_out_kernel,
        grid_spec=pltpu.PrefetchScalarGridSpec(
            num_scalar_prefetch=1,
            grid=(1,),
            in_specs=[core_block(picks)] + [whole_spec(a) for a in arrays],
            out_specs=whole_spec(out),
        ),
        out_shape=out,
        compiler_params=params(28),
        cost_estimate=cost(0, 0),
        name="select_out",
    )(core, picks, *arrays)


def bits_of(axis):
    return lax.axis_size(axis).bit_length() - 1


def bit_on(axis, bit):
    return lax.shift_right_logical(lax.axis_index(axis), bit) % 2


def swap(value, axis, bit=0):
    pairs = [(source, source ^ (1 << bit)) for source in range(lax.axis_size(axis))]
    return lax.ppermute(value, axis, pairs)


def bit_order():
    count = bits_of("shard")
    return list(range(count - 1, 0, -1)) + [0]


def row_place(bit):
    place = bit_on("shard", bit)
    if bit == bits_of("shard") - 1:
        place = jnp.bitwise_xor(place, lax.axis_index("tensor"))
    return place


def ordered(on, mine, other, axis):
    return jnp.concatenate((jnp.where(on, other, mine), jnp.where(on, mine, other)), axis)


def after(value, *deps):
    return lax.optimization_barrier((value,) + deps)[0]


def gather_start(part):
    rows, cols = part.shape
    return part.reshape((1,) * bits_of("shard") + (rows, cols))


def joint(values, deps):
    return lax.optimization_barrier(tuple(values) + tuple(deps))[: len(values)]


def gather_join(held, bit, got):
    return ordered(row_place(bit) == 1, held, got, bits_of("shard") - 1 - bit)


def gather_send(held, bits):
    for bit in bits[:-1]:
        held = gather_join(held, bit, swap(held, "shard", bit))
    return held, swap(held, "shard", bits[-1])


def choose(array, index, axis):
    return lax.dynamic_slice_in_dim(array, index, 1, axis)


def add_rounded(a, b):
    return (a.astype(F32) + b.astype(F32)).astype(BF)


def split_rows(part):
    count = bits_of("shard")
    return part.reshape((2,) * count + (part.shape[0] >> count, part.shape[1]))


def scatter_add(held, bit, got):
    axis = bits_of("shard") - 1 - bit
    return add_rounded(choose(held, row_place(bit), axis), got)


def scatter_send(held, bits):
    for bit in bits[:-1]:
        held = scatter_add(held, bit, scatter_send(held, (bit,))[1])
    axis = bits_of("shard") - 1 - bits[-1]
    return held, swap(choose(held, 1 - row_place(bits[-1]), axis), "shard", bits[-1])


def ctx_half(held, own):
    axis = held.ndim - 2
    half = held.shape[axis] // 2
    return lax.dynamic_slice_in_dim(held, own * half, half, axis)


def ctx_split_send(held):
    return swap(ctx_half(held, 1 - bit_on("ctx", 0)), "ctx")


def ctx_split_add(held, got):
    return add_rounded(ctx_half(held, bit_on("ctx", 0)), got)


def flat(held):
    return held.reshape(held.shape[-2:])


def ctx_send(held):
    held = flat(held)
    for bit in range(bits_of("ctx") - 1):
        held = add_rounded(held, swap(held, "ctx", bit))
    return held, swap(held, "ctx", bits_of("ctx") - 1)


def ctx_add(held, got):
    return held.astype(F32) + got.astype(F32)


def joint_swap(value, mask):
    size = lax.axis_size("shard") * lax.axis_size("ctx")
    return lax.ppermute(value, ("shard", "ctx"), [(i, i ^ mask) for i in range(size)])


def joint_parts(value, bits):
    value = value.astype(BF)
    low = 1 << bits[0]
    if len(bits) == 1:
        return [value, joint_swap(value, low), jnp.zeros_like(value), jnp.zeros_like(value)]
    high = 1 << bits[1]
    return [value, joint_swap(value, low), joint_swap(value, high), joint_swap(value, low | high)]


def add_parts(parts):
    a, b, c, d = [part.astype(F32) for part in parts]
    return (a + b) + (c + d)


def joint_groups():
    bits = list(range(bits_of("shard") + bits_of("ctx")))
    return [bits[i : i + 2] for i in range(0, len(bits), 2)]


def roll_axis(shaped, axis_pos, levels, backward):
    token_axis = 4 + axis_pos
    length = shaped.shape[token_axis]
    border = length - length // 2 if backward else length // 2
    before = lax.slice_in_dim(shaped, 0, border, axis=token_axis)
    after = lax.slice_in_dim(shaped, border, length, axis=token_axis)
    moving = after if backward else before
    if axis_pos < levels:
        moving = swap(moving, "ctx", levels - 1 - axis_pos)
    else:
        moving = jnp.roll(moving, 1 if backward else -1, axis=1 + axis_pos)
    return jnp.concatenate((moving, before) if backward else (after, moving), axis=token_axis)


def window_roll(windows, clips, counts, backward):
    shaped = windows.reshape((clips,) + counts + (WT, WH, WW, windows.shape[-1]))
    for axis_pos in range(3):
        shaped = roll_axis(shaped, axis_pos, bits_of("ctx"), backward)
    return shaped.reshape(windows.shape)


def frame_sources():
    source = np.zeros((4, HELD), np.int64)
    for h in range(2 * WH):
        for w in range(2 * WW):
            here = (h // WH) * 2 + w // WW
            there_h, there_w = (h + WH // 2) % (2 * WH), (w + WW // 2) % (2 * WW)
            there = (there_h // WH) * 2 + there_w // WW
            for a in range(WT // 2):
                row = (a * WH + h % WH) * WW + w % WW
                source[here, row] = there * HELD + (a * WH + there_h % WH) * WW + there_w % WW
    return source


def picks_in():
    source = frame_sources()
    there, row = source // HELD, source % HELD
    picks = np.full((4, TOKS), -1)
    picks[:, :HELD] = there * SENT_IN + row + SENT_IN - HELD
    picks[:, HELD:WTOK] = there * SENT_IN + row
    both = []
    for rows in (picks, np.concatenate((picks[2:], picks[:2]))):
        both.append(np.concatenate((rows[:, :SENT_IN].reshape(-1, 1), rows[:, WTOK - SENT_IN :].reshape(-1, 1))))
    return jnp.asarray(np.stack(both), jnp.int32)


def picks_out():
    place = np.argsort(frame_sources().reshape(-1)).reshape(4, HELD)
    there, row = place // HELD, place % HELD
    both = []
    for core in range(2):
        block = ((there // 2 + core) % 2) * 2 * SENT_OUT + (there % 2) * SENT_OUT
        picks = np.zeros((4, WTOK), np.int64)
        picks[:, HELD:] = block + row
        picks[:, :HELD] = block + row + HELD - (TOKS - SENT_OUT)
        both.append(np.concatenate((picks[:, :SENT_IN].reshape(-1, 1), picks[:, WTOK - SENT_IN :].reshape(-1, 1))))
    return jnp.asarray(np.stack(both), jnp.int32)


def plain_ring(clips):
    return bits_of("ctx") == 1 and clips == 1


def shift_start(arrays, clips):
    if plain_ring(clips):
        sent = jnp.concatenate([a[:, :SENT_IN] for a in arrays], 0)
        return swap(sent.reshape(-1, sent.shape[-1]), "ctx")
    return arrays[0][:1, :8]


def shift_in(arrays, got, clips, counts, core_row):
    if plain_ring(clips):
        xm, cm, other = select_in(core_row, picks_in(), *arrays, got)
        return xm, cm, swap(other, "tensor")
    half = arrays[0].shape[0] // 2
    core = lax.axis_index("tensor")
    mine, sent = [], []
    for array in arrays:
        moved = jnp.pad(window_roll(array, clips, counts, False), ((0, 0), (0, TOKS - WTOK), (0, 0)))
        mine.append(lax.dynamic_slice_in_dim(moved, core * half, half, 0))
        sent.append(lax.dynamic_slice_in_dim(moved, (1 - core) * half, half, 0))
    return mine[0], mine[1], swap(jnp.concatenate(sent, 0), "tensor")


def leave_start(pieces, clips):
    nearm, nearo, farm, faro = pieces
    width = nearm.shape[-1]
    if not plain_ring(clips):
        cut = TOKS - SENT_OUT
        mine, other = [jnp.concatenate((near[:, :cut], far), 1) for near, far in ((nearm, farm), (nearo, faro))]
        return mine, swap(other, "tensor")
    nearm, nearo, farm, faro = [piece.reshape(-1, width) for piece in pieces]
    corner = lax.ppermute(faro, ("ctx", "tensor"), [(i, i ^ 3) for i in range(4)])
    return nearm, swap(nearo, "tensor"), swap(farm, "ctx"), corner


def leave_end(parts, clips, counts, core_row, *deps):
    parts = (after(parts[0], *deps),) + tuple(parts[1:])
    if plain_ring(clips):
        return select_out(core_row, picks_out(), parts)
    windows = ordered(lax.axis_index("tensor") == 1, parts[0], parts[1], 0)
    return window_roll(windows[:, :WTOK], clips, counts, True).astype(F32)


def on_device(
    clip_input,
    cotangent,
    gain_one,
    shift_one,
    w_qkv,
    b_qv,
    w_proj,
    b_proj,
    bias_table,
    gain_two,
    shift_two,
    w_fc1,
    b_fc1,
    w_fc2,
    b_fc2,
    rel_index,
    regions,
):
    clips, window_count, tokens, half_width = clip_input.shape
    heads = bias_table.shape[0]
    levels = bits_of("ctx")
    counts = tuple(1 if axis_pos < levels else 2 for axis_pos in range(3))
    core = lax.axis_index("tensor")
    core_row = core.astype(jnp.int32).reshape(1)
    total_windows = clips * window_count
    held_windows = total_windows // 2
    scale = HD ** (-0.5)
    hidden = w_fc1.shape[1]

    own = pack(gain_one, shift_one, b_qv, b_proj, gain_two, shift_two, b_fc2, b_fc1, bias_table)
    qkv = gather_start(w_qkv.transpose(1, 0, 2).reshape(w_qkv.shape[1], -1))
    rest = gather_start(jnp.concatenate((w_proj.T, w_fc1, w_fc2.T), 1))
    index = jnp.pad(rel_index.T, ((0, TOKS - tokens), (0, TOKS - tokens)))
    index = lax.dynamic_slice_in_dim(index, core * (TOKS - HALF_ROWS), HALF_ROWS, 0)
    block = HALF_ROWS // ROWS
    cut = block // 2
    early_blocks = 5
    labels = jnp.tile(regions, (clips, 1))
    labels = lax.dynamic_slice_in_dim(labels, core * held_windows, held_windows, 0)
    labels = jnp.pad(labels, ((0, 0), (0, TOKS - tokens)))[:, None, :]

    order = bit_order()
    first, middle, last = order[0], order[1:-1], order[-1]
    clip_rows = clip_input.reshape(total_windows, tokens, half_width)
    cot_rows = cotangent.reshape(total_windows, tokens, half_width)

    pair_rows = (clip_rows, cot_rows)
    pair_got = shift_start(pair_rows, clips)
    qkv_got, own, index = joint((swap(qkv, "shard", first), own, index), ())
    got = swap(own, "tensor")
    qkv = gather_join(qkv, first, qkv_got)
    qkv, qkv_got = gather_send(qkv, middle)
    rest = after(rest, qkv)
    rest_got = swap(rest, "shard", first)
    part_own = lookup(after(index, qkv), own, got, heads, 0, early_blocks)
    qkv_got, pair_got, rest_got, part_own = joint((qkv_got, pair_got, rest_got, part_own), ())
    qkv = gather_join(qkv, middle[-1], qkv_got)
    rest = gather_join(rest, first, rest_got)
    rest, rest_got = gather_send(rest, middle)
    qkv_got = swap(qkv, "shard", last)
    xm, cm, other = shift_in(pair_rows, pair_got, clips, counts, core_row)
    bias_own = lookup(after(index, xm), own, got, heads, early_blocks, block - early_blocks, (part_own,))
    rest_got, qkv_got, other, bias_own = joint((rest_got, qkv_got, other, bias_own), ())
    qkv = gather_join(qkv, last, qkv_got)
    qkv = qkv.reshape(-1, qkv.shape[-1])
    qkv_other = swap(qkv, "tensor")
    rest = gather_join(rest, middle[-1], rest_got)
    rest_got = swap(rest, "shard", last)
    bias_got = swap(bias_own, "tensor")
    queries, keys, values, first_t = front(xm, other, own, got, qkv, qkv_other, scale * LOG2E, ())
    att, exact, lse = attend(core_row, queries, keys, values, labels, bias_own, bias_got)
    rest_got, att = joint((rest_got, att), ())
    edge = half_width + hidden
    early, late = [gather_join(rest[..., span], last, rest_got[..., span]) for span in (slice(0, edge), slice(edge, None))]
    early, late = [w.reshape(-1, w.shape[-1]) for w in (early, late)]
    early_other, late_other = swap(early, "tensor"), swap(late, "tensor")
    mid, second, act, slope = middle_forward(xm, other, att, own, got, early, early_other)
    *block_pieces, grad_mid, grad_att, one_mine, one_other, two_mine, two_other, small_mid, small_wide = middle_back(cm, other, mid, second, act, slope, att, own, got, early, early_other, late, late_other, ())

    order = order[::-1]
    twice = bits_of("ctx") == 1
    args = (core_row, queries, keys, values, labels, bias_own, bias_got)
    block_parts = leave_start(block_pieces, clips)
    one_got, two_got = swap(one_other, "tensor"), swap(two_other, "tensor")
    qo, ko, vo, pair_o, sent_o = attend_back(*args, exact, lse, grad_att, scale, 1)
    one_got, two_got, qo, sent_o, *moved = joint((one_got, two_got, qo, sent_o) + tuple(block_parts[1:]), ())
    block_parts = (block_parts[0],) + tuple(moved)
    one, two = split_rows(add_rounded(one_mine, one_got)), split_rows(add_rounded(two_mine, two_got))
    one_got = scatter_send(one, order[:1])[1]
    two_got = ctx_split_send(two) if twice else scatter_send(two, order[:1])[1]
    side = side_grads(first_t, (qo, ko, vo))
    side_got, sent_o = swap(side, "tensor"), swap(sent_o, "tensor")
    qm, km, vm, pair_m, sent_m = attend_back(*args, exact, lse, after(grad_att, side), scale, 0)
    one_got, two_got, side, sent_o, qm, sent_m = joint((one_got, two_got, side_got, sent_o, qm, sent_m), ())
    one = scatter_add(one, order[0], one_got)
    two = ctx_split_add(two, two_got) if twice else scatter_add(two, order[0], two_got)
    one_got = scatter_send(one, order[1:2])[1]
    two_bits = order if twice else order[1:]
    two_got = scatter_send(two, two_bits[:1])[1]
    sent_m = swap(sent_m, "tensor")
    place = row_place(0).astype(jnp.int32).reshape(1)
    *grad_pieces, qkv_grads, qkv_sent, small_end = back(place, lax.axis_size("shard"), xm, other, first_t, (after(qm, one, two), km, vm), (qo, ko, vo), grad_mid, own, got, qkv, qkv_other, side)
    block_out = leave_end(block_parts, clips, counts, core_row, small_end)
    one_got, two_got, sent_m, block_out = joint((one_got, two_got, sent_m, block_out), ())
    one = scatter_add(one, order[1], one_got)
    two = scatter_add(two, two_bits[0], two_got)
    shape = (2,) * (len(order) - 1) + (1,) + qkv_grads.shape[1:]
    qkv_got = swap(qkv_sent.reshape(shape), "shard", order[0])
    grad_parts = leave_start(grad_pieces, clips)
    two_got = scatter_send(two, two_bits[1:2])[1]
    one, one_got = scatter_send(one, order[2:])
    pairs = (pair_m, pair_o, sent_m, sent_o)
    (folded,) = fold(core_row, after(index, one, two), pairs, heads, 0, cut)
    qkv_got, two_got, one_got, folded, *moved = joint((qkv_got, two_got, one_got, folded) + tuple(grad_parts[1:]), ())
    grad_parts = (grad_parts[0],) + tuple(moved)
    qkv_grads = add_rounded(qkv_grads.reshape(shape), qkv_got)
    two = scatter_add(two, two_bits[1], two_got)
    one = scatter_add(one, order[-1], one_got)
    qkv_got = scatter_send(qkv_grads, order[1:2])[1]
    two, two_got = scatter_send(two, two_bits[2:])
    one, one_got = ctx_send(one)
    fold_mine, fold_other = fold(core_row, after(index, one, two, qkv_grads), pairs, heads, cut, block - cut, (folded, small_mid, small_wide, small_end))
    qkv_got, two_got, one_got, fold_mine, fold_other = joint((qkv_got, two_got, one_got, fold_mine, fold_other), ())
    small = fold_mine + swap(fold_other, "tensor")
    qkv_grads = scatter_add(qkv_grads, order[1], qkv_got)
    qkv_grads, qkv_got = scatter_send(qkv_grads, order[2:])
    two = scatter_add(two, two_bits[-1], two_got)
    two, two_got = (two, swap(two, "ctx")) if twice else ctx_send(two)
    groups = joint_groups()
    for group in groups[:-2]:
        small = add_parts(joint_parts(small, group))
    parts = joint_parts(small, groups[-2])
    grad_input = leave_end(grad_parts, clips, counts, core_row, small)
    *parts, grad_input = joint(tuple(parts) + (grad_input,), ())
    small = add_parts(parts)
    parts = joint_parts(small, groups[-1])
    qkv_got, two_got, one_got = joint((qkv_got, two_got, one_got), (small,))
    qkv_grads = scatter_add(qkv_grads, order[-1], qkv_got)
    qkv_grads, qkv_got = ctx_send(qkv_grads)
    one = ctx_add(one, one_got)
    two = flat(ordered(bit_on("ctx", 0) == 1, two, two_got, two.ndim - 2)).astype(F32) if twice else ctx_add(two, two_got)
    qkv_grads = ctx_add(qkv_grads, qkv_got)
    d_gain1, d_shift1, d_bqv, d_bp, d_table, d_gain2, d_shift2, d_b1, d_b2 = unpack(parts, heads)
    rows = w_fc1.shape[0]
    return (
        block_out.reshape(clip_input.shape),
        grad_input.reshape(clip_input.shape),
        d_gain1,
        d_shift1,
        qkv_grads.reshape(rows, 3, half_width).transpose(1, 0, 2),
        d_bqv,
        two[:, :half_width].T,
        d_bp,
        d_table,
        d_gain2,
        d_shift2,
        one,
        d_b1,
        two[:, half_width:].T,
        d_b2,
    )


def solution(mesh):
    in_specs = (
        P("shard", "ctx", None, "tensor"),
        P("shard", "ctx", None, "tensor"),
        P("tensor"),
        P("tensor"),
        P(None, "shard", "tensor"),
        P(None, "tensor"),
        P("tensor", "shard"),
        P("tensor"),
        P("tensor", None),
        P("tensor"),
        P("tensor"),
        P("shard", "tensor"),
        P("tensor"),
        P("tensor", "shard"),
        P("tensor"),
        P(),
        P("ctx", None),
    )
    out_specs = (
        P("shard", "ctx", None, "tensor"),
        P("shard", "ctx", None, "tensor"),
        P("tensor"),
        P("tensor"),
        P(None, "shard", "tensor"),
        P(None, "tensor"),
        P("tensor", "shard"),
        P("tensor"),
        P("tensor", None),
        P("tensor"),
        P("tensor"),
        P("shard", "tensor"),
        P("tensor"),
        P("tensor", "shard"),
        P("tensor"),
    )
    return jax.shard_map(
        on_device, mesh=mesh, in_specs=in_specs, out_specs=out_specs, check_vma=False
    )
```

```python
import functools

import jax
import jax.numpy as jnp
import numpy as np
from jax import lax
from jax.experimental import pallas as pl
from jax.experimental.pallas import tpu as pltpu
from jax.sharding import PartitionSpec as P

BF = jnp.bfloat16
F32 = jnp.float32
HD = 32
WT, WH, WW = 8, 7, 7
WTOK = WT * WH * WW
TOKS = 400
LANES = 512
HALF_ROWS = 208
TABLE = 2535
COARSE = 10
FINE = 256
ROWS = 16
GROUP = 4
BACK_GROUP = 2
EPSILON = 1e-05
HELD = WTOK // 2
SENT_IN = 200
SENT_OUT = 208
LOG2E = 1.4426950408889634
VECTOR_ROWS = 96
GAIN1, SHIFT1, BIAS_Q, BIAS_V, BIAS_P, GAIN2, SHIFT2, BIAS2, BIAS1 = range(80, 89)
ANY = pl.BlockSpec(memory_space=pl.ANY)


def dot(a, b, ca, cb):
    return lax.dot_general(a, b, (((ca,), (cb,)), ((), ())), preferred_element_type=F32)


def cost(flops, moved, trans=0):
    return pl.CostEstimate(flops=1, bytes_accessed=1, transcendentals=0)


def params(size=56):
    return pltpu.CompilerParams(vmem_limit_bytes=size * 1024 * 1024)


def whole_spec(array):
    rank = len(array.shape)
    return pl.BlockSpec(array.shape, lambda *_: (0,) * rank)


def window_spec(array, skip=0):
    rank = len(array.shape)
    return pl.BlockSpec((1,) + array.shape[1:], lambda w, *_: (w + skip,) + (0,) * (rank - 1))


def flip(values, axis=1):
    half = values.shape[axis] // 2
    low = lax.slice_in_dim(values, 0, half, axis=axis)
    high = lax.slice_in_dim(values, half, 2 * half, axis=axis)
    return jnp.concatenate([high, low], axis)


def row_pair(own_ref, got_ref, row, count=1):
    return jnp.concatenate([ref[r : r + 1, :] for ref in (own_ref, got_ref) for r in range(row, row + count)], 1)


def normed(values):
    width = values.shape[1]
    center = jnp.sum(values, 1, keepdims=True) / width
    spread = jnp.sum(values * values, 1, keepdims=True) / width - center * center
    inv = lax.rsqrt(spread + EPSILON)
    return (values - center) * inv, inv


def norm_back(upstream, xhat, inv, gain):
    width = xhat.shape[1]
    scaled = upstream * gain
    total = jnp.sum(scaled, 1, keepdims=True) / width
    along = jnp.sum(scaled * xhat, 1, keepdims=True) / width
    return inv * (scaled - total - xhat * along)


def pack_kernel(gain1, shift1, bqv, bp, gain2, shift2, b2, b1, table, out_ref):
    out_ref[...] = jnp.zeros_like(out_ref)
    heads = table.shape[0]
    for c in range(COARSE):
        size = min(FINE, TABLE - c * FINE)
        out_ref[c * heads : (c + 1) * heads, :size] = table[:, c * FINE : c * FINE + size]
    rows = ((GAIN1, gain1), (SHIFT1, shift1), (BIAS_P, bp), (GAIN2, gain2), (SHIFT2, shift2), (BIAS2, b2))
    for row, ref in rows:
        out_ref[row : row + 1, :] = ref[...].reshape(1, -1)
    out_ref[BIAS_Q : BIAS_Q + 2, :] = bqv[...]
    wide = b1[...].reshape(1, -1)
    for i in range(4):
        out_ref[BIAS1 + i : BIAS1 + i + 1, :] = wide[:, i * 256 : (i + 1) * 256]


def pack(*arrays):
    return pl.pallas_call(
        pack_kernel,
        out_shape=jax.ShapeDtypeStruct((VECTOR_ROWS, FINE), F32),
        cost_estimate=cost(1000, 200000),
        name="pack",
    )(*arrays)


def unpack_kernel(a_ref, b_ref, c_ref, d_ref, gain1, shift1, bqv, bp, table, gain2, shift2, b1, b2):
    a, b, c, d = [ref[...].astype(F32) for ref in (a_ref, b_ref, c_ref, d_ref)]
    total = (a + b) + (c + d)
    heads = table.shape[0]
    for c in range(COARSE):
        size = min(FINE, TABLE - c * FINE)
        table[:, c * FINE : c * FINE + size] = total[c * heads : (c + 1) * heads, :size]
    rows = ((GAIN1, gain1), (SHIFT1, shift1), (BIAS_P, bp), (GAIN2, gain2), (SHIFT2, shift2), (BIAS2, b2))
    for row, ref in rows:
        ref[...] = total[row : row + 1].reshape(-1)
    bqv[...] = total[BIAS_Q : BIAS_Q + 2]
    b1[...] = jnp.concatenate([total[BIAS1 + i : BIAS1 + i + 1] for i in range(4)], 1).reshape(-1)


def unpack(parts, heads):
    vector = jax.ShapeDtypeStruct((FINE,), F32)
    return pl.pallas_call(
        unpack_kernel,
        out_shape=[vector, vector, jax.ShapeDtypeStruct((2, FINE), F32), vector, jax.ShapeDtypeStruct((heads, TABLE), F32), vector, vector, jax.ShapeDtypeStruct((4 * FINE,), F32), vector],
        cost_estimate=cost(1000, 200000),
        name="unpack",
    )(*parts)


def lane_tiles(width):
    return [(t, t * 128, min(128, width - t * 128)) for t in range(-(-width // 128))]


def put_rows(scratch, start, rows):
    for t, begin, size in lane_tiles(rows.shape[1]):
        scratch[t, start : start + rows.shape[0], :size] = rows[:, begin : begin + size]


def strided_rows(scratch, start, count, step, width):
    parts = [scratch[t, pl.ds(start, count, stride=step), :][:, :size] for t, _, size in lane_tiles(width)]
    return jnp.concatenate(parts, 1)


def one_hot(fine_row, width):
    rows = lax.broadcasted_iota(jnp.int32, (FINE, width), 0).astype(jnp.int16)
    return jnp.where(rows == fine_row.astype(jnp.int16), jnp.ones((), BF), jnp.zeros((), BF))


def lookup_kernel(heads, idx_ref, own_ref, got_ref, *rest):
    out_ref, scratch, table = rest[-3:]
    width = idx_ref.shape[1]

    @pl.when(pl.program_id(0) == 0)
    def _():
        for c in range(COARSE):
            span = slice(c * heads, (c + 1) * heads)
            level_rows = jnp.concatenate([own_ref[span, :], got_ref[span, :]], 0)
            table[2 * c * heads : 2 * (c + 1) * heads, :] = (level_rows * LOG2E).astype(BF)

    for r in range(ROWS):
        idx = idx_ref[r : r + 1, :]
        hot = one_hot(jnp.bitwise_and(idx, FINE - 1), width)
        level = lax.shift_right_logical(idx, 8)
        picked = dot(table[...], hot, 1, 0)
        acc = picked[: 2 * heads]
        for c in range(1, COARSE):
            acc = jnp.where(level == c, picked[2 * c * heads : 2 * (c + 1) * heads], acc)
        put_rows(scratch, 2 * r * heads, acc)
    for h in range(2 * heads):
        out_ref[h, :, :width] = strided_rows(scratch, h, ROWS, 2 * heads, width).astype(BF)


def lookup(idx, own, got, heads, start, count, filled=()):
    width = idx.shape[1]
    return pl.pallas_call(
        functools.partial(lookup_kernel, heads),
        grid=(count,),
        in_specs=[pl.BlockSpec((ROWS, width), lambda i: (start + i, 0)), whole_spec(own), whole_spec(got)] + [ANY] * len(filled),
        out_specs=pl.BlockSpec((2 * heads, ROWS, LANES), lambda i: (0, start + i, 0)),
        out_shape=jax.ShapeDtypeStruct((2 * heads, HALF_ROWS, LANES), BF),
        input_output_aliases={3: 0} if filled else {},
        scratch_shapes=[pltpu.VMEM((-(-width // 128), 2 * ROWS * heads, 128), F32), pltpu.VMEM((2 * COARSE * heads, FINE), BF)],
        compiler_params=params(),
        cost_estimate=cost(0, 0),
        name="table_lookup",
    )(idx, own, got, *filled)


def fold_rows(heads, idx_ref, pair_m, pair_o, sent_m, sent_o, scratch, total):
    width = idx_ref.shape[1]
    for h in range(heads):
        put_rows(scratch, h * ROWS, pair_m[h, :, :width].astype(F32) + sent_o[h, :, :width].astype(F32))
        put_rows(scratch, (heads + h) * ROWS, pair_o[h, :, :width].astype(F32) + sent_m[h, :, :width].astype(F32))
    part = jnp.zeros(total.shape, F32)
    fine = jnp.bitwise_and(idx_ref[...], FINE - 1).T.astype(jnp.int16)
    cells = lax.broadcasted_iota(jnp.int32, (width, FINE), 1).astype(jnp.int16)
    for r in range(ROWS):
        hot = jnp.where(cells == fine[:, r : r + 1], jnp.ones((), BF), jnp.zeros((), BF))
        level = lax.shift_right_logical(idx_ref[r : r + 1, :], 8)
        grads = strided_rows(scratch, r, 2 * heads, ROWS, width)
        parts = [jnp.where(level == c, grads, 0.0) for c in range(COARSE)]
        part = part + dot(jnp.concatenate(parts, 0).astype(BF), hot, 1, 0)
    total[...] += part


def fold_start_kernel(heads, core_ref, idx_ref, pair_m, pair_o, sent_m, sent_o, total, scratch):
    step = pl.program_id(0)

    @pl.when(step == 0)
    def _():
        total[...] = jnp.zeros_like(total)

    @pl.when(jnp.logical_or(step > 0, core_ref[0] == 0))
    def _():
        fold_rows(heads, idx_ref, pair_m, pair_o, sent_m, sent_o, scratch, total)


def fold_end_kernel(heads, core_ref, idx_ref, pair_m, pair_o, sent_m, sent_o, init_ref, mid_ref, wide_ref, end_ref, mine_ref, other_ref, scratch, total):
    step = pl.program_id(0)

    @pl.when(step == 0)
    def _():
        total[...] = init_ref[...]

    fold_rows(heads, idx_ref, pair_m, pair_o, sent_m, sent_o, scratch, total)

    @pl.when(step == pl.num_programs(0) - 1)
    def _():
        for half, ref in enumerate((mine_ref, other_ref)):
            for c in range(COARSE):
                at = (2 * c + half) * heads
                ref[c * heads : (c + 1) * heads, :] = total[at : at + heads, :]
            span = slice(half * 256, (half + 1) * 256)
            rows = ((GAIN1, end_ref, 2), (SHIFT1, end_ref, 3), (BIAS_Q, end_ref, 0), (BIAS_V, end_ref, 1), (BIAS_P, mid_ref, 3), (GAIN2, mid_ref, 1), (SHIFT2, mid_ref, 2), (BIAS2, mid_ref, 0))
            for row, source, at in rows:
                ref[row : row + 1, :] = source[at : at + 1, span]
            for i in range(4):
                at = half * 1024 + i * 256
                ref[BIAS1 + i : BIAS1 + i + 1, :] = wide_ref[:, at : at + 256]
            ref[BIAS1 + 4 :, :] = jnp.zeros((VECTOR_ROWS - BIAS1 - 4, 256), F32)


def fold(core, idx, pairs, heads, start, count, extra=()):
    width = idx.shape[1]
    scratch = [pltpu.VMEM((-(-width // 128), 2 * ROWS * heads, 128), F32)]
    total = jax.ShapeDtypeStruct((2 * COARSE * heads, FINE), F32)
    ends = jax.ShapeDtypeStruct((VECTOR_ROWS, FINE), F32)
    outs = [ends, ends] if extra else [total]
    pair = pl.BlockSpec((heads, ROWS, LANES), lambda i, core: (0, start + i, 0))
    return pl.pallas_call(
        functools.partial(fold_end_kernel if extra else fold_start_kernel, heads),
        grid_spec=pltpu.PrefetchScalarGridSpec(
            num_scalar_prefetch=1,
            grid=(count,),
            in_specs=[pl.BlockSpec((ROWS, width), lambda i, core: (start + i, 0))] + [pair] * 4 + [whole_spec(e) for e in extra],
            out_specs=[whole_spec(o) for o in outs],
            scratch_shapes=scratch + ([pltpu.VMEM(total.shape, F32)] if extra else []),
        ),
        out_shape=outs,
        compiler_params=params(),
        cost_estimate=cost(0, 0),
        name="table_fold",
    )(core, idx, *pairs, *extra)


def mask_pieces():
    pieces = []
    rest = np.float32(-100.0 * LOG2E)
    for _ in range(3):
        piece = np.float32(rest.astype(jnp.bfloat16))
        pieces.append(float(piece))
        rest = np.float32(rest - piece)
    return pieces


def region_rows(label):
    width = label.shape[1]
    rows = lax.broadcasted_iota(jnp.int32, (16, width), 0)
    lanes = lax.broadcasted_iota(jnp.int32, (16, width), 1)
    same = jnp.bitwise_and(rows, 3) == label
    level = lax.shift_right_logical(rows, 2)
    high, mid, low = mask_pieces()
    piece = jnp.where(level == 0, high, jnp.where(level == 1, mid, low))
    queries = jnp.where(rows < 12, jnp.where(same, 1.0, 0.0), jnp.where(rows == 15, 1.0, 0.0))
    past = jnp.where(jnp.logical_and(rows == 15, lanes >= WTOK), -1e30, 0.0)
    keys = jnp.where(rows < 12, jnp.where(same, 0.0, piece), past)
    return queries.astype(BF), keys.astype(BF)


def pick_bias(first, own_ref, got_ref, j):
    skip = 2 * HALF_ROWS - TOKS
    low = lax.select_n(first, got_ref[j, :, :TOKS], own_ref[j, :, :TOKS])
    high = lax.select_n(first, own_ref[j, skip:, :TOKS], got_ref[j, skip:, :TOKS])
    return jnp.concatenate([low, high], 0).astype(F32)


def attend_kernel(core_ref, q_ref, k_ref, v_ref, label_ref, own_ref, got_ref, att_ref, exact_ref, lse_ref):
    first = core_ref[0] == 0
    ones = jnp.ones((16, TOKS), BF)
    windows = range(q_ref.shape[0])
    regions = [region_rows(label_ref[w]) for w in windows]
    for j in range(GROUP):
        part = pl.ds(j * HD, HD)
        bias = pick_bias(first, own_ref, got_ref, j)
        for w in windows:
            query_rows, key_rows = regions[w]
            qa = jnp.concatenate([q_ref[w, part, :], query_rows], 0)
            ka = jnp.concatenate([k_ref[w, part, :], key_rows], 0)
            va = jnp.concatenate([v_ref[w, part, :], ones], 0)
            scores = dot(ka, qa, 0, 0) + bias
            peak = jnp.max(scores, 0, keepdims=True)
            weights = jnp.exp2(scores - peak).astype(BF)
            mixed = dot(va, weights, 1, 0)
            total = mixed[HD : HD + 1]
            out = mixed[:HD] / total
            att_ref[w, part, :] = out.astype(BF)
            exact_ref[w, part, :] = out
            lse_ref[w, 0, j : j + 1, :] = peak + jnp.log2(total)


def attention_specs(wins, heads, skip=0, group=GROUP):
    half = heads // (2 * group)
    ratio = GROUP // group
    feat = pl.BlockSpec((wins, group * HD, TOKS), lambda h, core: (0, h + skip, 0))
    label = pl.BlockSpec((wins, 1, TOKS), lambda h, core: (0, 0, 0))
    own = pl.BlockSpec((group, HALF_ROWS, LANES), lambda h, core: (h + skip, 0, 0))
    got = pl.BlockSpec((group, HALF_ROWS, LANES), lambda h, core: ((h + skip + half) % (2 * half), 0, 0))
    stat = pl.BlockSpec((wins, 1, GROUP, TOKS), lambda h, core: (0, (h + skip) // ratio, 0, 0))
    return feat, label, own, got, stat


def attend(core, q, k, v, labels, own, got):
    wins, feats, toks = q.shape
    heads = feats // HD
    feat, label, own_spec, got_spec, stat = attention_specs(wins, heads)
    return pl.pallas_call(
        attend_kernel,
        grid_spec=pltpu.PrefetchScalarGridSpec(
            num_scalar_prefetch=1,
            grid=(heads // GROUP,),
            in_specs=[feat, feat, feat, label, own_spec, got_spec],
            out_specs=[feat, feat, stat],
        ),
        out_shape=[
            jax.ShapeDtypeStruct(q.shape, BF),
            jax.ShapeDtypeStruct(q.shape, F32),
            jax.ShapeDtypeStruct((wins, heads // GROUP, GROUP, toks), F32),
        ],
        compiler_params=params(),
        cost_estimate=cost(0, 0),
        name="attend",
    )(core, q, k, v, labels, own, got)


def split3(row):
    hi = row.astype(BF)
    rest = row - hi.astype(F32)
    mid = rest.astype(BF)
    return hi.astype(F32), mid.astype(F32), rest - mid.astype(F32)


def rows16(parts, width):
    rows = lax.broadcasted_iota(jnp.int32, (16, width), 0)
    out = jnp.zeros((16, width), F32)
    for i, part in enumerate(parts):
        out = jnp.where(rows == i, part, out)
    return out.astype(BF)


def attend_back_kernel(scale, core_ref, q_ref, k_ref, v_ref, label_ref, own_ref, got_ref, exact_ref, lse_ref, g_ref, dq_ref, dk_ref, dv_ref, pair_ref, sent_ref, sums):
    core = core_ref[0]
    first = core == 0
    step = TOKS - HALF_ROWS
    mine, other = pl.multiple_of(core * step, 8), pl.multiple_of((1 - core) * step, 8)
    minus = rows16([-1.0, -1.0, -1.0], TOKS)
    windows = range(q_ref.shape[0])
    regions = [region_rows(label_ref[w]) for w in windows]
    base = lax.rem(pl.program_id(0), GROUP // BACK_GROUP) * BACK_GROUP
    for j in range(BACK_GROUP):
        part = pl.ds(j * HD, HD)
        bias = pick_bias(first, own_ref, got_ref, j)
        total = None
        for w in windows:
            query_rows, key_rows = regions[w]
            q = q_ref[w, part, :]
            k = k_ref[w, part, :]
            g = g_ref[w, part, :]
            qa = jnp.concatenate([q, query_rows, rows16(split3(lse_ref[w, 0, pl.ds(base + j, 1), :]), TOKS)], 0)
            ka = jnp.concatenate([k, key_rows, minus], 0)
            va = jnp.concatenate([v_ref[w, part, :], minus], 0)
            along = jnp.sum(g.astype(F32) * exact_ref[w, part, :], 0, keepdims=True)
            ga = jnp.concatenate([g, rows16(split3(along), TOKS)], 0)
            probs = jnp.exp2(dot(ka, qa, 0, 0) + bias)
            wide = probs * dot(va, ga, 0, 0)
            grads = wide.astype(BF)
            low = probs.astype(BF)
            dv_ref[w, part, :] = dot(g, low, 1, 1).astype(BF)
            dk_ref[w, part, :] = (dot(q, grads, 1, 1) * (1.0 / LOG2E)).astype(BF)
            dq_ref[w, part, :] = (dot(k, grads, 1, 0) * scale).astype(BF)
            total = wide if total is None else total + wide
        sums[...] = total
        pair_ref[j, :, :TOKS] = sums[pl.ds(mine, HALF_ROWS), :].astype(BF)
        sent_ref[j, :, :TOKS] = sums[pl.ds(other, HALF_ROWS), :].astype(BF)


def attend_back(core, q, k, v, labels, own, got, exact, lse, g, scale, side):
    wins, feats, toks = q.shape
    heads = feats // HD
    blocks = heads // (2 * BACK_GROUP)
    feat, label, own_spec, got_spec, stat = attention_specs(wins, heads, side * blocks, BACK_GROUP)
    out = pl.BlockSpec((wins, BACK_GROUP * HD, toks), lambda h, core: (0, h, 0))
    pair = pl.BlockSpec((BACK_GROUP, HALF_ROWS, LANES), lambda h, core: (h, 0, 0))
    return pl.pallas_call(
        functools.partial(attend_back_kernel, scale),
        grid_spec=pltpu.PrefetchScalarGridSpec(
            num_scalar_prefetch=1,
            grid=(blocks,),
            in_specs=[feat, feat, feat, label, own_spec, got_spec, feat, stat, feat],
            out_specs=[out, out, out, pair, pair],
            scratch_shapes=[pltpu.VMEM((toks, toks), F32)],
        ),
        out_shape=[jax.ShapeDtypeStruct((wins, feats // 2, toks), BF)] * 3 + [jax.ShapeDtypeStruct((heads // 2, HALF_ROWS, LANES), BF)] * 2,
        compiler_params=params(),
        cost_estimate=cost(0, 0),
        name="attend_back",
    )(core, q, k, v, labels, own, got, exact, lse, g)


def front_kernel(scale, xm_ref, xo_ref, own_ref, got_ref, wm_ref, wo_ref, *rest):
    q_ref, k_ref, v_ref, first_ref = rest[-4:]
    x = jnp.concatenate([xm_ref[0], xo_ref[0]], 1).astype(F32)
    xhat, _ = normed(x)
    first = (xhat * row_pair(own_ref, got_ref, GAIN1) + row_pair(own_ref, got_ref, SHIFT1)).astype(BF)
    first_ref[0] = first.T
    for t, (w_ref, vec_ref) in enumerate(((wm_ref, own_ref), (wo_ref, got_ref))):
        cols = w_ref.shape[1] // 3
        rows = pl.ds(t * cols, cols)
        made = dot(first if t == 0 else flip(first), w_ref[...], 1, 0)
        q = (made[:, :cols] + vec_ref[BIAS_Q : BIAS_Q + 1, :]) * scale
        v = made[:, 2 * cols :] + vec_ref[BIAS_V : BIAS_V + 1, :]
        q_ref[0, rows, :] = q.astype(BF).T
        k_ref[0, rows, :] = made[:, cols : 2 * cols].astype(BF).T
        v_ref[0, rows, :] = v.astype(BF).T


def front(xm, xo, own, got, wm, wo, scale, deps):
    wins, toks, half = xm.shape
    out = jax.ShapeDtypeStruct((wins, 2 * (wm.shape[1] // 3), toks), BF)
    return pl.pallas_call(
        functools.partial(front_kernel, scale),
        grid=(wins,),
        in_specs=[window_spec(xm), window_spec(xo), whole_spec(own), whole_spec(got), whole_spec(wm), whole_spec(wo)] + [ANY] * len(deps),
        out_specs=[window_spec(out)] * 4,
        out_shape=[out] * 4,
        compiler_params=params(),
        cost_estimate=cost(8 * wins * toks * half * wm.shape[1], wins * toks * half * 16 + wm.size * 4),
        name="front",
    )(xm, xo, own, got, wm, wo, *deps)


def middle_kernel(xm_ref, xo_ref, att_ref, own_ref, got_ref, wm_ref, wo_ref, *rest):
    mid_ref, second_ref, act_ref, slope_ref = rest[-4:]
    half = xm_ref.shape[2]
    wide = wm_ref.shape[1] - half
    branch = dot(att_ref[0, :half, :].T, wm_ref[:, :half], 1, 1) + flip(dot(att_ref[0, half:, :].T, wo_ref[:, :half], 1, 1))
    x = jnp.concatenate([xm_ref[0], xo_ref[0]], 1).astype(F32)
    middle = x + (branch + row_pair(own_ref, got_ref, BIAS_P))
    mid_ref[0] = middle
    xhat, _ = normed(middle)
    second = (xhat * row_pair(own_ref, got_ref, GAIN2) + row_pair(own_ref, got_ref, SHIFT2)).astype(BF)
    second_ref[0] = second
    turned = flip(second)
    for t, (w_ref, vec_ref) in enumerate(((wm_ref, own_ref), (wo_ref, got_ref))):
        for s in range(0, wide, 256):
            at = t * wide + s
            bias = vec_ref[BIAS1 + s // 256 : BIAS1 + s // 256 + 1, :]
            hidden = dot(second if t == 0 else turned, w_ref[:, half + s : half + s + 256], 1, 0) + bias
            phi = 0.5 + 0.5 * lax.erf(hidden * (0.5**0.5))
            bell = jnp.exp2(hidden * hidden * (-0.5 * LOG2E)) * (1.0 / (2.0 * np.pi) ** 0.5)
            act_ref[0, :, at : at + 256] = (hidden * phi).astype(BF)
            slope_ref[0, :, at : at + 256] = (phi + hidden * bell).astype(BF)


def middle_forward(xm, xo, att, own, got, wm, wo):
    wins, toks, half = xm.shape
    width = 2 * half
    hidden = 2 * (wm.shape[1] - half)
    wide = jax.ShapeDtypeStruct((wins, toks, hidden), BF)
    outs = [jax.ShapeDtypeStruct((wins, toks, width), F32), jax.ShapeDtypeStruct((wins, toks, width), BF), wide, wide]
    fixed = (own, got, wm, wo)
    return pl.pallas_call(
        middle_kernel,
        grid=(wins,),
        in_specs=[window_spec(a) for a in (xm, xo, att)] + [whole_spec(a) for a in fixed],
        out_specs=[window_spec(o) for o in outs],
        out_shape=outs,
        compiler_params=params(28),
        cost_estimate=cost(8 * wins * toks * width * wm.shape[1], wins * toks * (width * 10 + hidden * 4) + wm.size * 4, wins * toks * hidden),
        name="middle_forward",
    )(xm, xo, att, *fixed)


def put_pieces(out, nearm_ref, nearo_ref, farm_ref, faro_ref):
    half = out.shape[1] // 2
    for ref, rows, cols in ((nearm_ref, 0, 0), (nearo_ref, 0, half), (farm_ref, TOKS - SENT_OUT, 0), (faro_ref, TOKS - SENT_OUT, half)):
        ref[0] = out[rows : rows + SENT_OUT, cols : cols + half]


def middle_back_kernel(cm_ref, co_ref, mid_ref, second_ref, act_ref, slope_ref, att_ref, own_ref, got_ref, wm_ref, wo_ref, fm_ref, fo_ref, *rest):
    nearm_ref, nearo_ref, farm_ref, faro_ref, gm_ref, gr_ref, onem_ref, oneo_ref, twom_ref, twoo_ref, small_ref, wide_ref, accm, acco = rest[-14:]
    win = pl.program_id(0)
    half = cm_ref.shape[2]
    wide = fm_ref.shape[1]

    @pl.when(win == 0)
    def _():
        accm[...] = jnp.zeros_like(accm)
        acco[...] = jnp.zeros_like(acco)
        small_ref[...] = jnp.zeros_like(small_ref)
        wide_ref[...] = jnp.zeros_like(wide_ref)

    cot = jnp.concatenate([cm_ref[0], co_ref[0]], 1)
    cot_turned = flip(cot)
    cot_t = cot.T
    second_t = second_ref[0].T
    sides = (
        (wm_ref, fm_ref, accm, cot, cot_t, second_t),
        (wo_ref, fo_ref, acco, cot_turned, flip(cot_t, 0), flip(second_t, 0)),
    )
    made, pulled = [], []
    for t, (w_ref, f_ref, acc, c, c_t, s_t) in enumerate(sides):
        forward = jnp.zeros(cot.shape, F32)
        grad_second = jnp.zeros(cot.shape, F32)
        for s in range(0, wide, 512):
            span = slice(t * wide + s, t * wide + s + 512)
            fc2 = f_ref[:, s : s + 512]
            active = act_ref[0, :, span]
            forward = forward + dot(active, fc2, 1, 1)
            grad = (dot(c, fc2, 1, 0) * slope_ref[0, :, span].astype(F32)).astype(BF)
            wide_ref[:, span] += jnp.sum(grad.astype(F32), 0, keepdims=True)
            acc[:, half + wide + s : half + wide + s + 512] += dot(c_t, active, 1, 0)
            acc[:, half + s : half + s + 512] += dot(s_t, grad, 1, 0)
            grad_second = grad_second + dot(grad, w_ref[:, half + s : half + s + 512], 1, 1)
        made.append(forward)
        pulled.append(grad_second)
    out = mid_ref[0] + (made[0] + flip(made[1]) + row_pair(own_ref, got_ref, BIAS2))
    put_pieces(out.astype(BF), nearm_ref, nearo_ref, farm_ref, faro_ref)
    grad_second = pulled[0] + flip(pulled[1])
    upstream = cot.astype(F32)
    xhat, inv = normed(mid_ref[0])
    grad_mid = upstream + norm_back(grad_second, xhat, inv, row_pair(own_ref, got_ref, GAIN2))
    gm_ref[0] = grad_mid
    branch = grad_mid.astype(BF)
    branch_t = branch.T
    gr_ref[0, :half, :] = dot(branch, wm_ref[:, :half], 1, 0).astype(BF).T
    gr_ref[0, half:, :] = dot(flip(branch), wo_ref[:, :half], 1, 0).astype(BF).T
    accm[:, :half] += dot(branch_t, att_ref[0, :half, :], 1, 1)
    acco[:, :half] += dot(flip(branch_t, 0), att_ref[0, half:, :], 1, 1)
    small_ref[0:1, :] += jnp.sum(upstream, 0, keepdims=True)
    small_ref[1:2, :] += jnp.sum(grad_second * xhat, 0, keepdims=True)
    small_ref[2:3, :] += jnp.sum(grad_second, 0, keepdims=True)
    small_ref[3:4, :] += jnp.sum(branch.astype(F32), 0, keepdims=True)

    @pl.when(win == pl.num_programs(0) - 1)
    def _():
        for acc, one_ref, two_ref in ((accm, onem_ref, twom_ref), (acco, oneo_ref, twoo_ref)):
            one_ref[...] = acc[:, half : half + wide].astype(BF)
            two_ref[:, :half] = acc[:, :half].astype(BF)
            two_ref[:, half:] = acc[:, half + wide :].astype(BF)


def middle_back(cm, co, mid, second, act, slope, att, own, got, wm, wo, fm, fo, deps):
    wins, toks, half = cm.shape
    width = 2 * half
    hidden = act.shape[2]
    windows = (cm, co, mid, second, act, slope, att)
    fixed = (own, got, wm, wo, fm, fo)
    plain = jax.ShapeDtypeStruct((wins, SENT_OUT, half), BF)
    outs = [plain, plain, plain, plain, jax.ShapeDtypeStruct(mid.shape, F32), jax.ShapeDtypeStruct((wins, width, toks), BF)]
    grads = jax.ShapeDtypeStruct((width, wm.shape[1] + fm.shape[1]), BF)
    one = jax.ShapeDtypeStruct((width, wm.shape[1] - half), BF)
    two = jax.ShapeDtypeStruct((width, half + fm.shape[1]), BF)
    sums = [one, one, two, two, jax.ShapeDtypeStruct((4, width), F32), jax.ShapeDtypeStruct((1, hidden), F32)]
    return pl.pallas_call(
        middle_back_kernel,
        grid=(wins,),
        in_specs=[window_spec(a, wins if a is co else 0) for a in windows] + [whole_spec(a) for a in fixed] + [ANY] * len(deps),
        out_specs=[window_spec(o) for o in outs] + [whole_spec(o) for o in sums],
        out_shape=[pltpu.HBM(o.shape, o.dtype) for o in outs + sums],
        scratch_shapes=[pltpu.VMEM(grads.shape, F32), pltpu.VMEM(grads.shape, F32)],
        compiler_params=params(28),
        cost_estimate=cost(12 * wins * toks * width * (width + 2 * hidden), wins * toks * (width * 16 + hidden * 4) + fm.size * 12),
        name="middle_back",
    )(*windows, *fixed, *deps)


def side_kernel(first_ref, dq_ref, dk_ref, dv_ref, do_ref):
    for c, ref in enumerate((dq_ref, dk_ref, dv_ref)):
        cols = ref.shape[1]
        part = sum(dot(flip(first_ref[w], 0), ref[w], 1, 1) for w in range(first_ref.shape[0]))
        do_ref[:, c * cols : (c + 1) * cols] = part.astype(BF)


def side_grads(first, grads):
    wins, width, toks = first.shape
    return pl.pallas_call(
        side_kernel,
        out_shape=jax.ShapeDtypeStruct((width, 3 * grads[0].shape[1]), BF),
        compiler_params=params(),
        cost_estimate=cost(0, 0),
        name="side_grads",
    )(first, *grads)


def back_kernel(place_ref, xm_ref, xo_ref, first_ref, qm_ref, km_ref, vm_ref, qo_ref, ko_ref, vo_ref, gm_ref, own_ref, got_ref, wm_ref, wo_ref, side_ref, nearm_ref, nearo_ref, farm_ref, faro_ref, keep_ref, send_ref, small_ref, acc):
    win = pl.program_id(0)

    @pl.when(win == 0)
    def _():
        acc[...] = side_ref[...].astype(F32)
        small_ref[...] = jnp.zeros_like(small_ref)

    xhat, inv = normed(jnp.concatenate([xm_ref[0], xo_ref[0]], 1).astype(F32))
    half = xm_ref.shape[2]
    mine = jnp.concatenate([qm_ref[0], km_ref[0], vm_ref[0]], 0)
    other = jnp.concatenate([qo_ref[0], ko_ref[0], vo_ref[0]], 0)
    acc[...] += dot(first_ref[0], mine, 1, 1)
    grad_first = dot(mine, wm_ref[...], 0, 1) + flip(dot(other, wo_ref[...], 0, 1))
    grad_first = grad_first.astype(BF).astype(F32)
    grad_x = gm_ref[0] + norm_back(grad_first, xhat, inv, row_pair(own_ref, got_ref, GAIN1))
    put_pieces(grad_x.astype(BF), nearm_ref, nearo_ref, farm_ref, faro_ref)
    ones = jnp.ones((8, mine.shape[1]), BF)
    for t, side in enumerate((mine, other)):
        sums = dot(ones, side, 1, 1)[0:1]
        span = slice(t * half, (t + 1) * half)
        small_ref[0:1, span] += sums[:, :half]
        small_ref[1:2, span] += sums[:, 2 * half :]
    small_ref[2:3, :] += jnp.sum(grad_first * xhat, 0, keepdims=True)
    small_ref[3:4, :] += jnp.sum(grad_first, 0, keepdims=True)

    @pl.when(win == pl.num_programs(0) - 1)
    def _():
        rows = keep_ref.shape[-2]
        own = place_ref[0]
        for i in range(keep_ref.shape[0]):
            for ref, side in ((keep_ref, own), (send_ref, 1 - own)):
                at = pl.multiple_of((2 * i + side) * rows, 16)
                ref[i] = acc[pl.ds(at, rows), :].astype(BF)


def back(place, blocks, xm, xo, first, mine, other, gm, own, got, wm, wo, side):
    wins, toks, half = xm.shape
    windows = (xm, xo, first) + mine + other + (gm,)
    fixed = (own, got, wm, wo, side)
    plain = jax.ShapeDtypeStruct((wins, SENT_OUT, half), BF)
    grads = jax.ShapeDtypeStruct((blocks // 2, 2 * half // blocks, wm.shape[1]), BF)
    small = jax.ShapeDtypeStruct((4, 2 * half), F32)
    outs = [plain] * 4 + [grads, grads, small]
    return pl.pallas_call(
        back_kernel,
        grid_spec=pltpu.PrefetchScalarGridSpec(
            num_scalar_prefetch=1,
            grid=(wins,),
            in_specs=[window_spec(a) for a in windows] + [whole_spec(a) for a in fixed],
            out_specs=[window_spec(plain)] * 4 + [whole_spec(grads), whole_spec(grads), whole_spec(small)],
            scratch_shapes=[pltpu.VMEM(wm.shape, F32)],
        ),
        out_shape=[pltpu.HBM(o.shape, o.dtype) for o in outs],
        compiler_params=params(),
        cost_estimate=cost(0, 0),
        name="back",
    )(place, *windows, *fixed)


def one_hot_rows(picks, size):
    cells = lax.broadcasted_iota(jnp.int32, (picks.shape[0], size), 1)
    return jnp.where(cells == picks, 1.0, 0.0).astype(BF)


def select_in_kernel(core_ref, picks_ref, x_ref, cot_ref, far_ref, xm_ref, cm_ref, other_ref):
    skip = WTOK - SENT_IN
    near = jnp.concatenate([jnp.concatenate([ref[w, skip:, :] for ref in (x_ref, cot_ref)], 1) for w in range(4)], 0)
    rows = far_ref.shape[0] // 2
    far = jnp.concatenate([far_ref[:rows, :], far_ref[rows:, :]], 1)
    low = dot(one_hot_rows(picks_ref[0, : 4 * SENT_IN, :], near.shape[0]), near, 1, 0)
    high = dot(one_hot_rows(picks_ref[0, 4 * SENT_IN :, :], far.shape[0]), far, 1, 0)
    places = lax.broadcasted_iota(jnp.int32, (SENT_IN - skip, 1), 0) + skip
    half = x_ref.shape[2]
    for w in range(4):
        first, last = low[w * SENT_IN : (w + 1) * SENT_IN], high[w * SENT_OUT : (w + 1) * SENT_OUT]
        over = jnp.where(places < HELD, first[skip:], last[: SENT_IN - skip])
        whole = jnp.concatenate([first[:skip], over, last[SENT_IN - skip :]], 0).astype(BF)
        if w < 2:
            xm_ref[w] = whole[:, :half]
            cm_ref[w] = whole[:, half:]
        else:
            other_ref[w - 2] = whole[:, :half]
            other_ref[w] = whole[:, half:]


def core_block(picks):
    return pl.BlockSpec((1,) + picks.shape[1:], lambda i, core: (core[0], 0, 0))


def select_in(core, picks, x, cot, far):
    out = jax.ShapeDtypeStruct((2, TOKS, x.shape[2]), BF)
    other = jax.ShapeDtypeStruct((4, TOKS, x.shape[2]), BF)
    return pl.pallas_call(
        select_in_kernel,
        grid_spec=pltpu.PrefetchScalarGridSpec(
            num_scalar_prefetch=1,
            grid=(1,),
            in_specs=[core_block(picks), whole_spec(x), whole_spec(cot), whole_spec(far)],
            out_specs=[whole_spec(out), whole_spec(out), whole_spec(other)],
        ),
        out_shape=[out, out, other],
        compiler_params=params(28),
        cost_estimate=cost(0, 0),
        name="select_in",
    )(core, picks, x, cot, far)


def select_out_kernel(core_ref, picks_ref, kept_ref, beside_ref, across_ref, corner_ref, out_ref):
    skip = WTOK - SENT_IN
    near = jnp.concatenate([kept_ref[...], beside_ref[...]], 0)
    far = jnp.concatenate([across_ref[...], corner_ref[...]], 0)
    low = dot(one_hot_rows(picks_ref[0, : 4 * SENT_IN, :], far.shape[0]), far, 1, 0)
    high = dot(one_hot_rows(picks_ref[0, 4 * SENT_IN :, :], near.shape[0]), near, 1, 0)
    rows = lax.broadcasted_iota(jnp.int32, (SENT_IN - skip, 1), 0) + skip
    for w in range(4):
        first, last = [part[w * SENT_IN : (w + 1) * SENT_IN] for part in (low, high)]
        out_ref[w, :skip, :] = first[:skip]
        out_ref[w, skip:SENT_IN, :] = jnp.where(rows < HELD, first[skip:], last[: SENT_IN - skip])
        out_ref[w, SENT_IN:, :] = last[SENT_IN - skip :]


def select_out(core, picks, arrays):
    out = jax.ShapeDtypeStruct((4, WTOK, arrays[0].shape[1]), F32)
    return pl.pallas_call(
        select_out_kernel,
        grid_spec=pltpu.PrefetchScalarGridSpec(
            num_scalar_prefetch=1,
            grid=(1,),
            in_specs=[core_block(picks)] + [whole_spec(a) for a in arrays],
            out_specs=whole_spec(out),
        ),
        out_shape=out,
        compiler_params=params(28),
        cost_estimate=cost(0, 0),
        name="select_out",
    )(core, picks, *arrays)


def bits_of(axis):
    return lax.axis_size(axis).bit_length() - 1


def bit_on(axis, bit):
    return lax.shift_right_logical(lax.axis_index(axis), bit) % 2


def swap(value, axis, bit=0):
    pairs = [(source, source ^ (1 << bit)) for source in range(lax.axis_size(axis))]
    return lax.ppermute(value, axis, pairs)


def bit_order():
    count = bits_of("shard")
    return list(range(count - 1, 0, -1)) + [0]


def row_place(bit):
    place = bit_on("shard", bit)
    if bit == bits_of("shard") - 1:
        place = jnp.bitwise_xor(place, lax.axis_index("tensor"))
    return place


def ordered(on, mine, other, axis):
    return jnp.concatenate((jnp.where(on, other, mine), jnp.where(on, mine, other)), axis)


def after(value, *deps):
    return lax.optimization_barrier((value,) + deps)[0]


def gather_start(part):
    rows, cols = part.shape
    return part.reshape((1,) * bits_of("shard") + (rows, cols))


def joint(values, deps):
    return lax.optimization_barrier(tuple(values) + tuple(deps))[: len(values)]


def gather_join(held, bit, got):
    return ordered(row_place(bit) == 1, held, got, bits_of("shard") - 1 - bit)


def gather_send(held, bits):
    for bit in bits[:-1]:
        held = gather_join(held, bit, swap(held, "shard", bit))
    return held, swap(held, "shard", bits[-1])


def choose(array, index, axis):
    return lax.dynamic_slice_in_dim(array, index, 1, axis)


def add_rounded(a, b):
    return (a.astype(F32) + b.astype(F32)).astype(BF)


def split_rows(part):
    count = bits_of("shard")
    return part.reshape((2,) * count + (part.shape[0] >> count, part.shape[1]))


def scatter_add(held, bit, got):
    axis = bits_of("shard") - 1 - bit
    return add_rounded(choose(held, row_place(bit), axis), got)


def scatter_send(held, bits):
    for bit in bits[:-1]:
        held = scatter_add(held, bit, scatter_send(held, (bit,))[1])
    axis = bits_of("shard") - 1 - bits[-1]
    return held, swap(choose(held, 1 - row_place(bits[-1]), axis), "shard", bits[-1])


def ctx_half(held, own):
    axis = held.ndim - 2
    half = held.shape[axis] // 2
    return lax.dynamic_slice_in_dim(held, own * half, half, axis)


def ctx_split_send(held):
    return swap(ctx_half(held, 1 - bit_on("ctx", 0)), "ctx")


def ctx_split_add(held, got):
    return add_rounded(ctx_half(held, bit_on("ctx", 0)), got)


def flat(held):
    return held.reshape(held.shape[-2:])


def ctx_send(held):
    held = flat(held)
    for bit in range(bits_of("ctx") - 1):
        held = add_rounded(held, swap(held, "ctx", bit))
    return held, swap(held, "ctx", bits_of("ctx") - 1)


def ctx_add(held, got):
    return held.astype(F32) + got.astype(F32)


def joint_swap(value, mask):
    size = lax.axis_size("shard") * lax.axis_size("ctx")
    return lax.ppermute(value, ("shard", "ctx"), [(i, i ^ mask) for i in range(size)])


def joint_parts(value, bits):
    value = value.astype(BF)
    low = 1 << bits[0]
    if len(bits) == 1:
        return [value, joint_swap(value, low), jnp.zeros_like(value), jnp.zeros_like(value)]
    high = 1 << bits[1]
    return [value, joint_swap(value, low), joint_swap(value, high), joint_swap(value, low | high)]


def add_parts(parts):
    a, b, c, d = [part.astype(F32) for part in parts]
    return (a + b) + (c + d)


def joint_groups():
    bits = list(range(bits_of("shard") + bits_of("ctx")))
    return [bits[i : i + 2] for i in range(0, len(bits), 2)]


def roll_axis(shaped, axis_pos, levels, backward):
    token_axis = 4 + axis_pos
    length = shaped.shape[token_axis]
    border = length - length // 2 if backward else length // 2
    before = lax.slice_in_dim(shaped, 0, border, axis=token_axis)
    after = lax.slice_in_dim(shaped, border, length, axis=token_axis)
    moving = after if backward else before
    if axis_pos < levels:
        moving = swap(moving, "ctx", levels - 1 - axis_pos)
    else:
        moving = jnp.roll(moving, 1 if backward else -1, axis=1 + axis_pos)
    return jnp.concatenate((moving, before) if backward else (after, moving), axis=token_axis)


def window_roll(windows, clips, counts, backward):
    shaped = windows.reshape((clips,) + counts + (WT, WH, WW, windows.shape[-1]))
    for axis_pos in range(3):
        shaped = roll_axis(shaped, axis_pos, bits_of("ctx"), backward)
    return shaped.reshape(windows.shape)


def frame_sources():
    source = np.zeros((4, HELD), np.int64)
    for h in range(2 * WH):
        for w in range(2 * WW):
            here = (h // WH) * 2 + w // WW
            there_h, there_w = (h + WH // 2) % (2 * WH), (w + WW // 2) % (2 * WW)
            there = (there_h // WH) * 2 + there_w // WW
            for a in range(WT // 2):
                row = (a * WH + h % WH) * WW + w % WW
                source[here, row] = there * HELD + (a * WH + there_h % WH) * WW + there_w % WW
    return source


def picks_in():
    source = frame_sources()
    there, row = source // HELD, source % HELD
    picks = np.full((4, TOKS), -1)
    picks[:, :HELD] = there * SENT_IN + row + SENT_IN - HELD
    picks[:, HELD:WTOK] = there * SENT_IN + row
    both = []
    for rows in (picks, np.concatenate((picks[2:], picks[:2]))):
        both.append(np.concatenate((rows[:, :SENT_IN].reshape(-1, 1), rows[:, WTOK - SENT_IN :].reshape(-1, 1))))
    return jnp.asarray(np.stack(both), jnp.int32)


def picks_out():
    place = np.argsort(frame_sources().reshape(-1)).reshape(4, HELD)
    there, row = place // HELD, place % HELD
    both = []
    for core in range(2):
        block = ((there // 2 + core) % 2) * 2 * SENT_OUT + (there % 2) * SENT_OUT
        picks = np.zeros((4, WTOK), np.int64)
        picks[:, HELD:] = block + row
        picks[:, :HELD] = block + row + HELD - (TOKS - SENT_OUT)
        both.append(np.concatenate((picks[:, :SENT_IN].reshape(-1, 1), picks[:, WTOK - SENT_IN :].reshape(-1, 1))))
    return jnp.asarray(np.stack(both), jnp.int32)


def plain_ring(clips):
    return bits_of("ctx") == 1 and clips == 1


def shift_start(arrays, clips):
    if plain_ring(clips):
        sent = jnp.concatenate([a[:, :SENT_IN] for a in arrays], 0)
        return swap(sent.reshape(-1, sent.shape[-1]), "ctx")
    return arrays[0][:1, :8]


def shift_in(arrays, got, clips, counts, core_row):
    if plain_ring(clips):
        xm, cm, other = select_in(core_row, picks_in(), *arrays, got)
        return xm, cm, swap(other, "tensor")
    half = arrays[0].shape[0] // 2
    core = lax.axis_index("tensor")
    mine, sent = [], []
    for array in arrays:
        moved = jnp.pad(window_roll(array, clips, counts, False), ((0, 0), (0, TOKS - WTOK), (0, 0)))
        mine.append(lax.dynamic_slice_in_dim(moved, core * half, half, 0))
        sent.append(lax.dynamic_slice_in_dim(moved, (1 - core) * half, half, 0))
    return mine[0], mine[1], swap(jnp.concatenate(sent, 0), "tensor")


def leave_start(pieces, clips):
    nearm, nearo, farm, faro = pieces
    width = nearm.shape[-1]
    if not plain_ring(clips):
        cut = TOKS - SENT_OUT
        mine, other = [jnp.concatenate((near[:, :cut], far), 1) for near, far in ((nearm, farm), (nearo, faro))]
        return mine, swap(other, "tensor")
    nearm, nearo, farm, faro = [piece.reshape(-1, width) for piece in pieces]
    corner = lax.ppermute(faro, ("ctx", "tensor"), [(i, i ^ 3) for i in range(4)])
    return nearm, swap(nearo, "tensor"), swap(farm, "ctx"), corner


def leave_end(parts, clips, counts, core_row, *deps):
    parts = (after(parts[0], *deps),) + tuple(parts[1:])
    if plain_ring(clips):
        return select_out(core_row, picks_out(), parts)
    windows = ordered(lax.axis_index("tensor") == 1, parts[0], parts[1], 0)
    return window_roll(windows[:, :WTOK], clips, counts, True).astype(F32)


def on_device(
    clip_input,
    cotangent,
    gain_one,
    shift_one,
    w_qkv,
    b_qv,
    w_proj,
    b_proj,
    bias_table,
    gain_two,
    shift_two,
    w_fc1,
    b_fc1,
    w_fc2,
    b_fc2,
    rel_index,
    regions,
):
    clips, window_count, tokens, half_width = clip_input.shape
    heads = bias_table.shape[0]
    levels = bits_of("ctx")
    counts = tuple(1 if axis_pos < levels else 2 for axis_pos in range(3))
    core = lax.axis_index("tensor")
    core_row = core.astype(jnp.int32).reshape(1)
    total_windows = clips * window_count
    held_windows = total_windows // 2
    scale = HD ** (-0.5)
    hidden = w_fc1.shape[1]

    own = pack(gain_one, shift_one, b_qv, b_proj, gain_two, shift_two, b_fc2, b_fc1, bias_table)
    qkv = gather_start(w_qkv.transpose(1, 0, 2).reshape(w_qkv.shape[1], -1))
    rest = gather_start(jnp.concatenate((w_proj.T, w_fc1, w_fc2.T), 1))
    index = jnp.pad(rel_index.T, ((0, TOKS - tokens), (0, TOKS - tokens)))
    index = lax.dynamic_slice_in_dim(index, core * (TOKS - HALF_ROWS), HALF_ROWS, 0)
    block = HALF_ROWS // ROWS
    cut = block // 2
    early_blocks = 5
    labels = jnp.tile(regions, (clips, 1))
    labels = lax.dynamic_slice_in_dim(labels, core * held_windows, held_windows, 0)
    labels = jnp.pad(labels, ((0, 0), (0, TOKS - tokens)))[:, None, :]

    order = bit_order()
    first, middle, last = order[0], order[1:-1], order[-1]
    clip_rows = clip_input.reshape(total_windows, tokens, half_width)
    cot_rows = cotangent.reshape(total_windows, tokens, half_width)

    pair_rows = (clip_rows, cot_rows)
    pair_got = shift_start(pair_rows, clips)
    qkv_got, own, index = joint((swap(qkv, "shard", first), own, index), ())
    got = swap(own, "tensor")
    qkv = gather_join(qkv, first, qkv_got)
    qkv, qkv_got = gather_send(qkv, middle)
    rest = after(rest, qkv)
    rest_got = swap(rest, "shard", first)
    part_own = lookup(after(index, qkv), own, got, heads, 0, early_blocks)
    qkv_got, pair_got, rest_got, part_own = joint((qkv_got, pair_got, rest_got, part_own), ())
    qkv = gather_join(qkv, middle[-1], qkv_got)
    rest = gather_join(rest, first, rest_got)
    rest, rest_got = gather_send(rest, middle)
    qkv_got = swap(qkv, "shard", last)
    bias_own = lookup(index, own, got, heads, early_blocks, block - early_blocks, (part_own,))
    rest_got, qkv_got, bias_own = joint((rest_got, qkv_got, bias_own), ())
    xm, cm, other = shift_in(pair_rows, after(pair_got, bias_own), clips, counts, core_row)
    qkv = gather_join(qkv, last, qkv_got)
    qkv = qkv.reshape(-1, qkv.shape[-1])
    qkv_other = swap(qkv, "tensor")
    rest = gather_join(rest, middle[-1], rest_got)
    rest_got = swap(rest, "shard", last)
    bias_got = swap(bias_own, "tensor")
    queries, keys, values, first_t = front(xm, other, own, got, qkv, qkv_other, scale * LOG2E, ())
    att, exact, lse = attend(core_row, queries, keys, values, labels, bias_own, bias_got)
    rest_got, att = joint((rest_got, att), ())
    edge = half_width + hidden
    early, late = [gather_join(rest[..., span], last, rest_got[..., span]) for span in (slice(0, edge), slice(edge, None))]
    early, late = [w.reshape(-1, w.shape[-1]) for w in (early, late)]
    early_other, late_other = swap(early, "tensor"), swap(late, "tensor")
    mid, second, act, slope = middle_forward(xm, other, att, own, got, early, early_other)
    *block_pieces, grad_mid, grad_att, one_mine, one_other, two_mine, two_other, small_mid, small_wide = middle_back(cm, other, mid, second, act, slope, att, own, got, early, early_other, late, late_other, ())

    order = order[::-1]
    twice = bits_of("ctx") == 1
    args = (core_row, queries, keys, values, labels, bias_own, bias_got)
    block_parts = leave_start(block_pieces, clips)
    one_got, two_got = swap(one_other, "tensor"), swap(two_other, "tensor")
    qo, ko, vo, pair_o, sent_o = attend_back(*args, exact, lse, grad_att, scale, 1)
    one_got, two_got, qo, sent_o, *moved = joint((one_got, two_got, qo, sent_o) + tuple(block_parts[1:]), ())
    block_parts = (block_parts[0],) + tuple(moved)
    one, two = split_rows(add_rounded(one_mine, one_got)), split_rows(add_rounded(two_mine, two_got))
    one_got = scatter_send(one, order[:1])[1]
    two_got = ctx_split_send(two) if twice else scatter_send(two, order[:1])[1]
    side = side_grads(first_t, (qo, ko, vo))
    side_got, sent_o = swap(side, "tensor"), swap(sent_o, "tensor")
    qm, km, vm, pair_m, sent_m = attend_back(*args, exact, lse, after(grad_att, side), scale, 0)
    one_got, two_got, side, sent_o, qm, sent_m = joint((one_got, two_got, side_got, sent_o, qm, sent_m), ())
    one = scatter_add(one, order[0], one_got)
    two = ctx_split_add(two, two_got) if twice else scatter_add(two, order[0], two_got)
    one_got = scatter_send(one, order[1:2])[1]
    two_bits = order if twice else order[1:]
    two_got = scatter_send(two, two_bits[:1])[1]
    sent_m = swap(sent_m, "tensor")
    place = row_place(0).astype(jnp.int32).reshape(1)
    *grad_pieces, qkv_grads, qkv_sent, small_end = back(place, lax.axis_size("shard"), xm, other, first_t, (after(qm, one, two), km, vm), (qo, ko, vo), grad_mid, own, got, qkv, qkv_other, side)
    block_out = leave_end(block_parts, clips, counts, core_row, small_end)
    one_got, two_got, sent_m, block_out = joint((one_got, two_got, sent_m, block_out), ())
    one = scatter_add(one, order[1], one_got)
    two = scatter_add(two, two_bits[0], two_got)
    shape = (2,) * (len(order) - 1) + (1,) + qkv_grads.shape[1:]
    qkv_got = swap(qkv_sent.reshape(shape), "shard", order[0])
    grad_parts = leave_start(grad_pieces, clips)
    two_got = scatter_send(two, two_bits[1:2])[1]
    one, one_got = scatter_send(one, order[2:])
    pairs = (pair_m, pair_o, sent_m, sent_o)
    (folded,) = fold(core_row, after(index, one, two), pairs, heads, 0, cut)
    qkv_got, two_got, one_got, folded, *moved = joint((qkv_got, two_got, one_got, folded) + tuple(grad_parts[1:]), ())
    grad_parts = (grad_parts[0],) + tuple(moved)
    qkv_grads = add_rounded(qkv_grads.reshape(shape), qkv_got)
    two = scatter_add(two, two_bits[1], two_got)
    one = scatter_add(one, order[-1], one_got)
    qkv_got = scatter_send(qkv_grads, order[1:2])[1]
    two, two_got = scatter_send(two, two_bits[2:])
    one, one_got = ctx_send(one)
    fold_mine, fold_other = fold(core_row, after(index, one, two, qkv_grads), pairs, heads, cut, block - cut, (folded, small_mid, small_wide, small_end))
    qkv_got, two_got, one_got, fold_mine, fold_other = joint((qkv_got, two_got, one_got, fold_mine, fold_other), ())
    small = fold_mine + swap(fold_other, "tensor")
    qkv_grads = scatter_add(qkv_grads, order[1], qkv_got)
    qkv_grads, qkv_got = scatter_send(qkv_grads, order[2:])
    two = scatter_add(two, two_bits[-1], two_got)
    two, two_got = (two, swap(two, "ctx")) if twice else ctx_send(two)
    groups = joint_groups()
    for group in groups[:-2]:
        small = add_parts(joint_parts(small, group))
    parts = joint_parts(small, groups[-2])
    grad_input = leave_end(grad_parts, clips, counts, core_row, small)
    *parts, grad_input = joint(tuple(parts) + (grad_input,), ())
    small = add_parts(parts)
    parts = joint_parts(small, groups[-1])
    qkv_got, two_got, one_got = joint((qkv_got, two_got, one_got), (small,))
    qkv_grads = scatter_add(qkv_grads, order[-1], qkv_got)
    qkv_grads, qkv_got = ctx_send(qkv_grads)
    one = ctx_add(one, one_got)
    two = flat(ordered(bit_on("ctx", 0) == 1, two, two_got, two.ndim - 2)).astype(F32) if twice else ctx_add(two, two_got)
    qkv_grads = ctx_add(qkv_grads, qkv_got)
    d_gain1, d_shift1, d_bqv, d_bp, d_table, d_gain2, d_shift2, d_b1, d_b2 = unpack(parts, heads)
    rows = w_fc1.shape[0]
    return (
        block_out.reshape(clip_input.shape),
        grad_input.reshape(clip_input.shape),
        d_gain1,
        d_shift1,
        qkv_grads.reshape(rows, 3, half_width).transpose(1, 0, 2),
        d_bqv,
        two[:, :half_width].T,
        d_bp,
        d_table,
        d_gain2,
        d_shift2,
        one,
        d_b1,
        two[:, half_width:].T,
        d_b2,
    )


def solution(mesh):
    in_specs = (
        P("shard", "ctx", None, "tensor"),
        P("shard", "ctx", None, "tensor"),
        P("tensor"),
        P("tensor"),
        P(None, "shard", "tensor"),
        P(None, "tensor"),
        P("tensor", "shard"),
        P("tensor"),
        P("tensor", None),
        P("tensor"),
        P("tensor"),
        P("shard", "tensor"),
        P("tensor"),
        P("tensor", "shard"),
        P("tensor"),
        P(),
        P("ctx", None),
    )
    out_specs = (
        P("shard", "ctx", None, "tensor"),
        P("shard", "ctx", None, "tensor"),
        P("tensor"),
        P("tensor"),
        P(None, "shard", "tensor"),
        P(None, "tensor"),
        P("tensor", "shard"),
        P("tensor"),
        P("tensor", None),
        P("tensor"),
        P("tensor"),
        P("shard", "tensor"),
        P("tensor"),
        P("tensor", "shard"),
        P("tensor"),
    )
    return jax.shard_map(
        on_device, mesh=mesh, in_specs=in_specs, out_specs=out_specs, check_vma=False
    )
```
